32 devices in a mesh: head: 2 (over x), expert: 16 (over z, y, core).
Axes of the slice: x: 2, y: 2, z: 4, core: 2. Of those that a mesh axis runs over, the one named last changes fastest.
Arguments:
- q_latent: bfloat16 [128, 64, 512], P('expert', 'head'), may hold values from -16 to 16
- q_rotary: bfloat16 [128, 64, 64], P('expert', 'head'), may hold values from -3 to 3
- cache_latent: bfloat16 [128, 128, 512], P('expert'), may hold values from -5 to 5
- cache_rotary: bfloat16 [128, 64, 128], P('expert'), may hold values from -5 to 5
- lengths: int32 [128], P('expert'), may hold values from 16 to 128, as said below
- w_value_out: bfloat16 [32768, 5120], P('head', 'expert'), may hold values from -0.25 to 0.25
- resid: bfloat16 [128, 5120], P('expert'), may hold values from -8 to 8
- norm_gain: float32 [5120], replicated, may hold values from 0.1 to 1.9
- route_ids: int32 [128, 6], P('expert'), may hold values from 0 to 15, as said below
- route_weights: float32 [128, 6], P('expert'), may hold values from 0.1 to 0.6
- w_gate_up: bfloat16 [16, 2, 768, 5120], P('expert', None, 'head'), may hold values from -0.078125 to 0.078125
- w_down: bfloat16 [16, 768, 5120], P('expert', 'head'), may hold values from -0.21875 to 0.21875
Outputs:
- mixed_out: float32 [128, 5120], P('expert', 'head')
The draws below stay inside these ranges and needn't reach their ends.
Inputs may be any that keep to these rules, and one draw needn't show every extreme that they name: `lengths`: slots at positions below a sequence's length are valid; some sequence has length 128. `route_ids`: each row names 6 different experts. Among the rows of one device (aligned blocks of 8 rows) no expert is named by more than 3 rows, and one expert is named by exactly 3 rows in every block.
All inputs are finite; a program needn't handle non-finite values.
Results may differ from the reference program's by a relative error of at most 0.0046.
Values may be sent and summed in bfloat16 or wider, within the bound.
A program may use at most 64 MiB of HBM per device.

```python
import jax
import jax.numpy as jnp
from jax import lax

D = 5120
HEADS = 64
LAT = 512
ROPE = 64
FF = 768
TOPK = 6
CAP = 128
SEQ_DEV = 8
SEQS = 128
EXPERTS = 16
MOST = 3
N_EXPERT = 16


def attention_fields(key):
    query_lat = jnp.clip(jax.random.normal(jax.random.fold_in(key, 11), (SEQS, HEADS, LAT)) * 0.6, -3.0, 3.0)
    query_rot = jnp.clip(jax.random.normal(jax.random.fold_in(key, 12), (SEQS, HEADS, ROPE)) * 0.6, -3.0, 3.0)
    cache_lat = jnp.clip(jax.random.normal(jax.random.fold_in(key, 13), (SEQS, CAP, LAT)), -5.0, 5.0)
    cache_rot = jnp.clip(jax.random.normal(jax.random.fold_in(key, 14), (SEQS, ROPE, CAP)), -5.0, 5.0)
    return (query_lat, query_rot, cache_lat, cache_rot)


def draw_q_latent(key, part):
    return attention_fields(key)[0].astype(jnp.bfloat16)


def draw_q_rotary(key, part):
    return attention_fields(key)[1].astype(jnp.bfloat16)


def draw_cache_latent(key, part):
    return attention_fields(key)[2].astype(jnp.bfloat16)


def draw_cache_rotary(key, part):
    return attention_fields(key)[3].astype(jnp.bfloat16)


def draw_lengths(key, part):
    drawn = jax.random.randint(jax.random.fold_in(key, 31), (SEQS,), CAP // 8, CAP + 1)
    longest = jax.random.randint(jax.random.fold_in(key, 32), (), 0, SEQS)
    return jnp.where(jnp.arange(SEQS) == longest, CAP, drawn).astype(jnp.int32)


def draw_resid(key, part):
    values = jnp.clip(jax.random.normal(jax.random.fold_in(key, 41), (SEQS, D)), -6.0, 6.0)
    return values.astype(jnp.bfloat16)


def draw_route_ids(key, part):
    block_count = SEQS // SEQ_DEV
    assigned = SEQ_DEV * TOPK
    span_size = (assigned + MOST - 1) // MOST
    popularity = jax.random.randint(jax.random.fold_in(key, 21), (EXPERTS,), 0, 4)
    hottest = jax.random.randint(jax.random.fold_in(key, 22), (), 0, EXPERTS)
    jitter = jax.random.randint(jax.random.fold_in(key, 23), (block_count, EXPERTS), 0, 1024)
    expert_ids = jnp.arange(EXPERTS, dtype=jnp.int32)
    ranking_score = jitter + popularity[None, :] * 256 + jnp.where(expert_ids == hottest, 1 << 20, 0)[None, :]
    distinct = ranking_score * EXPERTS + expert_ids[None, :]
    ranking = jnp.argsort(-distinct, axis=1)
    positions = jnp.arange(assigned, dtype=jnp.int32) % span_size
    picked = jnp.take(ranking, positions, axis=1)
    return picked.reshape(SEQS, TOPK).astype(jnp.int32)


def levels(key, dims, cuts, low, top_value):
    factor_of, own = 1.0, jax.random.fold_in(key, 6)
    for dim, parts in cuts:
        heights = jnp.exp(jax.random.uniform(jax.random.fold_in(own, dim), (parts,), jnp.float32, low / len(cuts), top_value / len(cuts)))
        factor_of = factor_of * jnp.repeat(heights, dims[dim] // parts).reshape([-1 if axis == dim else 1 for axis in range(len(dims))])
    return factor_of


def normal_values(key, extent, width, bound, shards=(), kind=jnp.bfloat16):
    entries = width * jax.random.normal(key, extent, jnp.float32)
    if shards:
        entries = entries * levels(key, extent, shards, -0.22, 0.18)
    return jnp.clip(entries, -bound, bound).astype(kind)


def setup_inputs(seed: int = 0) -> dict:
    splits = jax.random.split(jax.random.key(seed), 13)
    return {
        "q_latent": draw_q_latent(jax.random.fold_in(splits[12], 71), 0),
        "q_rotary": draw_q_rotary(jax.random.fold_in(splits[12], 71), 0),
        "cache_latent": draw_cache_latent(jax.random.fold_in(splits[12], 71), 0),
        "cache_rotary": draw_cache_rotary(jax.random.fold_in(splits[12], 71), 0),
        "lengths": draw_lengths(jax.random.fold_in(splits[12], 71), 0),
        "w_value_out": normal_values(splits[5], (HEADS * LAT, D), LAT ** -0.5, 0.25, ((0, 2), (1, 16))),
        "resid": draw_resid(jax.random.fold_in(splits[12], 71), 0),
        "norm_gain": jnp.clip(1.0 + 0.18 * jax.random.normal(splits[7], (D,), jnp.float32), 0.1, 1.9),
        "route_ids": draw_route_ids(jax.random.fold_in(splits[12], 71), 0),
        "route_weights": jnp.clip(0.1 + 0.5 * jax.random.uniform(splits[9], (SEQS, TOPK), jnp.float32) ** levels(splits[9], (SEQS, TOPK), ((0, 16),), -0.2, 0.2), 0.1, 0.6),
        "w_gate_up": normal_values(splits[10], (EXPERTS, 2, FF, D), D ** -0.5, 0.078125, ((0, 16), (2, 2))),
        "w_down": normal_values(splits[11], (EXPERTS, FF, D), FF ** -0.5, 0.21875, ((0, 16), (1, 2))),
    }


softmax_scale = 192.0 ** (-0.5)
norm_epsilon = 1e-06

def reference(q_latent, q_rotary, cache_latent, cache_rotary, lengths, w_value_out, resid, norm_gain, route_ids, route_weights, w_gate_up, w_down):
    cache_float = cache_latent.astype(jnp.float32)
    scores = jnp.einsum('shl,scl->shc', q_latent.astype(jnp.float32), cache_float)
    scores = scores + jnp.einsum('shr,src->shc', q_rotary.astype(jnp.float32), cache_rotary.astype(jnp.float32))
    scores = scores * softmax_scale
    position = jnp.arange(CAP, dtype=jnp.int32)
    valid_slot = position[None, None, :] < lengths[:, None, None]
    scores = jnp.where(valid_slot, scores, -1e+30)
    highest = lax.optimization_barrier(jnp.max(scores, axis=2, keepdims=True))
    weights = jnp.exp(scores - highest)
    probs = (weights / lax.optimization_barrier(jnp.sum(weights, axis=2, keepdims=True))).astype(jnp.bfloat16)
    latent_out = jnp.einsum('shc,scl->shl', probs.astype(jnp.float32), cache_float).astype(jnp.bfloat16)
    flattened = latent_out.reshape(SEQS, HEADS * LAT)
    attention = jnp.dot(flattened, w_value_out, preferred_element_type=jnp.float32).astype(jnp.bfloat16)
    stream = resid.astype(jnp.float32) + attention.astype(jnp.float32)
    mean_square = lax.optimization_barrier(jnp.mean(stream * stream, axis=1, keepdims=True))
    normed = (stream * lax.rsqrt(mean_square + norm_epsilon) * norm_gain).astype(jnp.bfloat16)
    flat_ids = route_ids.reshape(-1)
    flat_weights = route_weights.reshape(-1)
    token_of = jnp.arange(SEQS * TOPK, dtype=jnp.int32) // TOPK
    limit = N_EXPERT * MOST

    def add_expert(total, item):
        index, gate_up, down_matrix = item
        chosen = flat_ids == index
        picks = jnp.nonzero(chosen, size=limit, fill_value=0)[0].astype(jnp.int32)
        valid_row = jnp.arange(limit, dtype=jnp.int32) < jnp.sum(chosen.astype(jnp.int32))
        token_rows = token_of[picks]
        inputs = normed[token_rows]
        projected = jnp.einsum('rd,gfd->rgf', inputs.astype(jnp.float32), gate_up.astype(jnp.float32))
        hidden = (jax.nn.silu(projected[:, 0]) * projected[:, 1]).astype(jnp.bfloat16)
        expert_out = jnp.dot(hidden, down_matrix, preferred_element_type=jnp.float32).astype(jnp.bfloat16)
        row_weight = jnp.where(valid_row, flat_weights[picks], 0.0)
        total = total.at[token_rows].add(expert_out.astype(jnp.float32) * row_weight[:, None])
        return (total, None)
    mixture, unused = lax.scan(add_expert, jnp.zeros((SEQS, D), jnp.float32), (jnp.arange(EXPERTS, dtype=jnp.int32), w_gate_up, w_down))
    return stream + mixture
```

```python
import functools

import jax
import jax.numpy as jnp
from jax import lax
from jax.experimental import pallas as pl
from jax.experimental.pallas import tpu as pltpu
from jax.sharding import PartitionSpec as P

MESH = pl.DeviceIdType.MESH
softmax_scale = 192.0 ** (-0.5)
norm_epsilon = 1e-06

LINE, PAIR, CORE = 4, 2, 2
CHUNKS = 4
EXTRA = 128
SLOTS = 4


def rows_of(blocks):
    n, r, c = blocks.shape
    return blocks.astype(jnp.float32).reshape(n * r, c).astype(jnp.bfloat16)


def blocks_of(rows, n):
    return rows.reshape(n, rows.shape[0] // n, rows.shape[1]).astype(jnp.bfloat16)


def spread(z, y, c, buffers, up, down, side, sib, recv):
    def slot(zz, yy, cc):
        return (zz * PAIR + yy) * CORE + cc

    def copy(k, s, sems, index, target):
        return pltpu.make_async_remote_copy(
            src_ref=buffers.at[k, s],
            dst_ref=buffers.at[k, s],
            send_sem=sems.at[k, index],
            recv_sem=recv.at[k, s],
            device_id={"expert": target},
            device_id_type=MESH,
        )

    def each_send(k, zz, act):
        s = slot(zz, y, c)

        @pl.when(jnp.logical_and(zz <= z, z < LINE - 1))
        def _():
            act(copy(k, s, up, zz, slot(z + 1, y, c)))

        @pl.when(jnp.logical_and(zz >= z, z > 0))
        def _():
            act(copy(k, s, down, zz, slot(z - 1, y, c)))

        act(copy(k, s, side, zz, slot(z, 1 - y, c)))
        act(copy(k, s, sib, zz, slot(z, y, 1 - c)))

    def arrived(k, s):
        copy(k, s, sib, 0, slot(z, y, 1 - c)).wait_recv()

    def at_distance(d, act):
        if d == 0:
            act(z)
            return

        @pl.when(z - d >= 0)
        def _():
            act(z - d)

        @pl.when(z + d < LINE)
        def _():
            act(z + d)

    def step(k, d):
        def line(zz):
            if d > 0:
                arrived(k, slot(zz, y, c))
            each_send(k, zz, lambda x: x.start())

        def across(zz):
            s = slot(zz, 1 - y, c)
            arrived(k, s)
            copy(k, s, sib, LINE + zz, slot(z, y, 1 - c)).start()

        if d < LINE:
            at_distance(d, line)
        if d > 0:
            at_distance(d - 1, across)

    def finish(k):
        def body(i, carry):
            arrived(k, slot(lax.div(i, PAIR), lax.rem(i, PAIR), 1 - c))
            return carry

        lax.fori_loop(0, LINE * PAIR, body, 0)

    def drain(k):
        def body(zz, carry):
            each_send(k, zz, lambda x: x.wait_send())
            copy(k, slot(zz, 1 - y, c), sib, LINE + zz, slot(z, y, 1 - c)).wait_send()
            return carry

        lax.fori_loop(0, LINE, body, 0)

    return step, finish, drain


def layer_kernel(
    latent_ref, resid_ref, gain_ref, ids_ref, weights_ref, wvo_hbm, wgu_hbm, wdn_hbm,
    out_ref,
    wvo, wgu, wdn, gathered, partial, partner, outgoing, incoming, stream,
    tokens, rows_send, rows_recv, back_out, back_in,
    w_sem, g_up, g_down, g_side, g_sib, g_recv, t_up, t_down, t_side, t_sib, t_recv,
    x_sem, a_send, a_recv, b_send, b_recv,
):
    n = LINE * PAIR * CORE
    h, me = lax.axis_index("head"), lax.axis_index("expert")
    z, y, c = lax.div(me, PAIR * CORE), lax.rem(lax.div(me, CORE), PAIR), lax.rem(me, CORE)
    seqs, width = resid_ref.shape
    depth = gathered.shape[3]
    cols = partial.shape[1]
    half = out_ref.shape[1]
    quarter = half // 2
    top = ids_ref.shape[1]
    capacity = rows_send.shape[0] // n
    f32, bf16 = jnp.float32, jnp.bfloat16

    loads = [
        pltpu.make_async_copy(src, dst, w_sem.at[i])
        for i, (src, dst) in enumerate(((wvo_hbm, wvo), (wgu_hbm, wgu), (wdn_hbm, wdn)))
    ]
    for load in loads:
        load.start()

    barrier = pltpu.get_barrier_semaphore()

    def greet(o, carry):
        pl.semaphore_signal(
            barrier, inc=1, device_id={"expert": lax.rem(me + o, n)}, device_id_type=MESH
        )
        return carry

    lax.fori_loop(1, n, greet, 0)
    pl.semaphore_signal(barrier, inc=1, device_id={"head": 1 - h}, device_id_type=MESH)

    for k in range(CHUNKS):
        gathered[k, me] = latent_ref[:, k * depth : (k + 1) * depth]
    partial[...] = jnp.zeros_like(partial)
    pl.semaphore_wait(barrier, n)

    step, finish, drain = spread(z, y, c, gathered, g_up, g_down, g_side, g_sib, g_recv)
    tile = depth // 4

    def turn(t, carry):
        for d in range(LINE, -1, -1):
            k = t - d

            @pl.when(jnp.logical_and(k >= 0, k < CHUNKS))
            def _():
                step(k, d)

        @pl.when(t == LINE)
        def _():
            loads[0].wait()

        @pl.when(t >= LINE)
        def _():
            k = t - LINE
            finish(k)
            for j in range(4):
                x = rows_of(gathered[k, :, :, j * tile : (j + 1) * tile])
                w = wvo[pl.ds(pl.multiple_of(k * depth + j * tile, tile), tile), :]
                partial[...] += jnp.dot(x, w, preferred_element_type=f32)

        return carry

    lax.fori_loop(0, CHUNKS + LINE, turn, 0)

    swap = pltpu.make_async_remote_copy(
        src_ref=partial, dst_ref=partner, send_sem=x_sem.at[0], recv_sem=x_sem.at[1],
        device_id={"head": 1 - h}, device_id_type=MESH,
    )
    swap.start()
    swap.wait_recv()
    outgoing[...] = blocks_of(partial[...] + partner[...], n)

    def owner(o, source, target, send, recv):
        to = lax.rem(me + o, n)
        return pltpu.make_async_remote_copy(
            src_ref=source.at[to], dst_ref=target.at[me], send_sem=send.at[to],
            recv_sem=recv.at[me], device_id={"expert": to}, device_id_type=MESH,
        )

    def exchange_start(source, target, send, recv):
        def body(o, carry):
            owner(o, source, target, send, recv).start()
            return carry

        lax.fori_loop(1, n, body, 0)

    def exchange_recv(source, target, send, recv):
        def body(o, carry):
            who = lax.rem(me + o, n)
            pltpu.make_async_remote_copy(
                src_ref=source.at[who], dst_ref=target.at[who], send_sem=send.at[who],
                recv_sem=recv.at[who], device_id={"expert": who}, device_id_type=MESH,
            ).wait_recv()
            return carry

        lax.fori_loop(1, n, body, 0)

    def exchange_sent(source, target, send, recv):
        def body(o, carry):
            owner(o, source, target, send, recv).wait_send()
            return carry

        lax.fori_loop(1, n, body, 0)

    exchange_start(outgoing, incoming, a_send, a_recv)
    incoming[me] = outgoing[me]
    ids = ids_ref[...]
    lane = lax.broadcasted_iota(jnp.int32, (seqs, EXTRA), 1)
    named = jnp.zeros((seqs, EXTRA), f32)
    for k in range(top):
        named = named + jnp.where(ids[:, k : k + 1] == lane, 1.0, 0.0)
    exchange_recv(outgoing, incoming, a_send, a_recv)

    for e in range(n):
        stream[:, e * cols : (e + 1) * cols] = incoming[e].astype(f32)
    rows = stream[...] + resid_ref[...].astype(f32)
    stream[...] = rows
    mean_square = jnp.sum(rows * rows, axis=1, keepdims=True) * (1.0 / width)
    normed = rows * lax.rsqrt(mean_square + norm_epsilon) * gain_ref[...]
    tokens[0, me, :, :width] = normed.astype(bf16)
    tokens[0, me, :, width:] = named.astype(bf16)

    t_step, t_finish, t_drain = spread(z, y, c, tokens, t_up, t_down, t_side, t_sib, t_recv)
    for d in range(LINE + 1):
        t_step(0, d)

    wide = n * 2 * SLOTS
    place = lax.broadcasted_iota(jnp.int32, (seqs, wide), 1)
    which, part, at = place // (2 * SLOTS), (place // SLOTS) % 2, place % SLOTS
    hit = jnp.zeros((seqs, wide), f32)
    share = jnp.zeros((seqs, wide), f32)
    for k in range(top):
        same = ids[:, k : k + 1] == which
        hit = hit + jnp.where(same, 1.0, 0.0)
        share = share + jnp.where(same, weights_ref[:, k : k + 1], 0.0)
    token = lax.broadcasted_iota(jnp.int32, (seqs, wide), 0)
    rank = jnp.zeros((seqs, wide), f32)
    for t in range(seqs - 1):
        rank = rank + jnp.where(token > t, hit[t : t + 1, :], 0.0)
    blend = jnp.where(rank == at.astype(f32), share, 0.0)

    t_finish(0)
    loads[1].wait()

    total = n * seqs
    flags = rows_of(tokens[0, :, :, width:])
    mine = jnp.where(lax.broadcasted_iota(jnp.int32, (8, EXTRA), 1) == me, 1.0, 0.0).astype(bf16)
    chosen = lax.dot_general(mine, flags, (((1,), (1,)), ((), ())), preferred_element_type=f32)
    first = lax.broadcasted_iota(jnp.int32, (total, total), 0)
    second = lax.broadcasted_iota(jnp.int32, (total, total), 1)
    ahead = jnp.where(
        jnp.logical_and(first < second, first // seqs == second // seqs), 1.0, 0.0
    ).astype(bf16)
    order = jnp.dot(chosen.astype(bf16), ahead, preferred_element_type=f32)
    count = capacity * n
    row = lax.broadcasted_iota(jnp.int32, (count, total), 0)
    tok = lax.broadcasted_iota(jnp.int32, (count, total), 1)
    fits = jnp.logical_and(order[0:1, :] == (row // n).astype(f32), tok // seqs == row % n)
    pick = jnp.where(fits, chosen[0:1, :], 0.0).astype(bf16)

    units = wgu.shape[1]
    gate = jnp.zeros((count, units), f32)
    lift = jnp.zeros((count, units), f32)
    span = width // 5
    for j in range(5):
        piece = slice(j * span, (j + 1) * span)
        x = jnp.dot(pick, rows_of(tokens[0, :, :, piece]), preferred_element_type=f32).astype(bf16)
        gate += lax.dot_general(
            x, wgu[0, :, piece], (((1,), (1,)), ((), ())), preferred_element_type=f32
        )
        lift += lax.dot_general(
            x, wgu[1, :, piece], (((1,), (1,)), ((), ())), preferred_element_type=f32
        )
    hidden = (gate / (1.0 + jnp.exp(-gate)) * lift).astype(bf16)
    loads[2].wait()
    theirs = pl.ds(pl.multiple_of((1 - h) * half, half), half)
    ours = pl.ds(pl.multiple_of(h * half, half), half)
    rows_send[...] = jnp.dot(hidden, wdn[:, theirs], preferred_element_type=f32).astype(bf16)
    trade = pltpu.make_async_remote_copy(
        src_ref=rows_send, dst_ref=rows_recv, send_sem=x_sem.at[2], recv_sem=x_sem.at[3],
        device_id={"head": 1 - h}, device_id_type=MESH,
    )
    trade.start()
    own = jnp.dot(hidden, wdn[:, ours], preferred_element_type=f32)
    dest = lax.broadcasted_iota(jnp.int32, (n * 2 * SLOTS, count), 0)
    from_row = lax.broadcasted_iota(jnp.int32, (n * 2 * SLOTS, count), 1)
    home = from_row == (dest % SLOTS) * n + dest // (2 * SLOTS)
    upper = (dest // SLOTS) % 2
    trade.wait_recv()
    summed = (own + rows_recv[...].astype(f32)).astype(bf16)
    back = jnp.zeros((n * 2 * SLOTS, quarter), f32)
    for a in range(2):
        put = jnp.where(jnp.logical_and(home, upper == a), 1.0, 0.0).astype(bf16)
        back += jnp.dot(put, summed[:, a * quarter : (a + 1) * quarter], preferred_element_type=f32)
    back_out[...] = blocks_of(back, n)
    exchange_start(back_out, back_in, b_send, b_recv)
    back_in[me] = back_out[me]
    exchange_recv(back_out, back_in, b_send, b_recv)

    returned = rows_of(back_in[...])
    for a in range(2):
        mix = jnp.where(part == a, blend, 0.0)
        high = mix.astype(bf16)
        low = (mix - high.astype(f32)).astype(bf16)
        added = jnp.dot(high, returned, preferred_element_type=f32)
        added = added + jnp.dot(low, returned, preferred_element_type=f32)
        start = pl.multiple_of(h * half + a * quarter, quarter)
        out_ref[:, a * quarter : (a + 1) * quarter] = stream[:, pl.ds(start, quarter)] + added

    for k in range(CHUNKS):
        drain(k)
    t_drain(0)
    swap.wait_send()
    trade.wait_send()
    exchange_sent(outgoing, incoming, a_send, a_recv)
    exchange_sent(back_out, back_in, b_send, b_recv)


def fused(latents, resid, norm_gain, route_ids, route_weights, w_value_out, w_gate_up, w_down):
    n = LINE * PAIR * CORE
    seqs, width = resid.shape
    depth = latents.shape[1] // CHUNKS
    cols = w_value_out.shape[1]
    half = width // 2
    capacity = -(-(seqs * route_ids.shape[1]) // n)
    gate_up, down = w_gate_up[0], w_down[0]
    bf16, f32 = jnp.bfloat16, jnp.float32
    vmem, anywhere = pl.BlockSpec(memory_space=pltpu.VMEM), pl.BlockSpec(memory_space=pl.ANY)
    dma = pltpu.SemaphoreType.DMA
    return pl.pallas_call(
        layer_kernel,
        out_shape=jax.ShapeDtypeStruct((seqs, half), f32),
        in_specs=[vmem] * 5 + [anywhere] * 3,
        out_specs=vmem,
        scratch_shapes=[
            pltpu.VMEM(w_value_out.shape, bf16),
            pltpu.VMEM(gate_up.shape, bf16),
            pltpu.VMEM(down.shape, bf16),
            pltpu.VMEM((CHUNKS, n, seqs, depth), bf16),
            pltpu.VMEM((n * seqs, cols), f32),
            pltpu.VMEM((n * seqs, cols), f32),
            pltpu.VMEM((n, seqs, cols), bf16),
            pltpu.VMEM((n, seqs, cols), bf16),
            pltpu.VMEM((seqs, width), f32),
            pltpu.VMEM((1, n, seqs, width + EXTRA), bf16),
            pltpu.VMEM((capacity * n, half), bf16),
            pltpu.VMEM((capacity * n, half), bf16),
            pltpu.VMEM((n, 2 * SLOTS, half // 2), bf16),
            pltpu.VMEM((n, 2 * SLOTS, half // 2), bf16),
            dma((3,)),
            dma((CHUNKS, LINE)), dma((CHUNKS, LINE)), dma((CHUNKS, LINE)),
            dma((CHUNKS, PAIR * LINE)), dma((CHUNKS, n)),
            dma((1, LINE)), dma((1, LINE)), dma((1, LINE)), dma((1, PAIR * LINE)), dma((1, n)),
            dma((4,)), dma((n,)), dma((n,)), dma((n,)), dma((n,)),
        ],
        compiler_params=pltpu.CompilerParams(
            collective_id=0, has_side_effects=True, vmem_limit_bytes=56 * 1024 * 1024
        ),
    )(latents, resid, norm_gain[None, :], route_ids, route_weights, w_value_out, gate_up, down)


def attend(q_latent, q_rotary, cache_latent, cache_rotary, lengths):
    scores = jnp.einsum("shl,scl->shc", q_latent, cache_latent, preferred_element_type=jnp.float32)
    scores = scores + jnp.einsum(
        "shr,src->shc", q_rotary, cache_rotary, preferred_element_type=jnp.float32
    )
    scores = scores * softmax_scale
    position = lax.broadcasted_iota(jnp.int32, scores.shape, 2)
    scores = jnp.where(position < lengths[:, None, None], scores, -1e30)
    highest = jnp.max(scores, axis=2, keepdims=True)
    weights = jnp.exp(scores - highest)
    probs = (weights / jnp.sum(weights, axis=2, keepdims=True)).astype(jnp.bfloat16)
    return jnp.einsum(
        "shc,scl->shl", probs, cache_latent, preferred_element_type=jnp.float32
    ).astype(jnp.bfloat16)


def on_device(
    q_latent,
    q_rotary,
    cache_latent,
    cache_rotary,
    lengths,
    w_value_out,
    resid,
    norm_gain,
    route_ids,
    route_weights,
    w_gate_up,
    w_down,
):
    seq_local = q_latent.shape[0]
    latent_out = attend(q_latent, q_rotary, cache_latent, cache_rotary, lengths)
    flattened = latent_out.reshape(seq_local, -1)
    if (
        lax.axis_size("head") == 2
        and lax.axis_size("expert") == LINE * PAIR * CORE
        and seq_local == 8
    ):
        return fused(
            flattened, resid, norm_gain, route_ids, route_weights, w_value_out, w_gate_up, w_down
        )
    column_terms = jnp.dot(
        lax.all_gather(flattened, "expert", axis=0, tiled=True),
        w_value_out,
        preferred_element_type=jnp.float32,
    )
    column_sums = lax.psum(column_terms, "head")
    attention = lax.all_to_all(
        column_sums.astype(jnp.bfloat16), "expert", split_axis=0, concat_axis=1, tiled=True
    )
    stream = resid.astype(jnp.float32) + attention.astype(jnp.float32)
    mean_square = jnp.mean(stream * stream, axis=1, keepdims=True)
    normed = (stream * lax.rsqrt(mean_square + norm_epsilon) * norm_gain).astype(jnp.bfloat16)
    expert_count = lax.axis_size("expert")
    top_count = route_ids.shape[1]
    capacity = max(2, -(-(seq_local * top_count) // expert_count))
    flat_ids = route_ids.reshape(-1)
    one_hot = (flat_ids[:, None] == jnp.arange(expert_count, dtype=jnp.int32)[None, :]).astype(
        jnp.int32
    )
    earlier = jnp.cumsum(one_hot, axis=0) - one_hot
    slot_index = jnp.sum(earlier * one_hot, axis=1)
    target = (flat_ids * capacity + slot_index).reshape(seq_local, top_count)
    places = jnp.arange(expert_count * capacity, dtype=jnp.int32)
    matches = target[None, :, :] == places[:, None, None]
    selector = jnp.sum(matches.astype(jnp.int32), axis=2).astype(jnp.bfloat16)
    blending = jnp.sum(jnp.where(matches, route_weights[None, :, :], 0.0), axis=2)
    outgoing = jnp.dot(selector, normed, preferred_element_type=jnp.float32).astype(jnp.bfloat16)
    outgoing = outgoing.reshape(expert_count, capacity, -1)
    gate_up = w_gate_up[0]
    down_local = w_down[0]
    col_width = stream.shape[1] // lax.axis_size("head")
    offset = lax.axis_index("head") * col_width
    arrived = lax.all_to_all(outgoing, "expert", split_axis=0, concat_axis=0, tiled=True)
    flat_rows = arrived.reshape(-1, arrived.shape[2])
    projected = jnp.einsum("rd,gfd->rgf", flat_rows, gate_up, preferred_element_type=jnp.float32)
    hidden = (jax.nn.silu(projected[:, 0]) * projected[:, 1]).astype(jnp.bfloat16)
    partial_rows = jnp.dot(hidden, down_local, preferred_element_type=jnp.float32)
    expert_terms = partial_rows.reshape(arrived.shape[0], arrived.shape[1], -1)
    summed_rows = lax.psum(expert_terms.astype(jnp.bfloat16), "head")
    returned = lax.all_to_all(summed_rows, "expert", split_axis=0, concat_axis=0, tiled=True)
    back_rows = returned.reshape(expert_count * capacity, -1).astype(jnp.float32)
    mixture = jnp.dot(blending.T, back_rows, precision=lax.Precision.HIGHEST)
    mixed_full = stream + mixture
    return lax.dynamic_slice_in_dim(mixed_full, offset, col_width, 1)


def solution(mesh):
    placed = (
        P("expert", "head", None),
        P("expert", "head", None),
        P("expert", None, None),
        P("expert", None, None),
        P("expert"),
        P("head", "expert"),
        P("expert", None),
        P(),
        P("expert", None),
        P("expert", None),
        P("expert", None, "head", None),
        P("expert", "head", None),
    )
    return jax.shard_map(
        on_device, mesh=mesh, in_specs=placed, out_specs=P("expert", "head"), check_vma=False
    )
```

```python
import functools

import jax
import jax.numpy as jnp
from jax import lax
from jax.experimental import pallas as pl
from jax.experimental.pallas import tpu as pltpu
from jax.sharding import PartitionSpec as P

MESH = pl.DeviceIdType.MESH
softmax_scale = 192.0 ** (-0.5)
norm_epsilon = 1e-06

LINE, PAIR, CORE = 4, 2, 2
CHUNKS = 4
EXTRA = 128
SLOTS = 4
PARTS = 2


def rows_of(blocks):
    n, r, c = blocks.shape
    return blocks.astype(jnp.float32).reshape(n * r, c).astype(jnp.bfloat16)


def blocks_of(rows, n):
    return rows.reshape(n, rows.shape[0] // n, rows.shape[1]).astype(jnp.bfloat16)


def spread(z, y, c, buffers, up, down, side, sib, recv):
    def slot(zz, yy, cc):
        return (zz * PAIR + yy) * CORE + cc

    def copy(k, s, sems, index, target):
        return pltpu.make_async_remote_copy(
            src_ref=buffers.at[k, s],
            dst_ref=buffers.at[k, s],
            send_sem=sems.at[k, index],
            recv_sem=recv.at[k, s],
            device_id={"expert": target},
            device_id_type=MESH,
        )

    def each_send(k, zz, act):
        s = slot(zz, y, c)

        @pl.when(jnp.logical_and(zz <= z, z < LINE - 1))
        def _():
            act(copy(k, s, up, zz, slot(z + 1, y, c)))

        @pl.when(jnp.logical_and(zz >= z, z > 0))
        def _():
            act(copy(k, s, down, zz, slot(z - 1, y, c)))

        act(copy(k, s, side, zz, slot(z, 1 - y, c)))
        act(copy(k, s, sib, zz, slot(z, y, 1 - c)))

    def arrived(k, s):
        copy(k, s, sib, 0, slot(z, y, 1 - c)).wait_recv()

    def at_distance(d, act):
        if d == 0:
            act(z)
            return

        @pl.when(z - d >= 0)
        def _():
            act(z - d)

        @pl.when(z + d < LINE)
        def _():
            act(z + d)

    def step(k, d):
        def line(zz):
            if d > 0:
                arrived(k, slot(zz, y, c))
            each_send(k, zz, lambda x: x.start())

        def across(zz):
            s = slot(zz, 1 - y, c)
            arrived(k, s)
            copy(k, s, sib, LINE + zz, slot(z, y, 1 - c)).start()

        if d < LINE:
            at_distance(d, line)
        if d > 0:
            at_distance(d - 1, across)

    def finish(k):
        def body(i, carry):
            arrived(k, slot(lax.div(i, PAIR), lax.rem(i, PAIR), 1 - c))
            return carry

        lax.fori_loop(0, LINE * PAIR, body, 0)

    def drain(k):
        def body(zz, carry):
            each_send(k, zz, lambda x: x.wait_send())
            copy(k, slot(zz, 1 - y, c), sib, LINE + zz, slot(z, y, 1 - c)).wait_send()
            return carry

        lax.fori_loop(0, LINE, body, 0)

    return step, finish, drain


def layer_kernel(
    q_ref, qr_ref, cache_ref, rot_ref, len_ref, resid_ref, gain_ref, ids_ref, weights_ref, wvo_hbm, wgu_hbm, wdn_hbm,
    out_ref,
    wvo, wgu, wdn, heads, gathered, partial, partner, outgoing, incoming, stream,
    tokens, rows_send, rows_recv, back_out, back_in,
    w_sem, g_up, g_down, g_side, g_sib, g_recv, t_up, t_down, t_side, t_sib, t_recv,
    x_sem, y_send, y_recv, a_send, a_recv, b_send, b_recv,
):
    n = LINE * PAIR * CORE
    h, me = lax.axis_index("head"), lax.axis_index("expert")
    z, y, c = lax.div(me, PAIR * CORE), lax.rem(lax.div(me, CORE), PAIR), lax.rem(me, CORE)
    seqs, width = resid_ref.shape
    per_chunk, latent = gathered.shape[2], gathered.shape[4]
    cols = partial.shape[1]
    half = out_ref.shape[1]
    piece = half // (PARTS * 2)
    span = width // PARTS
    top = ids_ref.shape[1]
    capacity = rows_send.shape[1] // n
    f32, bf16 = jnp.float32, jnp.bfloat16

    loads = [
        pltpu.make_async_copy(src, dst, w_sem.at[i])
        for i, (src, dst) in enumerate(((wvo_hbm, wvo), (wgu_hbm, wgu), (wdn_hbm, wdn)))
    ]
    for load in loads:
        load.start()

    barrier = pltpu.get_barrier_semaphore()

    def greet(o, carry):
        pl.semaphore_signal(
            barrier, inc=1, device_id={"expert": lax.rem(me + o, n)}, device_id_type=MESH
        )
        return carry

    lax.fori_loop(1, n, greet, 0)
    pl.semaphore_signal(barrier, inc=1, device_id={"head": 1 - h}, device_id_type=MESH)

    count = q_ref.shape[1]
    slot = lax.broadcasted_iota(jnp.int32, (count, cache_ref.shape[1]), 1)
    for s in range(seqs):
        cache = cache_ref[s]
        scores = lax.dot_general(
            q_ref[s], cache, (((1,), (1,)), ((), ())), preferred_element_type=f32
        )
        scores = scores + jnp.dot(qr_ref[s], rot_ref[s], preferred_element_type=f32)
        scores = jnp.where(slot < len_ref[s : s + 1, :], scores * softmax_scale, -1e30)
        raised = jnp.exp(scores - jnp.max(scores, axis=1, keepdims=True))
        probs = (raised / jnp.sum(raised, axis=1, keepdims=True)).astype(bf16)
        heads[:, s, :] = jnp.dot(probs, cache, preferred_element_type=f32)
    for k in range(CHUNKS):
        gathered[k, me] = heads[k * per_chunk : (k + 1) * per_chunk].astype(bf16)
    partial[...] = jnp.zeros_like(partial)
    pl.semaphore_wait(barrier, n)

    step, finish, drain = spread(z, y, c, gathered, g_up, g_down, g_side, g_sib, g_recv)
    step(0, 0)
    step(1, 0)

    def turn(t, carry):
        for d in range(LINE, -1, -1):
            k = t - d if d else t + 1

            @pl.when(jnp.logical_and(k >= 0, k < CHUNKS))
            def _():
                step(k, d)

        @pl.when(t == LINE)
        def _():
            loads[0].wait()

        @pl.when(t >= LINE)
        def _():
            k = t - LINE
            finish(k)
            for j in range(0, per_chunk, 2):
                x = jnp.concatenate(
                    [rows_of(gathered[k, :, j]), rows_of(gathered[k, :, j + 1])], axis=1
                )
                start = pl.multiple_of((k * per_chunk + j) * latent, 2 * latent)
                partial[...] += lax.dot_general(
                    x, wvo[:, pl.ds(start, 2 * latent)], (((1,), (1,)), ((), ())),
                    preferred_element_type=f32,
                )

        return carry

    lax.fori_loop(1, CHUNKS + LINE, turn, 0)

    swap = pltpu.make_async_remote_copy(
        src_ref=partial, dst_ref=partner, send_sem=x_sem.at[0], recv_sem=x_sem.at[1],
        device_id={"head": 1 - h}, device_id_type=MESH,
    )
    swap.start()
    swap.wait_recv()
    outgoing[...] = blocks_of(partial[...] + partner[...], n)

    def owner(o, source, target, send, recv):
        to = lax.rem(me + o, n)
        return pltpu.make_async_remote_copy(
            src_ref=source.at[to], dst_ref=target.at[me], send_sem=send.at[to],
            recv_sem=recv.at[me], device_id={"expert": to}, device_id_type=MESH,
        )

    def exchange_start(source, target, send, recv):
        def body(o, carry):
            owner(o, source, target, send, recv).start()
            return carry

        lax.fori_loop(1, n, body, 0)

    def exchange_recv(source, target, send, recv):
        def body(o, carry):
            who = lax.rem(me + o, n)
            pltpu.make_async_remote_copy(
                src_ref=source.at[who], dst_ref=target.at[who], send_sem=send.at[who],
                recv_sem=recv.at[who], device_id={"expert": who}, device_id_type=MESH,
            ).wait_recv()
            return carry

        lax.fori_loop(1, n, body, 0)

    def exchange_sent(source, target, send, recv):
        def body(o, carry):
            owner(o, source, target, send, recv).wait_send()
            return carry

        lax.fori_loop(1, n, body, 0)

    exchange_start(outgoing, incoming, a_send, a_recv)
    incoming[me] = outgoing[me]
    ids = ids_ref[...]
    lane = lax.broadcasted_iota(jnp.int32, (seqs, EXTRA), 1)
    named = jnp.zeros((seqs, EXTRA), f32)
    for k in range(top):
        named = named + jnp.where(ids[:, k : k + 1] == lane, 1.0, 0.0)
    exchange_recv(outgoing, incoming, a_send, a_recv)

    for e in range(n):
        stream[:, e * cols : (e + 1) * cols] = incoming[e].astype(f32)
    rows = stream[...] + resid_ref[...].astype(f32)
    stream[...] = rows
    mean_square = jnp.sum(rows * rows, axis=1, keepdims=True) * (1.0 / width)
    normed = rows * lax.rsqrt(mean_square + norm_epsilon) * gain_ref[...]
    for k in range(PARTS):
        tokens[k, me, :, :span] = normed[:, k * span : (k + 1) * span].astype(bf16)
        tokens[k, me, :, span:] = named.astype(bf16)

    t_step, t_finish, t_drain = spread(z, y, c, tokens, t_up, t_down, t_side, t_sib, t_recv)
    for d in range(LINE + 1):
        for k in range(PARTS):
            t_step(k, d)

    wide = n * 2 * SLOTS
    place = lax.broadcasted_iota(jnp.int32, (seqs, wide), 1)
    which, part, at = place // (2 * SLOTS), (place // SLOTS) % 2, place % SLOTS
    hit = jnp.zeros((seqs, wide), f32)
    share = jnp.zeros((seqs, wide), f32)
    for k in range(top):
        same = ids[:, k : k + 1] == which
        hit = hit + jnp.where(same, 1.0, 0.0)
        share = share + jnp.where(same, weights_ref[:, k : k + 1], 0.0)
    token = lax.broadcasted_iota(jnp.int32, (seqs, wide), 0)
    rank = jnp.zeros((seqs, wide), f32)
    for t in range(seqs - 1):
        rank = rank + jnp.where(token > t, hit[t : t + 1, :], 0.0)
    blend = jnp.where(rank == at.astype(f32), share, 0.0)

    t_finish(0)
    loads[1].wait()

    total = n * seqs
    flags = rows_of(tokens[0, :, :, span:])
    mine = jnp.where(lax.broadcasted_iota(jnp.int32, (8, EXTRA), 1) == me, 1.0, 0.0).astype(bf16)
    chosen = lax.dot_general(mine, flags, (((1,), (1,)), ((), ())), preferred_element_type=f32)
    first = lax.broadcasted_iota(jnp.int32, (total, total), 0)
    second = lax.broadcasted_iota(jnp.int32, (total, total), 1)
    ahead = jnp.where(
        jnp.logical_and(first < second, first // seqs == second // seqs), 1.0, 0.0
    ).astype(bf16)
    order = jnp.dot(chosen.astype(bf16), ahead, preferred_element_type=f32)
    count = capacity * n
    row = lax.broadcasted_iota(jnp.int32, (count, total), 0)
    tok = lax.broadcasted_iota(jnp.int32, (count, total), 1)
    fits = jnp.logical_and(order[0:1, :] == (row // n).astype(f32), tok // seqs == row % n)
    pick = jnp.where(fits, chosen[0:1, :], 0.0).astype(bf16)

    units = wgu.shape[1]
    gate = jnp.zeros((count, units), f32)
    lift = jnp.zeros((count, units), f32)
    for k in range(PARTS):
        if k > 0:
            t_finish(k)
        for j in range(2):
            lanes = slice(j * span // 2, (j + 1) * span // 2)
            deep = slice(k * span + j * span // 2, k * span + (j + 1) * span // 2)
            x = jnp.dot(pick, rows_of(tokens[k, :, :, lanes]), preferred_element_type=f32)
            x = x.astype(bf16)
            gate += lax.dot_general(
                x, wgu[0, :, deep], (((1,), (1,)), ((), ())), preferred_element_type=f32
            )
            lift += lax.dot_general(
                x, wgu[1, :, deep], (((1,), (1,)), ((), ())), preferred_element_type=f32
            )
    hidden = (gate / (1.0 + jnp.exp(-gate)) * lift).astype(bf16)
    loads[2].wait()
    share_cols = half // PARTS

    def trade(p):
        return pltpu.make_async_remote_copy(
            src_ref=rows_send.at[p], dst_ref=rows_recv.at[p], send_sem=y_send.at[p],
            recv_sem=y_recv.at[p], device_id={"head": 1 - h}, device_id_type=MESH,
        )

    for p in range(PARTS):
        theirs = pl.ds(pl.multiple_of((1 - h) * half + p * share_cols, share_cols), share_cols)
        rows_send[p] = jnp.dot(hidden, wdn[:, theirs], preferred_element_type=f32).astype(bf16)
        trade(p).start()
    ours = pl.ds(pl.multiple_of(h * half, half), half)
    own = jnp.dot(hidden, wdn[:, ours], preferred_element_type=f32)
    dest = lax.broadcasted_iota(jnp.int32, (n * 2 * SLOTS, count), 0)
    from_row = lax.broadcasted_iota(jnp.int32, (n * 2 * SLOTS, count), 1)
    home = from_row == (dest % SLOTS) * n + dest // (2 * SLOTS)
    upper = (dest // SLOTS) % 2
    puts = [
        jnp.where(jnp.logical_and(home, upper == a), 1.0, 0.0).astype(bf16) for a in range(2)
    ]
    for p in range(PARTS):
        trade(p).wait_recv()
        summed = own[:, p * share_cols : (p + 1) * share_cols] + rows_recv[p].astype(f32)
        summed = summed.astype(bf16)
        back = jnp.dot(puts[0], summed[:, :piece], preferred_element_type=f32)
        back = back + jnp.dot(puts[1], summed[:, piece:], preferred_element_type=f32)
        back_out[p] = blocks_of(back, n)
        exchange_start(back_out.at[p], back_in.at[p], b_send.at[p], b_recv.at[p])
        back_in[p, me] = back_out[p, me]

    mixes = []
    for a in range(2):
        mix = jnp.where(part == a, blend, 0.0)
        high = mix.astype(bf16)
        mixes.append((high, (mix - high.astype(f32)).astype(bf16)))
    for p in range(PARTS):
        exchange_recv(back_out.at[p], back_in.at[p], b_send.at[p], b_recv.at[p])
        returned = rows_of(back_in[p])
        for a in range(2):
            added = jnp.dot(mixes[a][0], returned, preferred_element_type=f32)
            added = added + jnp.dot(mixes[a][1], returned, preferred_element_type=f32)
            here = p * share_cols + a * piece
            start = pl.multiple_of(h * half + here, piece)
            out_ref[:, here : here + piece] = stream[:, pl.ds(start, piece)] + added

    for k in range(CHUNKS):
        drain(k)
    swap.wait_send()
    exchange_sent(outgoing, incoming, a_send, a_recv)
    for p in range(PARTS):
        t_drain(p)
        trade(p).wait_send()
        exchange_sent(back_out.at[p], back_in.at[p], b_send.at[p], b_recv.at[p])


def fused(q_latent, q_rotary, cache_latent, cache_rotary, lengths, resid, norm_gain, route_ids, route_weights, w_value_out,
          w_gate_up, w_down):
    n = LINE * PAIR * CORE
    seqs, width = resid.shape
    head_count, latent = q_latent.shape[1:]
    cols = w_value_out.shape[1]
    half = width // 2
    capacity = -(-(seqs * route_ids.shape[1]) // n)
    gate_up, down = w_gate_up[0], w_down[0]
    bf16, f32 = jnp.bfloat16, jnp.float32
    vmem, anywhere = pl.BlockSpec(memory_space=pltpu.VMEM), pl.BlockSpec(memory_space=pl.ANY)
    dma = pltpu.SemaphoreType.DMA
    return pl.pallas_call(
        layer_kernel,
        out_shape=jax.ShapeDtypeStruct((seqs, half), f32),
        in_specs=[vmem] * 9 + [anywhere] * 3,
        out_specs=vmem,
        scratch_shapes=[
            pltpu.VMEM(w_value_out.shape[::-1], bf16),
            pltpu.VMEM(gate_up.shape, bf16),
            pltpu.VMEM(down.shape, bf16),
            pltpu.VMEM((head_count, seqs, latent), f32),
            pltpu.VMEM((CHUNKS, n, head_count // CHUNKS, seqs, latent), bf16),
            pltpu.VMEM((n * seqs, cols), f32),
            pltpu.VMEM((n * seqs, cols), f32),
            pltpu.VMEM((n, seqs, cols), bf16),
            pltpu.VMEM((n, seqs, cols), bf16),
            pltpu.VMEM((seqs, width), f32),
            pltpu.VMEM((PARTS, n, seqs, width // PARTS + EXTRA), bf16),
            pltpu.VMEM((PARTS, capacity * n, half // PARTS), bf16),
            pltpu.VMEM((PARTS, capacity * n, half // PARTS), bf16),
            pltpu.VMEM((PARTS, n, 2 * SLOTS, half // (2 * PARTS)), bf16),
            pltpu.VMEM((PARTS, n, 2 * SLOTS, half // (2 * PARTS)), bf16),
            dma((3,)),
            dma((CHUNKS, LINE)), dma((CHUNKS, LINE)), dma((CHUNKS, LINE)),
            dma((CHUNKS, PAIR * LINE)), dma((CHUNKS, n)),
            dma((PARTS, LINE)), dma((PARTS, LINE)), dma((PARTS, LINE)),
            dma((PARTS, PAIR * LINE)), dma((PARTS, n)),
            dma((2,)), dma((PARTS,)), dma((PARTS,)), dma((n,)), dma((n,)),
            dma((PARTS, n)), dma((PARTS, n)),
        ],
        compiler_params=pltpu.CompilerParams(
            collective_id=0, has_side_effects=True, vmem_limit_bytes=56 * 1024 * 1024
        ),
    )(
        q_latent, q_rotary, cache_latent, cache_rotary, lengths[:, None], resid,
        norm_gain[None, :], route_ids, route_weights, w_value_out.T, gate_up, down,
    )


def attend(q_latent, q_rotary, cache_latent, cache_rotary, lengths):
    scores = jnp.einsum("shl,scl->shc", q_latent, cache_latent, preferred_element_type=jnp.float32)
    scores = scores + jnp.einsum(
        "shr,src->shc", q_rotary, cache_rotary, preferred_element_type=jnp.float32
    )
    scores = scores * softmax_scale
    position = lax.broadcasted_iota(jnp.int32, scores.shape, 2)
    scores = jnp.where(position < lengths[:, None, None], scores, -1e30)
    highest = jnp.max(scores, axis=2, keepdims=True)
    weights = jnp.exp(scores - highest)
    probs = (weights / jnp.sum(weights, axis=2, keepdims=True)).astype(jnp.bfloat16)
    return jnp.einsum(
        "shc,scl->shl", probs, cache_latent, preferred_element_type=jnp.float32
    ).astype(jnp.bfloat16)


def on_device(
    q_latent,
    q_rotary,
    cache_latent,
    cache_rotary,
    lengths,
    w_value_out,
    resid,
    norm_gain,
    route_ids,
    route_weights,
    w_gate_up,
    w_down,
):
    seq_local = q_latent.shape[0]
    if (
        lax.axis_size("head") == 2
        and lax.axis_size("expert") == LINE * PAIR * CORE
        and seq_local == 8
    ):
        return fused(
            q_latent, q_rotary, cache_latent, cache_rotary, lengths, resid, norm_gain,
            route_ids, route_weights, w_value_out, w_gate_up, w_down,
        )
    latent_out = attend(q_latent, q_rotary, cache_latent, cache_rotary, lengths)
    flattened = latent_out.reshape(seq_local, -1)
    column_terms = jnp.dot(
        lax.all_gather(flattened, "expert", axis=0, tiled=True),
        w_value_out,
        preferred_element_type=jnp.float32,
    )
    column_sums = lax.psum(column_terms, "head")
    attention = lax.all_to_all(
        column_sums.astype(jnp.bfloat16), "expert", split_axis=0, concat_axis=1, tiled=True
    )
    stream = resid.astype(jnp.float32) + attention.astype(jnp.float32)
    mean_square = jnp.mean(stream * stream, axis=1, keepdims=True)
    normed = (stream * lax.rsqrt(mean_square + norm_epsilon) * norm_gain).astype(jnp.bfloat16)
    expert_count = lax.axis_size("expert")
    top_count = route_ids.shape[1]
    capacity = max(2, -(-(seq_local * top_count) // expert_count))
    flat_ids = route_ids.reshape(-1)
    one_hot = (flat_ids[:, None] == jnp.arange(expert_count, dtype=jnp.int32)[None, :]).astype(
        jnp.int32
    )
    earlier = jnp.cumsum(one_hot, axis=0) - one_hot
    slot_index = jnp.sum(earlier * one_hot, axis=1)
    target = (flat_ids * capacity + slot_index).reshape(seq_local, top_count)
    places = jnp.arange(expert_count * capacity, dtype=jnp.int32)
    matches = target[None, :, :] == places[:, None, None]
    selector = jnp.sum(matches.astype(jnp.int32), axis=2).astype(jnp.bfloat16)
    blending = jnp.sum(jnp.where(matches, route_weights[None, :, :], 0.0), axis=2)
    outgoing = jnp.dot(selector, normed, preferred_element_type=jnp.float32).astype(jnp.bfloat16)
    outgoing = outgoing.reshape(expert_count, capacity, -1)
    gate_up = w_gate_up[0]
    down_local = w_down[0]
    col_width = stream.shape[1] // lax.axis_size("head")
    offset = lax.axis_index("head") * col_width
    arrived = lax.all_to_all(outgoing, "expert", split_axis=0, concat_axis=0, tiled=True)
    flat_rows = arrived.reshape(-1, arrived.shape[2])
    projected = jnp.einsum("rd,gfd->rgf", flat_rows, gate_up, preferred_element_type=jnp.float32)
    hidden = (jax.nn.silu(projected[:, 0]) * projected[:, 1]).astype(jnp.bfloat16)
    partial_rows = jnp.dot(hidden, down_local, preferred_element_type=jnp.float32)
    expert_terms = partial_rows.reshape(arrived.shape[0], arrived.shape[1], -1)
    summed_rows = lax.psum(expert_terms.astype(jnp.bfloat16), "head")
    returned = lax.all_to_all(summed_rows, "expert", split_axis=0, concat_axis=0, tiled=True)
    back_rows = returned.reshape(expert_count * capacity, -1).astype(jnp.float32)
    mixture = jnp.dot(blending.T, back_rows, precision=lax.Precision.HIGHEST)
    mixed_full = stream + mixture
    return lax.dynamic_slice_in_dim(mixed_full, offset, col_width, 1)


def solution(mesh):
    placed = (
        P("expert", "head", None),
        P("expert", "head", None),
        P("expert", None, None),
        P("expert", None, None),
        P("expert"),
        P("head", "expert"),
        P("expert", None),
        P(),
        P("expert", None),
        P("expert", None),
        P("expert", None, "head", None),
        P("expert", "head", None),
    )
    return jax.shard_map(
        on_device, mesh=mesh, in_specs=placed, out_specs=P("expert", "head"), check_vma=False
    )
```

```python
import functools

import jax
import jax.numpy as jnp
from jax import lax
from jax.experimental import pallas as pl
from jax.experimental.pallas import tpu as pltpu
from jax.sharding import PartitionSpec as P

MESH = pl.DeviceIdType.MESH
softmax_scale = 192.0 ** (-0.5)
norm_epsilon = 1e-06

LINE, PAIR, CORE = 4, 2, 2
CHUNKS = 4
EXTRA = 128
ROWS = 16
PARTS = 2


def rows_of(blocks):
    n, r, c = blocks.shape
    return blocks.astype(jnp.float32).reshape(n * r, c).astype(jnp.bfloat16)


def blocks_of(rows, n):
    return rows.reshape(n, rows.shape[0] // n, rows.shape[1]).astype(jnp.bfloat16)


def spread(z, y, c, far, buffers, up, down, side, sib, recv):
    def slot(zz, yy, cc):
        return (zz * PAIR + yy) * CORE + cc

    def copy(k, s, sems, index, target):
        return pltpu.make_async_remote_copy(
            src_ref=buffers.at[k, s],
            dst_ref=buffers.at[k, s],
            send_sem=sems.at[k, index],
            recv_sem=recv.at[k, s],
            device_id={"expert": target},
            device_id_type=MESH,
        )

    def each_send(k, zz, act):
        s = slot(zz, y, c)

        @pl.when(jnp.logical_and(zz <= z, z < LINE - 1))
        def _():
            act(copy(k, s, up, zz, slot(z + 1, y, c)))

        @pl.when(jnp.logical_and(zz >= z, z > 0))
        def _():
            act(copy(k, s, down, zz, slot(z - 1, y, c)))

        ends = jnp.logical_or(zz == 0, zz == LINE - 1)
        along = jnp.logical_and(jnp.logical_and(k < far, ends), zz != z)

        @pl.when(jnp.logical_not(along))
        def _():
            act(copy(k, s, side, zz, slot(z, 1 - y, c)))

        act(copy(k, s, sib, zz, slot(z, y, 1 - c)))

    def each_across(k, zz, act):
        s = slot(zz, 1 - y, c)

        @pl.when(jnp.logical_and(k < far, jnp.logical_and(zz == 0, z < LINE - 1)))
        def _():
            act(copy(k, s, up, LINE + zz, slot(z + 1, y, c)))

        @pl.when(jnp.logical_and(k < far, jnp.logical_and(zz == LINE - 1, z > 0)))
        def _():
            act(copy(k, s, down, LINE + zz, slot(z - 1, y, c)))

        act(copy(k, s, sib, LINE + zz, slot(z, y, 1 - c)))

    def arrived(k, s):
        copy(k, s, sib, 0, slot(z, y, 1 - c)).wait_recv()

    def at_distance(d, act):
        if d == 0:
            act(z)
            return

        @pl.when(z - d >= 0)
        def _():
            act(z - d)

        @pl.when(z + d < LINE)
        def _():
            act(z + d)

    def step(k, d):
        def line(zz):
            if d > 0:
                arrived(k, slot(zz, y, c))
            each_send(k, zz, lambda x: x.start())

        def across(zz):
            arrived(k, slot(zz, 1 - y, c))
            each_across(k, zz, lambda x: x.start())

        if d < LINE:
            at_distance(d, line)
        if d > 0:
            at_distance(d - 1, across)

    def finish(k):
        def body(i, carry):
            arrived(k, slot(lax.div(i, PAIR), lax.rem(i, PAIR), 1 - c))
            return carry

        lax.fori_loop(0, LINE * PAIR, body, 0)

    def drain(k):
        def body(zz, carry):
            each_send(k, zz, lambda x: x.wait_send())
            each_across(k, zz, lambda x: x.wait_send())
            return carry

        lax.fori_loop(0, LINE, body, 0)

    return step, finish, drain


def layer_kernel(
    q_ref, qr_ref, cache_ref, rot_ref, len_ref, resid_ref, gain_ref, ids_ref, weights_ref, wvo_hbm, wgu_hbm, wdn_hbm,
    out_ref,
    wvo, wgu, wdn, heads, gathered, partial, partner, last, last_partner, outgoing, incoming, stream,
    tokens, rows_send, rows_recv, back_out, back_in,
    w_sem, g_up, g_down, g_side, g_sib, g_recv, t_up, t_down, t_side, t_sib, t_recv,
    x_sem, y_send, y_recv, a_send, a_recv, b_send, b_recv,
):
    n = LINE * PAIR * CORE
    h, me = lax.axis_index("head"), lax.axis_index("expert")
    z, y, c = lax.div(me, PAIR * CORE), lax.rem(lax.div(me, CORE), PAIR), lax.rem(me, CORE)
    seqs, width = resid_ref.shape
    per_chunk, latent = gathered.shape[2], gathered.shape[4]
    cols = partial.shape[2]
    half = out_ref.shape[1]
    span = width // PARTS
    top = ids_ref.shape[1]
    capacity = rows_send.shape[1] // n
    pieces = ROWS // capacity
    piece = half // (PARTS * pieces)
    f32, bf16 = jnp.float32, jnp.bfloat16

    loads = [
        pltpu.make_async_copy(src, dst, w_sem.at[i])
        for i, (src, dst) in enumerate(((wvo_hbm, wvo), (wgu_hbm, wgu), (wdn_hbm, wdn)))
    ]
    for load in loads:
        load.start()

    barrier = pltpu.get_barrier_semaphore()

    def greet(o, carry):
        pl.semaphore_signal(
            barrier, inc=1, device_id={"expert": lax.rem(me + o, n)}, device_id_type=MESH
        )
        return carry

    lax.fori_loop(1, n, greet, 0)
    pl.semaphore_signal(barrier, inc=1, device_id={"head": 1 - h}, device_id_type=MESH)

    count = q_ref.shape[1]
    slot = lax.broadcasted_iota(jnp.int32, (count, cache_ref.shape[1]), 1)
    parts = []
    for s in range(seqs):
        scores = lax.dot_general(
            q_ref[s], cache_ref[s], (((1,), (1,)), ((), ())), preferred_element_type=f32
        )
        scores = scores + jnp.dot(qr_ref[s], rot_ref[s], preferred_element_type=f32)
        parts.append(jnp.where(slot < len_ref[s], scores * softmax_scale, -1e30))
    scores = jnp.concatenate(parts, axis=0)
    raised = jnp.exp(scores - jnp.max(scores, axis=1, keepdims=True))
    probs = (raised / jnp.sum(raised, axis=1, keepdims=True)).astype(bf16)
    for s in range(seqs):
        heads[:, s, :] = jnp.dot(
            probs[s * count : (s + 1) * count], cache_ref[s], preferred_element_type=f32
        )
    for k in range(CHUNKS):
        gathered[k, me] = heads[k * per_chunk : (k + 1) * per_chunk].astype(bf16)
    partial[...] = jnp.zeros_like(partial)
    pl.semaphore_wait(barrier, n)

    step, finish, drain = spread(z, y, c, CHUNKS // 2, gathered, g_up, g_down, g_side, g_sib, g_recv)
    swap = pltpu.make_async_remote_copy(
        src_ref=partial.at[0], dst_ref=partner, send_sem=x_sem.at[0], recv_sem=x_sem.at[1],
        device_id={"head": 1 - h}, device_id_type=MESH,
    )
    swap_last = pltpu.make_async_remote_copy(
        src_ref=last, dst_ref=last_partner, send_sem=x_sem.at[2], recv_sem=x_sem.at[3],
        device_id={"head": 1 - h}, device_id_type=MESH,
    )
    step(0, 0)
    step(1, 0)

    def turn(t, carry):
        for d in range(LINE, -1, -1):
            k = t - d if d else t + 1

            @pl.when(jnp.logical_and(k >= 0, k < CHUNKS))
            def _():
                step(k, d)

        @pl.when(t == LINE)
        def _():
            loads[0].wait()

        @pl.when(t >= LINE)
        def _():
            k = t - LINE
            finish(k)
            total = partial.at[k // (CHUNKS - 1)]
            for j in range(0, per_chunk, 2):
                x = jnp.concatenate(
                    [rows_of(gathered[k, :, j]), rows_of(gathered[k, :, j + 1])], axis=1
                )
                start = pl.multiple_of((k * per_chunk + j) * latent, 2 * latent)
                total[...] += lax.dot_general(
                    x, wvo[:, pl.ds(start, 2 * latent)], (((1,), (1,)), ((), ())),
                    preferred_element_type=f32,
                )

            @pl.when(k == CHUNKS - 2)
            def _():
                swap.start()

        return carry

    lax.fori_loop(1, CHUNKS + LINE, turn, 0)

    last[...] = partial[1].astype(bf16)
    swap_last.start()
    for k in range(CHUNKS):
        drain(k)
    swap.wait_recv()
    sums = partial[0] + partial[1] + partner[...]
    swap_last.wait_recv()
    outgoing[...] = blocks_of(sums + last_partner[...].astype(f32), n)

    def owner(o, source, target, send, recv):
        to = lax.rem(me + o, n)
        return pltpu.make_async_remote_copy(
            src_ref=source.at[to], dst_ref=target.at[me], send_sem=send.at[to],
            recv_sem=recv.at[me], device_id={"expert": to}, device_id_type=MESH,
        )

    def exchange_start(source, target, send, recv):
        def body(o, carry):
            owner(o, source, target, send, recv).start()
            return carry

        lax.fori_loop(1, n, body, 0)

    def exchange_recv(source, target, send, recv):
        def body(o, carry):
            who = lax.rem(me + o, n)
            pltpu.make_async_remote_copy(
                src_ref=source.at[who], dst_ref=target.at[who], send_sem=send.at[who],
                recv_sem=recv.at[who], device_id={"expert": who}, device_id_type=MESH,
            ).wait_recv()
            return carry

        lax.fori_loop(1, n, body, 0)

    def exchange_sent(source, target, send, recv):
        def body(o, carry):
            owner(o, source, target, send, recv).wait_send()
            return carry

        lax.fori_loop(1, n, body, 0)

    exchange_start(outgoing, incoming, a_send, a_recv)
    incoming[me] = outgoing[me]
    ids = ids_ref[...]
    lane = lax.broadcasted_iota(jnp.int32, (seqs, EXTRA), 1)
    named = jnp.zeros((seqs, EXTRA), f32)
    for k in range(top):
        named = named + jnp.where(ids[:, k : k + 1] == lane, 1.0, 0.0)
    exchange_recv(outgoing, incoming, a_send, a_recv)

    for e in range(n):
        stream[:, e * cols : (e + 1) * cols] = incoming[e].astype(f32)
    rows = stream[...] + resid_ref[...].astype(f32)
    stream[...] = rows
    mean_square = jnp.sum(rows * rows, axis=1, keepdims=True) * (1.0 / width)
    normed = rows * lax.rsqrt(mean_square + norm_epsilon) * gain_ref[...]
    for k in range(PARTS):
        tokens[k, me, :, :span] = normed[:, k * span : (k + 1) * span].astype(bf16)
        tokens[k, me, :, span:] = named.astype(bf16)

    t_step, t_finish, t_drain = spread(z, y, c, PARTS // 2, tokens, t_up, t_down, t_side, t_sib, t_recv)
    for d in range(LINE + 1):
        for k in range(PARTS):
            t_step(k, d)

    wide = n * ROWS
    place = lax.broadcasted_iota(jnp.int32, (seqs, wide), 1)
    which, at = place // ROWS, place % ROWS
    hit = jnp.zeros((seqs, wide), f32)
    share = jnp.zeros((seqs, wide), f32)
    for k in range(top):
        same = ids[:, k : k + 1] == which
        hit = hit + jnp.where(same, 1.0, 0.0)
        share = share + jnp.where(same, weights_ref[:, k : k + 1], 0.0)
    token = lax.broadcasted_iota(jnp.int32, (seqs, wide), 0)
    rank = jnp.zeros((seqs, wide), f32)
    for t in range(seqs - 1):
        rank = rank + jnp.where(token > t, hit[t : t + 1, :], 0.0)
    mixes = []
    for a in range(pieces):
        mix = jnp.where(rank == (at - a * capacity).astype(f32), share, 0.0)
        high = mix.astype(bf16)
        mixes.append((high, (mix - high.astype(f32)).astype(bf16)))
    swap.wait_send()
    swap_last.wait_send()
    exchange_sent(outgoing, incoming, a_send, a_recv)

    t_finish(0)
    loads[1].wait()

    total = n * seqs
    flags = rows_of(tokens[0, :, :, span:])
    mine = jnp.where(lax.broadcasted_iota(jnp.int32, (8, EXTRA), 1) == me, 1.0, 0.0).astype(bf16)
    chosen = lax.dot_general(mine, flags, (((1,), (1,)), ((), ())), preferred_element_type=f32)
    first = lax.broadcasted_iota(jnp.int32, (total, total), 0)
    second = lax.broadcasted_iota(jnp.int32, (total, total), 1)
    ahead = jnp.where(
        jnp.logical_and(first < second, first // seqs == second // seqs), 1.0, 0.0
    ).astype(bf16)
    order = jnp.dot(chosen.astype(bf16), ahead, preferred_element_type=f32)
    count = capacity * n
    row = lax.broadcasted_iota(jnp.int32, (count, total), 0)
    tok = lax.broadcasted_iota(jnp.int32, (count, total), 1)
    fits = jnp.logical_and(order[0:1, :] == (row // n).astype(f32), tok // seqs == row % n)
    pick = jnp.where(fits, chosen[0:1, :], 0.0).astype(bf16)

    units = wgu.shape[1]
    gate = jnp.zeros((count, units), f32)
    lift = jnp.zeros((count, units), f32)
    for k in range(PARTS):
        if k > 0:
            t_finish(k)
        for j in range(2):
            lanes = slice(j * span // 2, (j + 1) * span // 2)
            deep = slice(k * span + j * span // 2, k * span + (j + 1) * span // 2)
            x = jnp.dot(pick, rows_of(tokens[k, :, :, lanes]), preferred_element_type=f32)
            x = x.astype(bf16)
            gate += lax.dot_general(
                x, wgu[0, :, deep], (((1,), (1,)), ((), ())), preferred_element_type=f32
            )
            lift += lax.dot_general(
                x, wgu[1, :, deep], (((1,), (1,)), ((), ())), preferred_element_type=f32
            )
    hidden = (gate / (1.0 + jnp.exp(-gate)) * lift).astype(bf16)
    loads[2].wait()
    share_cols = half // PARTS

    def trade(p):
        return pltpu.make_async_remote_copy(
            src_ref=rows_send.at[p], dst_ref=rows_recv.at[p], send_sem=y_send.at[p],
            recv_sem=y_recv.at[p], device_id={"head": 1 - h}, device_id_type=MESH,
        )

    for p in range(PARTS):
        theirs = pl.ds(pl.multiple_of((1 - h) * half + p * share_cols, share_cols), share_cols)
        rows_send[p] = jnp.dot(hidden, wdn[:, theirs], preferred_element_type=f32).astype(bf16)
        trade(p).start()
    ours = pl.ds(pl.multiple_of(h * half, half), half)
    own = jnp.dot(hidden, wdn[:, ours], preferred_element_type=f32)
    dest = lax.broadcasted_iota(jnp.int32, (wide, count), 0)
    from_row = lax.broadcasted_iota(jnp.int32, (wide, count), 1)
    home = (from_row % n) * ROWS + from_row // n
    puts = [jnp.where(dest == home + a * capacity, 1.0, 0.0).astype(bf16) for a in range(pieces)]
    for p in range(PARTS):
        t_drain(p)
    for p in range(PARTS):
        trade(p).wait_recv()
        summed = own[:, p * share_cols : (p + 1) * share_cols] + rows_recv[p].astype(f32)
        summed = summed.astype(bf16)
        back = jnp.zeros((wide, piece), f32)
        for a in range(pieces):
            columns = summed[:, a * piece : (a + 1) * piece]
            back = back + jnp.dot(puts[a], columns, preferred_element_type=f32)
        back_out[p] = blocks_of(back, n)
        exchange_start(back_out.at[p], back_in.at[p], b_send.at[p], b_recv.at[p])
        back_in[p, me] = back_out[p, me]

    for p in range(PARTS):
        exchange_recv(back_out.at[p], back_in.at[p], b_send.at[p], b_recv.at[p])
        returned = rows_of(back_in[p])
        for a in range(pieces):
            added = jnp.dot(mixes[a][0], returned, preferred_element_type=f32)
            added = added + jnp.dot(mixes[a][1], returned, preferred_element_type=f32)
            here = p * share_cols + a * piece
            start = pl.multiple_of(h * half + here, piece)
            out_ref[:, here : here + piece] = stream[:, pl.ds(start, piece)] + added

    for p in range(PARTS):
        trade(p).wait_send()
        exchange_sent(back_out.at[p], back_in.at[p], b_send.at[p], b_recv.at[p])


def fused(q_latent, q_rotary, cache_latent, cache_rotary, lengths, resid, norm_gain, route_ids, route_weights, w_value_out,
          w_gate_up, w_down):
    n = LINE * PAIR * CORE
    seqs, width = resid.shape
    head_count, latent = q_latent.shape[1:]
    cols = w_value_out.shape[1]
    half = width // 2
    capacity = -(-(seqs * route_ids.shape[1]) // n)
    gate_up, down = w_gate_up[0], w_down[0]
    bf16, f32 = jnp.bfloat16, jnp.float32
    vmem, anywhere = pl.BlockSpec(memory_space=pltpu.VMEM), pl.BlockSpec(memory_space=pl.ANY)
    dma = pltpu.SemaphoreType.DMA
    return pl.pallas_call(
        layer_kernel,
        out_shape=jax.ShapeDtypeStruct((seqs, half), f32),
        in_specs=[vmem] * 4 + [pl.BlockSpec(memory_space=pltpu.SMEM)] + [vmem] * 4 + [anywhere] * 3,
        out_specs=vmem,
        scratch_shapes=[
            pltpu.VMEM(w_value_out.shape[::-1], bf16),
            pltpu.VMEM(gate_up.shape, bf16),
            pltpu.VMEM(down.shape, bf16),
            pltpu.VMEM((head_count, seqs, latent), f32),
            pltpu.VMEM((CHUNKS, n, head_count // CHUNKS, seqs, latent), bf16),
            pltpu.VMEM((2, n * seqs, cols), f32),
            pltpu.VMEM((n * seqs, cols), f32),
            pltpu.VMEM((n * seqs, cols), bf16),
            pltpu.VMEM((n * seqs, cols), bf16),
            pltpu.VMEM((n, seqs, cols), bf16),
            pltpu.VMEM((n, seqs, cols), bf16),
            pltpu.VMEM((seqs, width), f32),
            pltpu.VMEM((PARTS, n, seqs, width // PARTS + EXTRA), bf16),
            pltpu.VMEM((PARTS, capacity * n, half // PARTS), bf16),
            pltpu.VMEM((PARTS, capacity * n, half // PARTS), bf16),
            pltpu.VMEM((PARTS, n, ROWS, half // (PARTS * (ROWS // capacity))), bf16),
            pltpu.VMEM((PARTS, n, ROWS, half // (PARTS * (ROWS // capacity))), bf16),
            dma((3,)),
            dma((CHUNKS, PAIR * LINE)), dma((CHUNKS, PAIR * LINE)), dma((CHUNKS, LINE)),
            dma((CHUNKS, PAIR * LINE)), dma((CHUNKS, n)),
            dma((PARTS, PAIR * LINE)), dma((PARTS, PAIR * LINE)), dma((PARTS, LINE)),
            dma((PARTS, PAIR * LINE)), dma((PARTS, n)),
            dma((4,)), dma((PARTS,)), dma((PARTS,)), dma((n,)), dma((n,)),
            dma((PARTS, n)), dma((PARTS, n)),
        ],
        compiler_params=pltpu.CompilerParams(
            collective_id=0, has_side_effects=True, vmem_limit_bytes=56 * 1024 * 1024
        ),
    )(
        q_latent, q_rotary, cache_latent, cache_rotary, lengths, resid,
        norm_gain[None, :], route_ids, route_weights, w_value_out.T, gate_up, down,
    )


def attend(q_latent, q_rotary, cache_latent, cache_rotary, lengths):
    scores = jnp.einsum("shl,scl->shc", q_latent, cache_latent, preferred_element_type=jnp.float32)
    scores = scores + jnp.einsum(
        "shr,src->shc", q_rotary, cache_rotary, preferred_element_type=jnp.float32
    )
    scores = scores * softmax_scale
    position = lax.broadcasted_iota(jnp.int32, scores.shape, 2)
    scores = jnp.where(position < lengths[:, None, None], scores, -1e30)
    highest = jnp.max(scores, axis=2, keepdims=True)
    weights = jnp.exp(scores - highest)
    probs = (weights / jnp.sum(weights, axis=2, keepdims=True)).astype(jnp.bfloat16)
    return jnp.einsum(
        "shc,scl->shl", probs, cache_latent, preferred_element_type=jnp.float32
    ).astype(jnp.bfloat16)


def on_device(
    q_latent,
    q_rotary,
    cache_latent,
    cache_rotary,
    lengths,
    w_value_out,
    resid,
    norm_gain,
    route_ids,
    route_weights,
    w_gate_up,
    w_down,
):
    seq_local = q_latent.shape[0]
    if (
        lax.axis_size("head") == 2
        and lax.axis_size("expert") == LINE * PAIR * CORE
        and seq_local == 8
    ):
        return fused(
            q_latent, q_rotary, cache_latent, cache_rotary, lengths, resid, norm_gain,
            route_ids, route_weights, w_value_out, w_gate_up, w_down,
        )
    latent_out = attend(q_latent, q_rotary, cache_latent, cache_rotary, lengths)
    flattened = latent_out.reshape(seq_local, -1)
    column_terms = jnp.dot(
        lax.all_gather(flattened, "expert", axis=0, tiled=True),
        w_value_out,
        preferred_element_type=jnp.float32,
    )
    column_sums = lax.psum(column_terms, "head")
    attention = lax.all_to_all(
        column_sums.astype(jnp.bfloat16), "expert", split_axis=0, concat_axis=1, tiled=True
    )
    stream = resid.astype(jnp.float32) + attention.astype(jnp.float32)
    mean_square = jnp.mean(stream * stream, axis=1, keepdims=True)
    normed = (stream * lax.rsqrt(mean_square + norm_epsilon) * norm_gain).astype(jnp.bfloat16)
    expert_count = lax.axis_size("expert")
    top_count = route_ids.shape[1]
    capacity = max(2, -(-(seq_local * top_count) // expert_count))
    flat_ids = route_ids.reshape(-1)
    one_hot = (flat_ids[:, None] == jnp.arange(expert_count, dtype=jnp.int32)[None, :]).astype(
        jnp.int32
    )
    earlier = jnp.cumsum(one_hot, axis=0) - one_hot
    slot_index = jnp.sum(earlier * one_hot, axis=1)
    target = (flat_ids * capacity + slot_index).reshape(seq_local, top_count)
    places = jnp.arange(expert_count * capacity, dtype=jnp.int32)
    matches = target[None, :, :] == places[:, None, None]
    selector = jnp.sum(matches.astype(jnp.int32), axis=2).astype(jnp.bfloat16)
    blending = jnp.sum(jnp.where(matches, route_weights[None, :, :], 0.0), axis=2)
    outgoing = jnp.dot(selector, normed, preferred_element_type=jnp.float32).astype(jnp.bfloat16)
    outgoing = outgoing.reshape(expert_count, capacity, -1)
    gate_up = w_gate_up[0]
    down_local = w_down[0]
    col_width = stream.shape[1] // lax.axis_size("head")
    offset = lax.axis_index("head") * col_width
    arrived = lax.all_to_all(outgoing, "expert", split_axis=0, concat_axis=0, tiled=True)
    flat_rows = arrived.reshape(-1, arrived.shape[2])
    projected = jnp.einsum("rd,gfd->rgf", flat_rows, gate_up, preferred_element_type=jnp.float32)
    hidden = (jax.nn.silu(projected[:, 0]) * projected[:, 1]).astype(jnp.bfloat16)
    partial_rows = jnp.dot(hidden, down_local, preferred_element_type=jnp.float32)
    expert_terms = partial_rows.reshape(arrived.shape[0], arrived.shape[1], -1)
    summed_rows = lax.psum(expert_terms.astype(jnp.bfloat16), "head")
    returned = lax.all_to_all(summed_rows, "expert", split_axis=0, concat_axis=0, tiled=True)
    back_rows = returned.reshape(expert_count * capacity, -1).astype(jnp.float32)
    mixture = jnp.dot(blending.T, back_rows, precision=lax.Precision.HIGHEST)
    mixed_full = stream + mixture
    return lax.dynamic_slice_in_dim(mixed_full, offset, col_width, 1)


def solution(mesh):
    placed = (
        P("expert", "head", None),
        P("expert", "head", None),
        P("expert", None, None),
        P("expert", None, None),
        P("expert"),
        P("head", "expert"),
        P("expert", None),
        P(),
        P("expert", None),
        P("expert", None),
        P("expert", None, "head", None),
        P("expert", "head", None),
    )
    return jax.shard_map(
        on_device, mesh=mesh, in_specs=placed, out_specs=P("expert", "head"), check_vma=False
    )
```

```python
import functools

import jax
import jax.numpy as jnp
from jax import lax
from jax.experimental import pallas as pl
from jax.experimental.pallas import tpu as pltpu
from jax.sharding import PartitionSpec as P

MESH = pl.DeviceIdType.MESH
softmax_scale = 192.0 ** (-0.5)
norm_epsilon = 1e-06

LINE, PAIR, CORE = 4, 2, 2
CHUNKS = 8
EXTRA = 128
ROWS = 16
PARTS = 2


def rows_of(blocks):
    n, r, c = blocks.shape
    return blocks.astype(jnp.float32).reshape(n * r, c).astype(jnp.bfloat16)


def blocks_of(rows, n):
    return rows.reshape(n, rows.shape[0] // n, rows.shape[1]).astype(jnp.bfloat16)


def spread(z, y, c, far, buffers, up, down, side, sib, recv):
    def slot(zz, yy, cc):
        return (zz * PAIR + yy) * CORE + cc

    def copy(k, s, sems, index, target):
        return pltpu.make_async_remote_copy(
            src_ref=buffers.at[k, s],
            dst_ref=buffers.at[k, s],
            send_sem=sems.at[k, index],
            recv_sem=recv.at[k, s],
            device_id={"expert": target},
            device_id_type=MESH,
        )

    def each_send(k, zz, act):
        s = slot(zz, y, c)

        @pl.when(jnp.logical_and(zz <= z, z < LINE - 1))
        def _():
            act(copy(k, s, up, zz, slot(z + 1, y, c)))

        @pl.when(jnp.logical_and(zz >= z, z > 0))
        def _():
            act(copy(k, s, down, zz, slot(z - 1, y, c)))

        ends = jnp.logical_or(zz == 0, zz == LINE - 1)
        along = jnp.logical_and(jnp.logical_and(k < far, ends), zz != z)

        @pl.when(jnp.logical_not(along))
        def _():
            act(copy(k, s, side, zz, slot(z, 1 - y, c)))

        act(copy(k, s, sib, zz, slot(z, y, 1 - c)))

    def each_across(k, zz, act):
        s = slot(zz, 1 - y, c)

        @pl.when(jnp.logical_and(k < far, jnp.logical_and(zz == 0, z < LINE - 1)))
        def _():
            act(copy(k, s, up, LINE + zz, slot(z + 1, y, c)))

        @pl.when(jnp.logical_and(k < far, jnp.logical_and(zz == LINE - 1, z > 0)))
        def _():
            act(copy(k, s, down, LINE + zz, slot(z - 1, y, c)))

        act(copy(k, s, sib, LINE + zz, slot(z, y, 1 - c)))

    def arrived(k, s):
        copy(k, s, sib, 0, slot(z, y, 1 - c)).wait_recv()

    def at_distance(d, act):
        if d == 0:
            act(z)
            return

        @pl.when(z - d >= 0)
        def _():
            act(z - d)

        @pl.when(z + d < LINE)
        def _():
            act(z + d)

    def step(k, d):
        def line(zz):
            if d > 0:
                arrived(k, slot(zz, y, c))
            each_send(k, zz, lambda x: x.start())

        def across(zz):
            arrived(k, slot(zz, 1 - y, c))
            each_across(k, zz, lambda x: x.start())

        if d < LINE:
            at_distance(d, line)
        if d > 0:
            at_distance(d - 1, across)

    def finish(k):
        def body(i, carry):
            arrived(k, slot(lax.div(i, PAIR), lax.rem(i, PAIR), 1 - c))
            return carry

        lax.fori_loop(0, LINE * PAIR, body, 0)

    def drain(k):
        def body(zz, carry):
            each_send(k, zz, lambda x: x.wait_send())
            each_across(k, zz, lambda x: x.wait_send())
            return carry

        lax.fori_loop(0, LINE, body, 0)

    return step, finish, drain


def layer_kernel(
    q_ref, qr_ref, cache_ref, rot_ref, len_ref, resid_ref, gain_ref, ids_ref, weights_ref, wvo_hbm, wgu_hbm, wdn_hbm,
    out_ref,
    wvo, wgu, wdn, heads, gathered, partial, partner, last, last_partner, outgoing, incoming, stream,
    tokens, rows_send, rows_recv, back_out, back_in,
    w_sem, g_up, g_down, g_side, g_sib, g_recv, t_up, t_down, t_side, t_sib, t_recv,
    x_sem, y_send, y_recv, a_send, a_recv, b_send, b_recv,
):
    n = LINE * PAIR * CORE
    h, me = lax.axis_index("head"), lax.axis_index("expert")
    z, y, c = lax.div(me, PAIR * CORE), lax.rem(lax.div(me, CORE), PAIR), lax.rem(me, CORE)
    seqs, width = resid_ref.shape
    per_chunk, latent = gathered.shape[2], gathered.shape[4]
    cols = partial.shape[2]
    half = out_ref.shape[1]
    span = width // PARTS
    top = ids_ref.shape[1]
    capacity = rows_send.shape[1] // n
    pieces = ROWS // capacity
    piece = half // (PARTS * pieces)
    f32, bf16 = jnp.float32, jnp.bfloat16

    loads = [
        pltpu.make_async_copy(src, dst, w_sem.at[i])
        for i, (src, dst) in enumerate(((wvo_hbm, wvo), (wgu_hbm, wgu), (wdn_hbm, wdn)))
    ]
    for load in loads:
        load.start()

    barrier = pltpu.get_barrier_semaphore()

    def greet(o, carry):
        pl.semaphore_signal(
            barrier, inc=1, device_id={"expert": lax.rem(me + o, n)}, device_id_type=MESH
        )
        return carry

    lax.fori_loop(1, n, greet, 0)
    pl.semaphore_signal(barrier, inc=1, device_id={"head": 1 - h}, device_id_type=MESH)

    count = q_ref.shape[1]
    slot = lax.broadcasted_iota(jnp.int32, (count, cache_ref.shape[1]), 1)
    parts = []
    for s in range(seqs):
        scores = lax.dot_general(
            q_ref[s], cache_ref[s], (((1,), (1,)), ((), ())), preferred_element_type=f32
        )
        scores = scores + jnp.dot(qr_ref[s], rot_ref[s], preferred_element_type=f32)
        parts.append(jnp.where(slot < len_ref[s], scores * softmax_scale, -1e30))
    scores = jnp.concatenate(parts, axis=0)
    raised = jnp.exp(scores - jnp.max(scores, axis=1, keepdims=True))
    probs = (raised / jnp.sum(raised, axis=1, keepdims=True)).astype(bf16)
    for s in range(seqs):
        heads[:, s, :] = jnp.dot(
            probs[s * count : (s + 1) * count], cache_ref[s], preferred_element_type=f32
        )
    for k in range(CHUNKS):
        gathered[k, me] = heads[k * per_chunk : (k + 1) * per_chunk].astype(bf16)
    partial[...] = jnp.zeros_like(partial)
    pl.semaphore_wait(barrier, n)

    step, finish, drain = spread(z, y, c, CHUNKS // 2, gathered, g_up, g_down, g_side, g_sib, g_recv)
    swap = pltpu.make_async_remote_copy(
        src_ref=partial.at[0], dst_ref=partner, send_sem=x_sem.at[0], recv_sem=x_sem.at[1],
        device_id={"head": 1 - h}, device_id_type=MESH,
    )
    swap_last = pltpu.make_async_remote_copy(
        src_ref=last, dst_ref=last_partner, send_sem=x_sem.at[2], recv_sem=x_sem.at[3],
        device_id={"head": 1 - h}, device_id_type=MESH,
    )
    step(0, 0)
    step(1, 0)

    def turn(t, carry):
        for d in range(LINE, -1, -1):
            k = t - d if d else t + 1

            @pl.when(jnp.logical_and(k >= 0, k < CHUNKS))
            def _():
                step(k, d)

        @pl.when(t == LINE)
        def _():
            loads[0].wait()

        @pl.when(t >= LINE)
        def _():
            k = t - LINE
            finish(k)
            total = partial.at[k // (CHUNKS - 1)]
            for j in range(0, per_chunk, 2):
                x = jnp.concatenate(
                    [rows_of(gathered[k, :, j]), rows_of(gathered[k, :, j + 1])], axis=1
                )
                start = pl.multiple_of((k * per_chunk + j) * latent, 2 * latent)
                total[...] += lax.dot_general(
                    x, wvo[:, pl.ds(start, 2 * latent)], (((1,), (1,)), ((), ())),
                    preferred_element_type=f32,
                )

            @pl.when(k == CHUNKS - 2)
            def _():
                swap.start()

        return carry

    lax.fori_loop(1, CHUNKS + LINE, turn, 0)

    last[...] = partial[1].astype(bf16)
    swap_last.start()
    for k in range(CHUNKS):
        drain(k)
    swap.wait_recv()
    sums = partial[0] + partial[1] + partner[...]
    swap_last.wait_recv()
    outgoing[...] = blocks_of(sums + last_partner[...].astype(f32), n)

    def owner(o, source, target, send, recv):
        to = lax.rem(me + o, n)
        return pltpu.make_async_remote_copy(
            src_ref=source.at[to], dst_ref=target.at[me], send_sem=send.at[to],
            recv_sem=recv.at[me], device_id={"expert": to}, device_id_type=MESH,
        )

    def exchange_start(source, target, send, recv):
        def body(o, carry):
            owner(o, source, target, send, recv).start()
            return carry

        lax.fori_loop(1, n, body, 0)

    def exchange_recv(source, target, send, recv):
        def body(o, carry):
            who = lax.rem(me + o, n)
            pltpu.make_async_remote_copy(
                src_ref=source.at[who], dst_ref=target.at[who], send_sem=send.at[who],
                recv_sem=recv.at[who], device_id={"expert": who}, device_id_type=MESH,
            ).wait_recv()
            return carry

        lax.fori_loop(1, n, body, 0)

    def exchange_sent(source, target, send, recv):
        def body(o, carry):
            owner(o, source, target, send, recv).wait_send()
            return carry

        lax.fori_loop(1, n, body, 0)

    exchange_start(outgoing, incoming, a_send, a_recv)
    incoming[me] = outgoing[me]
    ids = ids_ref[...]
    lane = lax.broadcasted_iota(jnp.int32, (seqs, EXTRA), 1)
    named = jnp.zeros((seqs, EXTRA), f32)
    for k in range(top):
        named = named + jnp.where(ids[:, k : k + 1] == lane, 1.0, 0.0)
    exchange_recv(outgoing, incoming, a_send, a_recv)

    for e in range(n):
        stream[:, e * cols : (e + 1) * cols] = incoming[e].astype(f32)
    rows = stream[...] + resid_ref[...].astype(f32)
    stream[...] = rows
    mean_square = jnp.sum(rows * rows, axis=1, keepdims=True) * (1.0 / width)
    normed = rows * lax.rsqrt(mean_square + norm_epsilon) * gain_ref[...]
    for k in range(PARTS):
        tokens[k, me, :, :span] = normed[:, k * span : (k + 1) * span].astype(bf16)
        tokens[k, me, :, span:] = named.astype(bf16)

    t_step, t_finish, t_drain = spread(z, y, c, PARTS // 2, tokens, t_up, t_down, t_side, t_sib, t_recv)
    for d in range(LINE + 1):
        for k in range(PARTS):
            t_step(k, d)

    wide = n * ROWS
    place = lax.broadcasted_iota(jnp.int32, (seqs, wide), 1)
    which, at = place // ROWS, place % ROWS
    hit = jnp.zeros((seqs, wide), f32)
    share = jnp.zeros((seqs, wide), f32)
    for k in range(top):
        same = ids[:, k : k + 1] == which
        hit = hit + jnp.where(same, 1.0, 0.0)
        share = share + jnp.where(same, weights_ref[:, k : k + 1], 0.0)
    token = lax.broadcasted_iota(jnp.int32, (seqs, wide), 0)
    rank = jnp.zeros((seqs, wide), f32)
    for t in range(seqs - 1):
        rank = rank + jnp.where(token > t, hit[t : t + 1, :], 0.0)
    mixes = []
    for a in range(pieces):
        mix = jnp.where(rank == (at - a * capacity).astype(f32), share, 0.0)
        high = mix.astype(bf16)
        mixes.append((high, (mix - high.astype(f32)).astype(bf16)))
    swap.wait_send()
    swap_last.wait_send()
    exchange_sent(outgoing, incoming, a_send, a_recv)

    t_finish(0)
    loads[1].wait()

    total = n * seqs
    flags = rows_of(tokens[0, :, :, span:])
    mine = jnp.where(lax.broadcasted_iota(jnp.int32, (8, EXTRA), 1) == me, 1.0, 0.0).astype(bf16)
    chosen = lax.dot_general(mine, flags, (((1,), (1,)), ((), ())), preferred_element_type=f32)
    first = lax.broadcasted_iota(jnp.int32, (total, total), 0)
    second = lax.broadcasted_iota(jnp.int32, (total, total), 1)
    ahead = jnp.where(
        jnp.logical_and(first < second, first // seqs == second // seqs), 1.0, 0.0
    ).astype(bf16)
    order = jnp.dot(chosen.astype(bf16), ahead, preferred_element_type=f32)
    count = capacity * n
    row = lax.broadcasted_iota(jnp.int32, (count, total), 0)
    tok = lax.broadcasted_iota(jnp.int32, (count, total), 1)
    fits = jnp.logical_and(order[0:1, :] == (row // n).astype(f32), tok // seqs == row % n)
    pick = jnp.where(fits, chosen[0:1, :], 0.0).astype(bf16)

    units = wgu.shape[1]
    gate = jnp.zeros((count, units), f32)
    lift = jnp.zeros((count, units), f32)
    for k in range(PARTS):
        if k > 0:
            t_finish(k)
        for j in range(2):
            lanes = slice(j * span // 2, (j + 1) * span // 2)
            deep = slice(k * span + j * span // 2, k * span + (j + 1) * span // 2)
            x = jnp.dot(pick, rows_of(tokens[k, :, :, lanes]), preferred_element_type=f32)
            x = x.astype(bf16)
            gate += lax.dot_general(
                x, wgu[0, :, deep], (((1,), (1,)), ((), ())), preferred_element_type=f32
            )
            lift += lax.dot_general(
                x, wgu[1, :, deep], (((1,), (1,)), ((), ())), preferred_element_type=f32
            )
    hidden = (gate / (1.0 + jnp.exp(-gate)) * lift).astype(bf16)
    loads[2].wait()
    share_cols = half // PARTS

    def trade(p):
        return pltpu.make_async_remote_copy(
            src_ref=rows_send.at[p], dst_ref=rows_recv.at[p], send_sem=y_send.at[p],
            recv_sem=y_recv.at[p], device_id={"head": 1 - h}, device_id_type=MESH,
        )

    for p in range(PARTS):
        theirs = pl.ds(pl.multiple_of((1 - h) * half + p * share_cols, share_cols), share_cols)
        rows_send[p] = jnp.dot(hidden, wdn[:, theirs], preferred_element_type=f32).astype(bf16)
        trade(p).start()
    ours = pl.ds(pl.multiple_of(h * half, half), half)
    own = jnp.dot(hidden, wdn[:, ours], preferred_element_type=f32)
    dest = lax.broadcasted_iota(jnp.int32, (wide, count), 0)
    from_row = lax.broadcasted_iota(jnp.int32, (wide, count), 1)
    home = (from_row % n) * ROWS + from_row // n
    puts = [jnp.where(dest == home + a * capacity, 1.0, 0.0).astype(bf16) for a in range(pieces)]
    for p in range(PARTS):
        t_drain(p)
    for p in range(PARTS):
        trade(p).wait_recv()
        summed = own[:, p * share_cols : (p + 1) * share_cols] + rows_recv[p].astype(f32)
        summed = summed.astype(bf16)
        back = jnp.zeros((wide, piece), f32)
        for a in range(pieces):
            columns = summed[:, a * piece : (a + 1) * piece]
            back = back + jnp.dot(puts[a], columns, preferred_element_type=f32)
        back_out[p] = blocks_of(back, n)
        exchange_start(back_out.at[p], back_in.at[p], b_send.at[p], b_recv.at[p])
        back_in[p, me] = back_out[p, me]

    for p in range(PARTS):
        exchange_recv(back_out.at[p], back_in.at[p], b_send.at[p], b_recv.at[p])
        returned = rows_of(back_in[p])
        for a in range(pieces):
            added = jnp.dot(mixes[a][0], returned, preferred_element_type=f32)
            added = added + jnp.dot(mixes[a][1], returned, preferred_element_type=f32)
            here = p * share_cols + a * piece
            start = pl.multiple_of(h * half + here, piece)
            out_ref[:, here : here + piece] = stream[:, pl.ds(start, piece)] + added

    for p in range(PARTS):
        trade(p).wait_send()
        exchange_sent(back_out.at[p], back_in.at[p], b_send.at[p], b_recv.at[p])


def fused(q_latent, q_rotary, cache_latent, cache_rotary, lengths, resid, norm_gain, route_ids, route_weights, w_value_out,
          w_gate_up, w_down):
    n = LINE * PAIR * CORE
    seqs, width = resid.shape
    head_count, latent = q_latent.shape[1:]
    cols = w_value_out.shape[1]
    half = width // 2
    capacity = -(-(seqs * route_ids.shape[1]) // n)
    gate_up, down = w_gate_up[0], w_down[0]
    bf16, f32 = jnp.bfloat16, jnp.float32
    vmem, anywhere = pl.BlockSpec(memory_space=pltpu.VMEM), pl.BlockSpec(memory_space=pl.ANY)
    dma = pltpu.SemaphoreType.DMA
    return pl.pallas_call(
        layer_kernel,
        out_shape=jax.ShapeDtypeStruct((seqs, half), f32),
        in_specs=[vmem] * 4 + [pl.BlockSpec(memory_space=pltpu.SMEM)] + [vmem] * 4 + [anywhere] * 3,
        out_specs=vmem,
        scratch_shapes=[
            pltpu.VMEM(w_value_out.shape[::-1], bf16),
            pltpu.VMEM(gate_up.shape, bf16),
            pltpu.VMEM(down.shape, bf16),
            pltpu.VMEM((head_count, seqs, latent), f32),
            pltpu.VMEM((CHUNKS, n, head_count // CHUNKS, seqs, latent), bf16),
            pltpu.VMEM((2, n * seqs, cols), f32),
            pltpu.VMEM((n * seqs, cols), f32),
            pltpu.VMEM((n * seqs, cols), bf16),
            pltpu.VMEM((n * seqs, cols), bf16),
            pltpu.VMEM((n, seqs, cols), bf16),
            pltpu.VMEM((n, seqs, cols), bf16),
            pltpu.VMEM((seqs, width), f32),
            pltpu.VMEM((PARTS, n, seqs, width // PARTS + EXTRA), bf16),
            pltpu.VMEM((PARTS, capacity * n, half // PARTS), bf16),
            pltpu.VMEM((PARTS, capacity * n, half // PARTS), bf16),
            pltpu.VMEM((PARTS, n, ROWS, half // (PARTS * (ROWS // capacity))), bf16),
            pltpu.VMEM((PARTS, n, ROWS, half // (PARTS * (ROWS // capacity))), bf16),
            dma((3,)),
            dma((CHUNKS, PAIR * LINE)), dma((CHUNKS, PAIR * LINE)), dma((CHUNKS, LINE)),
            dma((CHUNKS, PAIR * LINE)), dma((CHUNKS, n)),
            dma((PARTS, PAIR * LINE)), dma((PARTS, PAIR * LINE)), dma((PARTS, LINE)),
            dma((PARTS, PAIR * LINE)), dma((PARTS, n)),
            dma((4,)), dma((PARTS,)), dma((PARTS,)), dma((n,)), dma((n,)),
            dma((PARTS, n)), dma((PARTS, n)),
        ],
        compiler_params=pltpu.CompilerParams(
            collective_id=0, has_side_effects=True, vmem_limit_bytes=56 * 1024 * 1024
        ),
    )(
        q_latent, q_rotary, cache_latent, cache_rotary, lengths, resid,
        norm_gain[None, :], route_ids, route_weights, w_value_out.T, gate_up, down,
    )


def attend(q_latent, q_rotary, cache_latent, cache_rotary, lengths):
    scores = jnp.einsum("shl,scl->shc", q_latent, cache_latent, preferred_element_type=jnp.float32)
    scores = scores + jnp.einsum(
        "shr,src->shc", q_rotary, cache_rotary, preferred_element_type=jnp.float32
    )
    scores = scores * softmax_scale
    position = lax.broadcasted_iota(jnp.int32, scores.shape, 2)
    scores = jnp.where(position < lengths[:, None, None], scores, -1e30)
    highest = jnp.max(scores, axis=2, keepdims=True)
    weights = jnp.exp(scores - highest)
    probs = (weights / jnp.sum(weights, axis=2, keepdims=True)).astype(jnp.bfloat16)
    return jnp.einsum(
        "shc,scl->shl", probs, cache_latent, preferred_element_type=jnp.float32
    ).astype(jnp.bfloat16)


def on_device(
    q_latent,
    q_rotary,
    cache_latent,
    cache_rotary,
    lengths,
    w_value_out,
    resid,
    norm_gain,
    route_ids,
    route_weights,
    w_gate_up,
    w_down,
):
    seq_local = q_latent.shape[0]
    if (
        lax.axis_size("head") == 2
        and lax.axis_size("expert") == LINE * PAIR * CORE
        and seq_local == 8
    ):
        return fused(
            q_latent, q_rotary, cache_latent, cache_rotary, lengths, resid, norm_gain,
            route_ids, route_weights, w_value_out, w_gate_up, w_down,
        )
    latent_out = attend(q_latent, q_rotary, cache_latent, cache_rotary, lengths)
    flattened = latent_out.reshape(seq_local, -1)
    column_terms = jnp.dot(
        lax.all_gather(flattened, "expert", axis=0, tiled=True),
        w_value_out,
        preferred_element_type=jnp.float32,
    )
    column_sums = lax.psum(column_terms, "head")
    attention = lax.all_to_all(
        column_sums.astype(jnp.bfloat16), "expert", split_axis=0, concat_axis=1, tiled=True
    )
    stream = resid.astype(jnp.float32) + attention.astype(jnp.float32)
    mean_square = jnp.mean(stream * stream, axis=1, keepdims=True)
    normed = (stream * lax.rsqrt(mean_square + norm_epsilon) * norm_gain).astype(jnp.bfloat16)
    expert_count = lax.axis_size("expert")
    top_count = route_ids.shape[1]
    capacity = max(2, -(-(seq_local * top_count) // expert_count))
    flat_ids = route_ids.reshape(-1)
    one_hot = (flat_ids[:, None] == jnp.arange(expert_count, dtype=jnp.int32)[None, :]).astype(
        jnp.int32
    )
    earlier = jnp.cumsum(one_hot, axis=0) - one_hot
    slot_index = jnp.sum(earlier * one_hot, axis=1)
    target = (flat_ids * capacity + slot_index).reshape(seq_local, top_count)
    places = jnp.arange(expert_count * capacity, dtype=jnp.int32)
    matches = target[None, :, :] == places[:, None, None]
    selector = jnp.sum(matches.astype(jnp.int32), axis=2).astype(jnp.bfloat16)
    blending = jnp.sum(jnp.where(matches, route_weights[None, :, :], 0.0), axis=2)
    outgoing = jnp.dot(selector, normed, preferred_element_type=jnp.float32).astype(jnp.bfloat16)
    outgoing = outgoing.reshape(expert_count, capacity, -1)
    gate_up = w_gate_up[0]
    down_local = w_down[0]
    col_width = stream.shape[1] // lax.axis_size("head")
    offset = lax.axis_index("head") * col_width
    arrived = lax.all_to_all(outgoing, "expert", split_axis=0, concat_axis=0, tiled=True)
    flat_rows = arrived.reshape(-1, arrived.shape[2])
    projected = jnp.einsum("rd,gfd->rgf", flat_rows, gate_up, preferred_element_type=jnp.float32)
    hidden = (jax.nn.silu(projected[:, 0]) * projected[:, 1]).astype(jnp.bfloat16)
    partial_rows = jnp.dot(hidden, down_local, preferred_element_type=jnp.float32)
    expert_terms = partial_rows.reshape(arrived.shape[0], arrived.shape[1], -1)
    summed_rows = lax.psum(expert_terms.astype(jnp.bfloat16), "head")
    returned = lax.all_to_all(summed_rows, "expert", split_axis=0, concat_axis=0, tiled=True)
    back_rows = returned.reshape(expert_count * capacity, -1).astype(jnp.float32)
    mixture = jnp.dot(blending.T, back_rows, precision=lax.Precision.HIGHEST)
    mixed_full = stream + mixture
    return lax.dynamic_slice_in_dim(mixed_full, offset, col_width, 1)


def solution(mesh):
    placed = (
        P("expert", "head", None),
        P("expert", "head", None),
        P("expert", None, None),
        P("expert", None, None),
        P("expert"),
        P("head", "expert"),
        P("expert", None),
        P(),
        P("expert", None),
        P("expert", None),
        P("expert", None, "head", None),
        P("expert", "head", None),
    )
    return jax.shard_map(
        on_device, mesh=mesh, in_specs=placed, out_specs=P("expert", "head"), check_vma=False
    )
```

```python
import functools

import jax
import jax.numpy as jnp
from jax import lax
from jax.experimental import pallas as pl
from jax.experimental.pallas import tpu as pltpu
from jax.sharding import PartitionSpec as P

MESH = pl.DeviceIdType.MESH
softmax_scale = 192.0 ** (-0.5)
norm_epsilon = 1e-06

LINE, PAIR, CORE = 4, 2, 2
CHUNKS = 4
EXTRA = 128
ROWS = 16
PARTS = 2


def rows_of(blocks):
    n, r, c = blocks.shape
    return blocks.astype(jnp.float32).reshape(n * r, c).astype(jnp.bfloat16)


def blocks_of(rows, n):
    return rows.reshape(n, rows.shape[0] // n, rows.shape[1]).astype(jnp.bfloat16)


def device(zz, yy, cc):
    return (zz * PAIR + yy) * CORE + cc


def block_of(e):
    cc, yy, zz = lax.rem(e, CORE), lax.rem(lax.div(e, CORE), PAIR), lax.div(e, PAIR * CORE)
    return (cc * PAIR + yy) * LINE + zz


def spread(z, y, c, far, buffers, up, down, side, sib, recv):
    def slot(zz, yy):
        return (c * PAIR + yy) * LINE + zz

    def copy(k, s, sems, index, target):
        return pltpu.make_async_remote_copy(
            src_ref=buffers.at[k, s],
            dst_ref=buffers.at[k, s],
            send_sem=sems.at[k, index],
            recv_sem=recv.at[k, lax.rem(s, PAIR * LINE)],
            device_id={"expert": target},
            device_id_type=MESH,
        )

    def group(k, yy, core):
        blocks = buffers.at[k, pl.ds((core * PAIR + yy) * LINE, LINE)]
        return pltpu.make_async_remote_copy(
            src_ref=blocks, dst_ref=blocks, send_sem=sib.at[k, yy],
            recv_sem=recv.at[k, PAIR * LINE + yy],
            device_id={"expert": device(z, y, 1 - c)}, device_id_type=MESH,
        )

    def each_send(k, zz, act):
        s = slot(zz, y)

        @pl.when(jnp.logical_and(zz <= z, z < LINE - 1))
        def _():
            act(copy(k, s, up, zz, device(z + 1, y, c)))

        @pl.when(jnp.logical_and(zz >= z, z > 0))
        def _():
            act(copy(k, s, down, zz, device(z - 1, y, c)))

        ends = jnp.logical_or(zz == 0, zz == LINE - 1)
        along = jnp.logical_and(jnp.logical_and(k < far, ends), zz != z)

        @pl.when(jnp.logical_not(along))
        def _():
            act(copy(k, s, side, zz, device(z, 1 - y, c)))

    def each_across(k, zz, act):
        s = slot(zz, 1 - y)

        @pl.when(jnp.logical_and(k < far, jnp.logical_and(zz == 0, z < LINE - 1)))
        def _():
            act(copy(k, s, up, LINE + zz, device(z + 1, y, c)))

        @pl.when(jnp.logical_and(k < far, jnp.logical_and(zz == LINE - 1, z > 0)))
        def _():
            act(copy(k, s, down, LINE + zz, device(z - 1, y, c)))

    def arrived(k, s):
        copy(k, s, side, 0, device(z, 1 - y, c)).wait_recv()

    def at_distance(d, act):
        if d == 0:
            act(z)
            return

        @pl.when(z - d >= 0)
        def _():
            act(z - d)

        @pl.when(z + d < LINE)
        def _():
            act(z + d)

    def step(k, d):
        def line(zz):
            if d > 0:
                arrived(k, slot(zz, y))
            each_send(k, zz, lambda x: x.start())

        def across(zz):
            arrived(k, slot(zz, 1 - y))
            each_across(k, zz, lambda x: x.start())

        if d < LINE:
            at_distance(d, line)
        if d == LINE - 1:
            group(k, y, c).start()
        if d > 0:
            at_distance(d - 1, across)
        if d == LINE:
            group(k, 1 - y, c).start()

    def finish(k):
        group(k, y, 1 - c).wait_recv()
        group(k, 1 - y, 1 - c).wait_recv()

    def drain(k):
        def body(zz, carry):
            each_send(k, zz, lambda x: x.wait_send())
            each_across(k, zz, lambda x: x.wait_send())
            return carry

        lax.fori_loop(0, LINE, body, 0)
        group(k, y, c).wait_send()
        group(k, 1 - y, c).wait_send()

    return step, finish, drain


def layer_kernel(
    q_ref, qr_ref, cache_ref, rot_ref, len_ref, resid_ref, gain_ref, ids_ref, weights_ref, wvo_hbm, wgu_hbm, wdn_hbm,
    out_ref,
    wvo, wgu, wdn, heads, gathered, partial, partner, last, last_partner, outgoing, incoming, stream,
    tokens, rows_send, rows_recv, back_out, back_in,
    w_sem, g_up, g_down, g_side, g_sib, g_recv, t_up, t_down, t_side, t_sib, t_recv,
    x_sem, y_send, y_recv, a_send, a_recv, b_send, b_recv,
):
    n = LINE * PAIR * CORE
    h, me = lax.axis_index("head"), lax.axis_index("expert")
    z, y, c = lax.div(me, PAIR * CORE), lax.rem(lax.div(me, CORE), PAIR), lax.rem(me, CORE)
    here = block_of(me)
    seqs, width = resid_ref.shape
    per_chunk, latent = gathered.shape[2], gathered.shape[4]
    cols = partial.shape[2]
    half = out_ref.shape[1]
    span = width // PARTS
    top = ids_ref.shape[1]
    capacity = rows_send.shape[1] // n
    pieces = ROWS // capacity
    piece = half // (PARTS * pieces)
    f32, bf16 = jnp.float32, jnp.bfloat16

    loads = [
        pltpu.make_async_copy(src, dst, w_sem.at[i])
        for i, (src, dst) in enumerate(((wvo_hbm, wvo), (wgu_hbm, wgu), (wdn_hbm, wdn)))
    ]
    for load in loads:
        load.start()

    barrier = pltpu.get_barrier_semaphore()

    def greet(o, carry):
        pl.semaphore_signal(
            barrier, inc=1, device_id={"expert": lax.rem(me + o, n)}, device_id_type=MESH
        )
        return carry

    lax.fori_loop(1, n, greet, 0)
    pl.semaphore_signal(barrier, inc=1, device_id={"head": 1 - h}, device_id_type=MESH)

    count = q_ref.shape[1]
    slot = lax.broadcasted_iota(jnp.int32, (count, cache_ref.shape[1]), 1)
    parts = []
    for s in range(seqs):
        scores = lax.dot_general(
            q_ref[s], cache_ref[s], (((1,), (1,)), ((), ())), preferred_element_type=f32
        )
        scores = scores + jnp.dot(qr_ref[s], rot_ref[s], preferred_element_type=f32)
        parts.append(jnp.where(slot < len_ref[s], scores * softmax_scale, -1e30))
    scores = jnp.concatenate(parts, axis=0)
    raised = jnp.exp(scores - jnp.max(scores, axis=1, keepdims=True))
    probs = (raised / jnp.sum(raised, axis=1, keepdims=True)).astype(bf16)
    for s in range(seqs):
        heads[:, s, :] = jnp.dot(
            probs[s * count : (s + 1) * count], cache_ref[s], preferred_element_type=f32
        )
    for k in range(CHUNKS):
        gathered[k, here] = heads[k * per_chunk : (k + 1) * per_chunk].astype(bf16)
    partial[...] = jnp.zeros_like(partial)
    pl.semaphore_wait(barrier, n)

    step, finish, drain = spread(z, y, c, CHUNKS // 2, gathered, g_up, g_down, g_side, g_sib, g_recv)
    swap = pltpu.make_async_remote_copy(
        src_ref=partial.at[0], dst_ref=partner, send_sem=x_sem.at[0], recv_sem=x_sem.at[1],
        device_id={"head": 1 - h}, device_id_type=MESH,
    )
    swap_last = pltpu.make_async_remote_copy(
        src_ref=last, dst_ref=last_partner, send_sem=x_sem.at[2], recv_sem=x_sem.at[3],
        device_id={"head": 1 - h}, device_id_type=MESH,
    )
    step(0, 0)
    step(1, 0)

    def turn(t, carry):
        for d in range(LINE, -1, -1):
            k = t - d if d else t + 1

            @pl.when(jnp.logical_and(k >= 0, k < CHUNKS))
            def _():
                step(k, d)

        @pl.when(t == LINE)
        def _():
            loads[0].wait()

        @pl.when(t >= LINE)
        def _():
            k = t - LINE
            finish(k)
            total = partial.at[k // (CHUNKS - 1)]
            for j in range(0, per_chunk, 2):
                x = jnp.concatenate(
                    [rows_of(gathered[k, :, j]), rows_of(gathered[k, :, j + 1])], axis=1
                )
                start = pl.multiple_of((k * per_chunk + j) * latent, 2 * latent)
                total[...] += lax.dot_general(
                    x, wvo[:, pl.ds(start, 2 * latent)], (((1,), (1,)), ((), ())),
                    preferred_element_type=f32,
                )

            @pl.when(k == CHUNKS - 2)
            def _():
                swap.start()

        return carry

    lax.fori_loop(1, CHUNKS + LINE, turn, 0)

    last[...] = partial[1].astype(bf16)
    swap_last.start()
    for k in range(CHUNKS):
        drain(k)
    swap.wait_recv()
    sums = partial[0] + partial[1] + partner[...]
    swap_last.wait_recv()
    outgoing[...] = blocks_of(sums + last_partner[...].astype(f32), n)

    def owner(o, source, target, send, recv):
        to = lax.rem(me + o, n)
        return pltpu.make_async_remote_copy(
            src_ref=source.at[block_of(to)], dst_ref=target.at[me], send_sem=send.at[to],
            recv_sem=recv.at[me], device_id={"expert": to}, device_id_type=MESH,
        )

    def exchange_start(source, target, send, recv):
        def body(o, carry):
            owner(o, source, target, send, recv).start()
            return carry

        lax.fori_loop(1, n, body, 0)

    def exchange_recv(source, target, send, recv):
        def body(o, carry):
            who = lax.rem(me + o, n)
            pltpu.make_async_remote_copy(
                src_ref=source.at[block_of(who)], dst_ref=target.at[who], send_sem=send.at[who],
                recv_sem=recv.at[who], device_id={"expert": who}, device_id_type=MESH,
            ).wait_recv()
            return carry

        lax.fori_loop(1, n, body, 0)

    def exchange_sent(source, target, send, recv):
        def body(o, carry):
            owner(o, source, target, send, recv).wait_send()
            return carry

        lax.fori_loop(1, n, body, 0)

    exchange_start(outgoing, incoming, a_send, a_recv)
    incoming[me] = outgoing[here]
    ids = ids_ref[...]
    lane = lax.broadcasted_iota(jnp.int32, (seqs, EXTRA), 1)
    named = jnp.zeros((seqs, EXTRA), f32)
    for k in range(top):
        named = named + jnp.where(ids[:, k : k + 1] == lane, 1.0, 0.0)
    exchange_recv(outgoing, incoming, a_send, a_recv)

    for e in range(n):
        stream[:, e * cols : (e + 1) * cols] = incoming[e].astype(f32)
    rows = stream[...] + resid_ref[...].astype(f32)
    stream[...] = rows
    mean_square = jnp.sum(rows * rows, axis=1, keepdims=True) * (1.0 / width)
    normed = rows * lax.rsqrt(mean_square + norm_epsilon) * gain_ref[...]
    for k in range(PARTS):
        tokens[k, here, :, :span] = normed[:, k * span : (k + 1) * span].astype(bf16)
        tokens[k, here, :, span:] = named.astype(bf16)

    t_step, t_finish, t_drain = spread(z, y, c, PARTS // 2, tokens, t_up, t_down, t_side, t_sib, t_recv)
    for d in range(LINE + 1):
        for k in range(PARTS):
            t_step(k, d)

    wide = n * ROWS
    place = lax.broadcasted_iota(jnp.int32, (seqs, wide), 1)
    which, at = place // ROWS, place % ROWS
    hit = jnp.zeros((seqs, wide), f32)
    share = jnp.zeros((seqs, wide), f32)
    for k in range(top):
        same = ids[:, k : k + 1] == which
        hit = hit + jnp.where(same, 1.0, 0.0)
        share = share + jnp.where(same, weights_ref[:, k : k + 1], 0.0)
    token = lax.broadcasted_iota(jnp.int32, (seqs, wide), 0)
    rank = jnp.zeros((seqs, wide), f32)
    for t in range(seqs - 1):
        rank = rank + jnp.where(token > t, hit[t : t + 1, :], 0.0)
    mixes = []
    for a in range(pieces):
        mix = jnp.where(rank == (at - a * capacity).astype(f32), share, 0.0)
        high = mix.astype(bf16)
        mixes.append((high, (mix - high.astype(f32)).astype(bf16)))
    swap.wait_send()
    swap_last.wait_send()
    exchange_sent(outgoing, incoming, a_send, a_recv)

    t_finish(0)
    loads[1].wait()

    total = n * seqs
    flags = rows_of(tokens[0, :, :, span:])
    mine = jnp.where(lax.broadcasted_iota(jnp.int32, (8, EXTRA), 1) == me, 1.0, 0.0).astype(bf16)
    chosen = lax.dot_general(mine, flags, (((1,), (1,)), ((), ())), preferred_element_type=f32)
    first = lax.broadcasted_iota(jnp.int32, (total, total), 0)
    second = lax.broadcasted_iota(jnp.int32, (total, total), 1)
    ahead = jnp.where(
        jnp.logical_and(first < second, first // seqs == second // seqs), 1.0, 0.0
    ).astype(bf16)
    order = jnp.dot(chosen.astype(bf16), ahead, preferred_element_type=f32)
    count = capacity * n
    row = lax.broadcasted_iota(jnp.int32, (count, total), 0)
    tok = lax.broadcasted_iota(jnp.int32, (count, total), 1)
    fits = jnp.logical_and(order[0:1, :] == (row // n).astype(f32), tok // seqs == row % n)
    pick = jnp.where(fits, chosen[0:1, :], 0.0).astype(bf16)

    units = wgu.shape[1]
    gate = jnp.zeros((count, units), f32)
    lift = jnp.zeros((count, units), f32)
    for k in range(PARTS):
        if k > 0:
            t_finish(k)
        for j in range(2):
            lanes = slice(j * span // 2, (j + 1) * span // 2)
            deep = slice(k * span + j * span // 2, k * span + (j + 1) * span // 2)
            x = jnp.dot(pick, rows_of(tokens[k, :, :, lanes]), preferred_element_type=f32)
            x = x.astype(bf16)
            gate += lax.dot_general(
                x, wgu[0, :, deep], (((1,), (1,)), ((), ())), preferred_element_type=f32
            )
            lift += lax.dot_general(
                x, wgu[1, :, deep], (((1,), (1,)), ((), ())), preferred_element_type=f32
            )
    hidden = (gate / (1.0 + jnp.exp(-gate)) * lift).astype(bf16)
    loads[2].wait()
    share_cols = half // PARTS

    def trade(p):
        return pltpu.make_async_remote_copy(
            src_ref=rows_send.at[p], dst_ref=rows_recv.at[p], send_sem=y_send.at[p],
            recv_sem=y_recv.at[p], device_id={"head": 1 - h}, device_id_type=MESH,
        )

    for p in range(PARTS):
        theirs = pl.ds(pl.multiple_of((1 - h) * half + p * share_cols, share_cols), share_cols)
        rows_send[p] = jnp.dot(hidden, wdn[:, theirs], preferred_element_type=f32).astype(bf16)
        trade(p).start()
    ours = pl.ds(pl.multiple_of(h * half, half), half)
    own = jnp.dot(hidden, wdn[:, ours], preferred_element_type=f32)
    dest = lax.broadcasted_iota(jnp.int32, (wide, count), 0)
    from_row = lax.broadcasted_iota(jnp.int32, (wide, count), 1)
    home = (from_row % n) * ROWS + from_row // n
    puts = [jnp.where(dest == home + a * capacity, 1.0, 0.0).astype(bf16) for a in range(pieces)]
    for p in range(PARTS):
        t_drain(p)
    for p in range(PARTS):
        trade(p).wait_recv()
        summed = own[:, p * share_cols : (p + 1) * share_cols] + rows_recv[p].astype(f32)
        summed = summed.astype(bf16)
        back = jnp.zeros((wide, piece), f32)
        for a in range(pieces):
            columns = summed[:, a * piece : (a + 1) * piece]
            back = back + jnp.dot(puts[a], columns, preferred_element_type=f32)
        back_out[p] = blocks_of(back, n)
        exchange_start(back_out.at[p], back_in.at[p], b_send.at[p], b_recv.at[p])
        back_in[p, me] = back_out[p, here]

    for p in range(PARTS):
        exchange_recv(back_out.at[p], back_in.at[p], b_send.at[p], b_recv.at[p])
        returned = rows_of(back_in[p])
        for a in range(pieces):
            added = jnp.dot(mixes[a][0], returned, preferred_element_type=f32)
            added = added + jnp.dot(mixes[a][1], returned, preferred_element_type=f32)
            at = p * share_cols + a * piece
            start = pl.multiple_of(h * half + at, piece)
            out_ref[:, at : at + piece] = stream[:, pl.ds(start, piece)] + added

    for p in range(PARTS):
        trade(p).wait_send()
        exchange_sent(back_out.at[p], back_in.at[p], b_send.at[p], b_recv.at[p])


def fused(q_latent, q_rotary, cache_latent, cache_rotary, lengths, resid, norm_gain, route_ids, route_weights, w_value_out,
          w_gate_up, w_down):
    n = LINE * PAIR * CORE
    seqs, width = resid.shape
    head_count, latent = q_latent.shape[1:]
    cols = w_value_out.shape[1]
    half = width // 2
    capacity = -(-(seqs * route_ids.shape[1]) // n)
    gate_up, down = w_gate_up[0], w_down[0]
    bf16, f32 = jnp.bfloat16, jnp.float32
    vmem, anywhere = pl.BlockSpec(memory_space=pltpu.VMEM), pl.BlockSpec(memory_space=pl.ANY)
    dma = pltpu.SemaphoreType.DMA
    return pl.pallas_call(
        layer_kernel,
        out_shape=jax.ShapeDtypeStruct((seqs, half), f32),
        in_specs=[vmem] * 4 + [pl.BlockSpec(memory_space=pltpu.SMEM)] + [vmem] * 4 + [anywhere] * 3,
        out_specs=vmem,
        scratch_shapes=[
            pltpu.VMEM(w_value_out.shape[::-1], bf16),
            pltpu.VMEM(gate_up.shape, bf16),
            pltpu.VMEM(down.shape, bf16),
            pltpu.VMEM((head_count, seqs, latent), f32),
            pltpu.VMEM((CHUNKS, n, head_count // CHUNKS, seqs, latent), bf16),
            pltpu.VMEM((2, n * seqs, cols), f32),
            pltpu.VMEM((n * seqs, cols), f32),
            pltpu.VMEM((n * seqs, cols), bf16),
            pltpu.VMEM((n * seqs, cols), bf16),
            pltpu.VMEM((n, seqs, cols), bf16),
            pltpu.VMEM((n, seqs, cols), bf16),
            pltpu.VMEM((seqs, width), f32),
            pltpu.VMEM((PARTS, n, seqs, width // PARTS + EXTRA), bf16),
            pltpu.VMEM((PARTS, capacity * n, half // PARTS), bf16),
            pltpu.VMEM((PARTS, capacity * n, half // PARTS), bf16),
            pltpu.VMEM((PARTS, n, ROWS, half // (PARTS * (ROWS // capacity))), bf16),
            pltpu.VMEM((PARTS, n, ROWS, half // (PARTS * (ROWS // capacity))), bf16),
            dma((3,)),
            dma((CHUNKS, PAIR * LINE)), dma((CHUNKS, PAIR * LINE)), dma((CHUNKS, LINE)),
            dma((CHUNKS, PAIR)), dma((CHUNKS, PAIR * LINE + PAIR)),
            dma((PARTS, PAIR * LINE)), dma((PARTS, PAIR * LINE)), dma((PARTS, LINE)),
            dma((PARTS, PAIR)), dma((PARTS, PAIR * LINE + PAIR)),
            dma((4,)), dma((PARTS,)), dma((PARTS,)), dma((n,)), dma((n,)),
            dma((PARTS, n)), dma((PARTS, n)),
        ],
        compiler_params=pltpu.CompilerParams(
            collective_id=0, has_side_effects=True, vmem_limit_bytes=56 * 1024 * 1024
        ),
    )(
        q_latent, q_rotary, cache_latent, cache_rotary, lengths, resid,
        norm_gain[None, :], route_ids, route_weights, w_value_out.T, gate_up, down,
    )


def attend(q_latent, q_rotary, cache_latent, cache_rotary, lengths):
    scores = jnp.einsum("shl,scl->shc", q_latent, cache_latent, preferred_element_type=jnp.float32)
    scores = scores + jnp.einsum(
        "shr,src->shc", q_rotary, cache_rotary, preferred_element_type=jnp.float32
    )
    scores = scores * softmax_scale
    position = lax.broadcasted_iota(jnp.int32, scores.shape, 2)
    scores = jnp.where(position < lengths[:, None, None], scores, -1e30)
    highest = jnp.max(scores, axis=2, keepdims=True)
    weights = jnp.exp(scores - highest)
    probs = (weights / jnp.sum(weights, axis=2, keepdims=True)).astype(jnp.bfloat16)
    return jnp.einsum(
        "shc,scl->shl", probs, cache_latent, preferred_element_type=jnp.float32
    ).astype(jnp.bfloat16)


def on_device(
    q_latent,
    q_rotary,
    cache_latent,
    cache_rotary,
    lengths,
    w_value_out,
    resid,
    norm_gain,
    route_ids,
    route_weights,
    w_gate_up,
    w_down,
):
    seq_local = q_latent.shape[0]
    if (
        lax.axis_size("head") == 2
        and lax.axis_size("expert") == LINE * PAIR * CORE
        and seq_local == 8
    ):
        return fused(
            q_latent, q_rotary, cache_latent, cache_rotary, lengths, resid, norm_gain,
            route_ids, route_weights, w_value_out, w_gate_up, w_down,
        )
    latent_out = attend(q_latent, q_rotary, cache_latent, cache_rotary, lengths)
    flattened = latent_out.reshape(seq_local, -1)
    column_terms = jnp.dot(
        lax.all_gather(flattened, "expert", axis=0, tiled=True),
        w_value_out,
        preferred_element_type=jnp.float32,
    )
    column_sums = lax.psum(column_terms, "head")
    attention = lax.all_to_all(
        column_sums.astype(jnp.bfloat16), "expert", split_axis=0, concat_axis=1, tiled=True
    )
    stream = resid.astype(jnp.float32) + attention.astype(jnp.float32)
    mean_square = jnp.mean(stream * stream, axis=1, keepdims=True)
    normed = (stream * lax.rsqrt(mean_square + norm_epsilon) * norm_gain).astype(jnp.bfloat16)
    expert_count = lax.axis_size("expert")
    top_count = route_ids.shape[1]
    capacity = max(2, -(-(seq_local * top_count) // expert_count))
    flat_ids = route_ids.reshape(-1)
    one_hot = (flat_ids[:, None] == jnp.arange(expert_count, dtype=jnp.int32)[None, :]).astype(
        jnp.int32
    )
    earlier = jnp.cumsum(one_hot, axis=0) - one_hot
    slot_index = jnp.sum(earlier * one_hot, axis=1)
    target = (flat_ids * capacity + slot_index).reshape(seq_local, top_count)
    places = jnp.arange(expert_count * capacity, dtype=jnp.int32)
    matches = target[None, :, :] == places[:, None, None]
    selector = jnp.sum(matches.astype(jnp.int32), axis=2).astype(jnp.bfloat16)
    blending = jnp.sum(jnp.where(matches, route_weights[None, :, :], 0.0), axis=2)
    outgoing = jnp.dot(selector, normed, preferred_element_type=jnp.float32).astype(jnp.bfloat16)
    outgoing = outgoing.reshape(expert_count, capacity, -1)
    gate_up = w_gate_up[0]
    down_local = w_down[0]
    col_width = stream.shape[1] // lax.axis_size("head")
    offset = lax.axis_index("head") * col_width
    arrived = lax.all_to_all(outgoing, "expert", split_axis=0, concat_axis=0, tiled=True)
    flat_rows = arrived.reshape(-1, arrived.shape[2])
    projected = jnp.einsum("rd,gfd->rgf", flat_rows, gate_up, preferred_element_type=jnp.float32)
    hidden = (jax.nn.silu(projected[:, 0]) * projected[:, 1]).astype(jnp.bfloat16)
    partial_rows = jnp.dot(hidden, down_local, preferred_element_type=jnp.float32)
    expert_terms = partial_rows.reshape(arrived.shape[0], arrived.shape[1], -1)
    summed_rows = lax.psum(expert_terms.astype(jnp.bfloat16), "head")
    returned = lax.all_to_all(summed_rows, "expert", split_axis=0, concat_axis=0, tiled=True)
    back_rows = returned.reshape(expert_count * capacity, -1).astype(jnp.float32)
    mixture = jnp.dot(blending.T, back_rows, precision=lax.Precision.HIGHEST)
    mixed_full = stream + mixture
    return lax.dynamic_slice_in_dim(mixed_full, offset, col_width, 1)


def solution(mesh):
    placed = (
        P("expert", "head", None),
        P("expert", "head", None),
        P("expert", None, None),
        P("expert", None, None),
        P("expert"),
        P("head", "expert"),
        P("expert", None),
        P(),
        P("expert", None),
        P("expert", None),
        P("expert", None, "head", None),
        P("expert", "head", None),
    )
    return jax.shard_map(
        on_device, mesh=mesh, in_specs=placed, out_specs=P("expert", "head"), check_vma=False
    )
```

```python
import functools

import jax
import jax.numpy as jnp
from jax import lax
from jax.experimental import pallas as pl
from jax.experimental.pallas import tpu as pltpu
from jax.sharding import PartitionSpec as P

MESH = pl.DeviceIdType.MESH
softmax_scale = 192.0 ** (-0.5)
norm_epsilon = 1e-06

LINE, PAIR, CORE = 4, 2, 2
CHUNKS = 2
EXTRA = 128
ROWS = 16
PARTS = 2


def rows_of(blocks):
    n, r, c = blocks.shape
    return blocks.astype(jnp.float32).reshape(n * r, c).astype(jnp.bfloat16)


def blocks_of(rows, n):
    return rows.reshape(n, rows.shape[0] // n, rows.shape[1]).astype(jnp.bfloat16)


def device(zz, yy, cc):
    return (zz * PAIR + yy) * CORE + cc


def block_of(e):
    cc, yy, zz = lax.rem(e, CORE), lax.rem(lax.div(e, CORE), PAIR), lax.div(e, PAIR * CORE)
    return (cc * PAIR + yy) * LINE + zz


def spread(z, y, c, far, buffers, up, down, side, sib, recv):
    def slot(zz, yy):
        return (c * PAIR + yy) * LINE + zz

    def copy(k, s, sems, index, target):
        return pltpu.make_async_remote_copy(
            src_ref=buffers.at[k, s],
            dst_ref=buffers.at[k, s],
            send_sem=sems.at[k, index],
            recv_sem=recv.at[k, lax.rem(s, PAIR * LINE)],
            device_id={"expert": target},
            device_id_type=MESH,
        )

    def group(k, yy, core):
        blocks = buffers.at[k, pl.ds((core * PAIR + yy) * LINE, LINE)]
        return pltpu.make_async_remote_copy(
            src_ref=blocks, dst_ref=blocks, send_sem=sib.at[k, yy],
            recv_sem=recv.at[k, PAIR * LINE + yy],
            device_id={"expert": device(z, y, 1 - c)}, device_id_type=MESH,
        )

    def each_send(k, zz, act):
        s = slot(zz, y)

        @pl.when(jnp.logical_and(zz <= z, z < LINE - 1))
        def _():
            act(copy(k, s, up, zz, device(z + 1, y, c)))

        @pl.when(jnp.logical_and(zz >= z, z > 0))
        def _():
            act(copy(k, s, down, zz, device(z - 1, y, c)))

        ends = jnp.logical_or(zz == 0, zz == LINE - 1)
        along = jnp.logical_and(jnp.logical_and(k < far, ends), zz != z)

        @pl.when(jnp.logical_not(along))
        def _():
            act(copy(k, s, side, zz, device(z, 1 - y, c)))

    def each_across(k, zz, act):
        s = slot(zz, 1 - y)

        @pl.when(jnp.logical_and(k < far, jnp.logical_and(zz == 0, z < LINE - 1)))
        def _():
            act(copy(k, s, up, LINE + zz, device(z + 1, y, c)))

        @pl.when(jnp.logical_and(k < far, jnp.logical_and(zz == LINE - 1, z > 0)))
        def _():
            act(copy(k, s, down, LINE + zz, device(z - 1, y, c)))

    def arrived(k, s):
        copy(k, s, side, 0, device(z, 1 - y, c)).wait_recv()

    def at_distance(d, act):
        if d == 0:
            act(z)
            return

        @pl.when(z - d >= 0)
        def _():
            act(z - d)

        @pl.when(z + d < LINE)
        def _():
            act(z + d)

    def step(k, d):
        def line(zz):
            if d > 0:
                arrived(k, slot(zz, y))
            each_send(k, zz, lambda x: x.start())

        def across(zz):
            arrived(k, slot(zz, 1 - y))
            each_across(k, zz, lambda x: x.start())

        if d < LINE:
            at_distance(d, line)
        if d == LINE - 1:
            group(k, y, c).start()
        if d > 0:
            at_distance(d - 1, across)
        if d == LINE:
            group(k, 1 - y, c).start()

    def finish(k):
        group(k, y, 1 - c).wait_recv()
        group(k, 1 - y, 1 - c).wait_recv()

    def drain(k):
        def body(zz, carry):
            each_send(k, zz, lambda x: x.wait_send())
            each_across(k, zz, lambda x: x.wait_send())
            return carry

        lax.fori_loop(0, LINE, body, 0)
        group(k, y, c).wait_send()
        group(k, 1 - y, c).wait_send()

    return step, finish, drain


def layer_kernel(
    q_ref, qr_ref, cache_ref, rot_ref, len_ref, resid_ref, gain_ref, ids_ref, weights_ref, wvo_hbm, wgu_hbm, wdn_hbm,
    out_ref,
    wvo, wgu, wdn, heads, gathered, partial, partner, last, last_partner, outgoing, incoming, stream,
    tokens, rows_send, rows_recv, back_out, back_in,
    w_sem, g_up, g_down, g_side, g_sib, g_recv, t_up, t_down, t_side, t_sib, t_recv,
    x_sem, y_send, y_recv, a_send, a_recv, b_send, b_recv,
):
    n = LINE * PAIR * CORE
    h, me = lax.axis_index("head"), lax.axis_index("expert")
    z, y, c = lax.div(me, PAIR * CORE), lax.rem(lax.div(me, CORE), PAIR), lax.rem(me, CORE)
    here = block_of(me)
    seqs, width = resid_ref.shape
    per_chunk, latent = gathered.shape[2], gathered.shape[4]
    cols = partial.shape[2]
    half = out_ref.shape[1]
    span = width // PARTS
    top = ids_ref.shape[1]
    capacity = rows_send.shape[1] // n
    pieces = ROWS // capacity
    piece = half // (PARTS * pieces)
    f32, bf16 = jnp.float32, jnp.bfloat16

    loads = [
        pltpu.make_async_copy(src, dst, w_sem.at[i])
        for i, (src, dst) in enumerate(((wvo_hbm, wvo), (wgu_hbm, wgu), (wdn_hbm, wdn)))
    ]
    for load in loads:
        load.start()

    barrier = pltpu.get_barrier_semaphore()

    def greet(o, carry):
        pl.semaphore_signal(
            barrier, inc=1, device_id={"expert": lax.rem(me + o, n)}, device_id_type=MESH
        )
        return carry

    lax.fori_loop(1, n, greet, 0)
    pl.semaphore_signal(barrier, inc=1, device_id={"head": 1 - h}, device_id_type=MESH)

    count = q_ref.shape[1]
    slot = lax.broadcasted_iota(jnp.int32, (count, cache_ref.shape[1]), 1)
    parts = []
    for s in range(seqs):
        scores = lax.dot_general(
            q_ref[s], cache_ref[s], (((1,), (1,)), ((), ())), preferred_element_type=f32
        )
        scores = scores + jnp.dot(qr_ref[s], rot_ref[s], preferred_element_type=f32)
        parts.append(jnp.where(slot < len_ref[s], scores * softmax_scale, -1e30))
    scores = jnp.concatenate(parts, axis=0)
    raised = jnp.exp(scores - jnp.max(scores, axis=1, keepdims=True))
    probs = (raised / jnp.sum(raised, axis=1, keepdims=True)).astype(bf16)
    for s in range(seqs):
        heads[:, s, :] = jnp.dot(
            probs[s * count : (s + 1) * count], cache_ref[s], preferred_element_type=f32
        )
    for k in range(CHUNKS):
        gathered[k, here] = heads[k * per_chunk : (k + 1) * per_chunk].astype(bf16)
    partial[...] = jnp.zeros_like(partial)
    pl.semaphore_wait(barrier, n)

    step, finish, drain = spread(z, y, c, CHUNKS // 2, gathered, g_up, g_down, g_side, g_sib, g_recv)
    swap = pltpu.make_async_remote_copy(
        src_ref=partial.at[0], dst_ref=partner, send_sem=x_sem.at[0], recv_sem=x_sem.at[1],
        device_id={"head": 1 - h}, device_id_type=MESH,
    )
    swap_last = pltpu.make_async_remote_copy(
        src_ref=last, dst_ref=last_partner, send_sem=x_sem.at[2], recv_sem=x_sem.at[3],
        device_id={"head": 1 - h}, device_id_type=MESH,
    )
    step(0, 0)
    step(1, 0)

    def turn(t, carry):
        for d in range(LINE, -1, -1):
            k = t - d if d else t + 1

            @pl.when(jnp.logical_and(k >= 0, k < CHUNKS))
            def _():
                step(k, d)

        @pl.when(t == LINE)
        def _():
            loads[0].wait()

        @pl.when(t >= LINE)
        def _():
            k = t - LINE
            finish(k)
            total = partial.at[k // (CHUNKS - 1)]
            for j in range(0, per_chunk, 2):
                x = jnp.concatenate(
                    [rows_of(gathered[k, :, j]), rows_of(gathered[k, :, j + 1])], axis=1
                )
                start = pl.multiple_of((k * per_chunk + j) * latent, 2 * latent)
                total[...] += lax.dot_general(
                    x, wvo[:, pl.ds(start, 2 * latent)], (((1,), (1,)), ((), ())),
                    preferred_element_type=f32,
                )

            @pl.when(k == CHUNKS - 2)
            def _():
                swap.start()

        return carry

    lax.fori_loop(1, CHUNKS + LINE, turn, 0)

    last[...] = partial[1].astype(bf16)
    swap_last.start()
    for k in range(CHUNKS):
        drain(k)
    swap.wait_recv()
    sums = partial[0] + partial[1] + partner[...]
    swap_last.wait_recv()
    outgoing[...] = blocks_of(sums + last_partner[...].astype(f32), n)

    def owner(o, source, target, send, recv):
        to = lax.rem(me + o, n)
        return pltpu.make_async_remote_copy(
            src_ref=source.at[block_of(to)], dst_ref=target.at[me], send_sem=send.at[to],
            recv_sem=recv.at[me], device_id={"expert": to}, device_id_type=MESH,
        )

    def exchange_start(source, target, send, recv):
        def body(o, carry):
            owner(o, source, target, send, recv).start()
            return carry

        lax.fori_loop(1, n, body, 0)

    def exchange_recv(source, target, send, recv):
        def body(o, carry):
            who = lax.rem(me + o, n)
            pltpu.make_async_remote_copy(
                src_ref=source.at[block_of(who)], dst_ref=target.at[who], send_sem=send.at[who],
                recv_sem=recv.at[who], device_id={"expert": who}, device_id_type=MESH,
            ).wait_recv()
            return carry

        lax.fori_loop(1, n, body, 0)

    def exchange_sent(source, target, send, recv):
        def body(o, carry):
            owner(o, source, target, send, recv).wait_send()
            return carry

        lax.fori_loop(1, n, body, 0)

    exchange_start(outgoing, incoming, a_send, a_recv)
    incoming[me] = outgoing[here]
    ids = ids_ref[...]
    lane = lax.broadcasted_iota(jnp.int32, (seqs, EXTRA), 1)
    named = jnp.zeros((seqs, EXTRA), f32)
    for k in range(top):
        named = named + jnp.where(ids[:, k : k + 1] == lane, 1.0, 0.0)
    exchange_recv(outgoing, incoming, a_send, a_recv)

    for e in range(n):
        stream[:, e * cols : (e + 1) * cols] = incoming[e].astype(f32)
    rows = stream[...] + resid_ref[...].astype(f32)
    stream[...] = rows
    mean_square = jnp.sum(rows * rows, axis=1, keepdims=True) * (1.0 / width)
    normed = rows * lax.rsqrt(mean_square + norm_epsilon) * gain_ref[...]
    for k in range(PARTS):
        tokens[k, here, :, :span] = normed[:, k * span : (k + 1) * span].astype(bf16)
        tokens[k, here, :, span:] = named.astype(bf16)

    t_step, t_finish, t_drain = spread(z, y, c, PARTS // 2, tokens, t_up, t_down, t_side, t_sib, t_recv)
    for d in range(LINE + 1):
        for k in range(PARTS):
            t_step(k, d)

    wide = n * ROWS
    place = lax.broadcasted_iota(jnp.int32, (seqs, wide), 1)
    which, at = place // ROWS, place % ROWS
    hit = jnp.zeros((seqs, wide), f32)
    share = jnp.zeros((seqs, wide), f32)
    for k in range(top):
        same = ids[:, k : k + 1] == which
        hit = hit + jnp.where(same, 1.0, 0.0)
        share = share + jnp.where(same, weights_ref[:, k : k + 1], 0.0)
    token = lax.broadcasted_iota(jnp.int32, (seqs, wide), 0)
    rank = jnp.zeros((seqs, wide), f32)
    for t in range(seqs - 1):
        rank = rank + jnp.where(token > t, hit[t : t + 1, :], 0.0)
    mixes = []
    for a in range(pieces):
        mix = jnp.where(rank == (at - a * capacity).astype(f32), share, 0.0)
        high = mix.astype(bf16)
        mixes.append((high, (mix - high.astype(f32)).astype(bf16)))
    swap.wait_send()
    swap_last.wait_send()
    exchange_sent(outgoing, incoming, a_send, a_recv)

    t_finish(0)
    loads[1].wait()

    total = n * seqs
    flags = rows_of(tokens[0, :, :, span:])
    mine = jnp.where(lax.broadcasted_iota(jnp.int32, (8, EXTRA), 1) == me, 1.0, 0.0).astype(bf16)
    chosen = lax.dot_general(mine, flags, (((1,), (1,)), ((), ())), preferred_element_type=f32)
    first = lax.broadcasted_iota(jnp.int32, (total, total), 0)
    second = lax.broadcasted_iota(jnp.int32, (total, total), 1)
    ahead = jnp.where(
        jnp.logical_and(first < second, first // seqs == second // seqs), 1.0, 0.0
    ).astype(bf16)
    order = jnp.dot(chosen.astype(bf16), ahead, preferred_element_type=f32)
    count = capacity * n
    row = lax.broadcasted_iota(jnp.int32, (count, total), 0)
    tok = lax.broadcasted_iota(jnp.int32, (count, total), 1)
    fits = jnp.logical_and(order[0:1, :] == (row // n).astype(f32), tok // seqs == row % n)
    pick = jnp.where(fits, chosen[0:1, :], 0.0).astype(bf16)

    units = wgu.shape[1]
    gate = jnp.zeros((count, units), f32)
    lift = jnp.zeros((count, units), f32)
    for k in range(PARTS):
        if k > 0:
            t_finish(k)
        for j in range(2):
            lanes = slice(j * span // 2, (j + 1) * span // 2)
            deep = slice(k * span + j * span // 2, k * span + (j + 1) * span // 2)
            x = jnp.dot(pick, rows_of(tokens[k, :, :, lanes]), preferred_element_type=f32)
            x = x.astype(bf16)
            gate += lax.dot_general(
                x, wgu[0, :, deep], (((1,), (1,)), ((), ())), preferred_element_type=f32
            )
            lift += lax.dot_general(
                x, wgu[1, :, deep], (((1,), (1,)), ((), ())), preferred_element_type=f32
            )
    hidden = (gate / (1.0 + jnp.exp(-gate)) * lift).astype(bf16)
    loads[2].wait()
    share_cols = half // PARTS

    def trade(p):
        return pltpu.make_async_remote_copy(
            src_ref=rows_send.at[p], dst_ref=rows_recv.at[p], send_sem=y_send.at[p],
            recv_sem=y_recv.at[p], device_id={"head": 1 - h}, device_id_type=MESH,
        )

    for p in range(PARTS):
        theirs = pl.ds(pl.multiple_of((1 - h) * half + p * share_cols, share_cols), share_cols)
        rows_send[p] = jnp.dot(hidden, wdn[:, theirs], preferred_element_type=f32).astype(bf16)
        trade(p).start()
    ours = pl.ds(pl.multiple_of(h * half, half), half)
    own = jnp.dot(hidden, wdn[:, ours], preferred_element_type=f32)
    dest = lax.broadcasted_iota(jnp.int32, (wide, count), 0)
    from_row = lax.broadcasted_iota(jnp.int32, (wide, count), 1)
    home = (from_row % n) * ROWS + from_row // n
    puts = [jnp.where(dest == home + a * capacity, 1.0, 0.0).astype(bf16) for a in range(pieces)]
    for p in range(PARTS):
        t_drain(p)
    for p in range(PARTS):
        trade(p).wait_recv()
        summed = own[:, p * share_cols : (p + 1) * share_cols] + rows_recv[p].astype(f32)
        summed = summed.astype(bf16)
        back = jnp.zeros((wide, piece), f32)
        for a in range(pieces):
            columns = summed[:, a * piece : (a + 1) * piece]
            back = back + jnp.dot(puts[a], columns, preferred_element_type=f32)
        back_out[p] = blocks_of(back, n)
        exchange_start(back_out.at[p], back_in.at[p], b_send.at[p], b_recv.at[p])
        back_in[p, me] = back_out[p, here]

    for p in range(PARTS):
        exchange_recv(back_out.at[p], back_in.at[p], b_send.at[p], b_recv.at[p])
        returned = rows_of(back_in[p])
        for a in range(pieces):
            added = jnp.dot(mixes[a][0], returned, preferred_element_type=f32)
            added = added + jnp.dot(mixes[a][1], returned, preferred_element_type=f32)
            at = p * share_cols + a * piece
            start = pl.multiple_of(h * half + at, piece)
            out_ref[:, at : at + piece] = stream[:, pl.ds(start, piece)] + added

    for p in range(PARTS):
        trade(p).wait_send()
        exchange_sent(back_out.at[p], back_in.at[p], b_send.at[p], b_recv.at[p])


def fused(q_latent, q_rotary, cache_latent, cache_rotary, lengths, resid, norm_gain, route_ids, route_weights, w_value_out,
          w_gate_up, w_down):
    n = LINE * PAIR * CORE
    seqs, width = resid.shape
    head_count, latent = q_latent.shape[1:]
    cols = w_value_out.shape[1]
    half = width // 2
    capacity = -(-(seqs * route_ids.shape[1]) // n)
    gate_up, down = w_gate_up[0], w_down[0]
    bf16, f32 = jnp.bfloat16, jnp.float32
    vmem, anywhere = pl.BlockSpec(memory_space=pltpu.VMEM), pl.BlockSpec(memory_space=pl.ANY)
    dma = pltpu.SemaphoreType.DMA
    return pl.pallas_call(
        layer_kernel,
        out_shape=jax.ShapeDtypeStruct((seqs, half), f32),
        in_specs=[vmem] * 4 + [pl.BlockSpec(memory_space=pltpu.SMEM)] + [vmem] * 4 + [anywhere] * 3,
        out_specs=vmem,
        scratch_shapes=[
            pltpu.VMEM(w_value_out.shape[::-1], bf16),
            pltpu.VMEM(gate_up.shape, bf16),
            pltpu.VMEM(down.shape, bf16),
            pltpu.VMEM((head_count, seqs, latent), f32),
            pltpu.VMEM((CHUNKS, n, head_count // CHUNKS, seqs, latent), bf16),
            pltpu.VMEM((2, n * seqs, cols), f32),
            pltpu.VMEM((n * seqs, cols), f32),
            pltpu.VMEM((n * seqs, cols), bf16),
            pltpu.VMEM((n * seqs, cols), bf16),
            pltpu.VMEM((n, seqs, cols), bf16),
            pltpu.VMEM((n, seqs, cols), bf16),
            pltpu.VMEM((seqs, width), f32),
            pltpu.VMEM((PARTS, n, seqs, width // PARTS + EXTRA), bf16),
            pltpu.VMEM((PARTS, capacity * n, half // PARTS), bf16),
            pltpu.VMEM((PARTS, capacity * n, half // PARTS), bf16),
            pltpu.VMEM((PARTS, n, ROWS, half // (PARTS * (ROWS // capacity))), bf16),
            pltpu.VMEM((PARTS, n, ROWS, half // (PARTS * (ROWS // capacity))), bf16),
            dma((3,)),
            dma((CHUNKS, PAIR * LINE)), dma((CHUNKS, PAIR * LINE)), dma((CHUNKS, LINE)),
            dma((CHUNKS, PAIR)), dma((CHUNKS, PAIR * LINE + PAIR)),
            dma((PARTS, PAIR * LINE)), dma((PARTS, PAIR * LINE)), dma((PARTS, LINE)),
            dma((PARTS, PAIR)), dma((PARTS, PAIR * LINE + PAIR)),
            dma((4,)), dma((PARTS,)), dma((PARTS,)), dma((n,)), dma((n,)),
            dma((PARTS, n)), dma((PARTS, n)),
        ],
        compiler_params=pltpu.CompilerParams(
            collective_id=0, has_side_effects=True, vmem_limit_bytes=56 * 1024 * 1024
        ),
    )(
        q_latent, q_rotary, cache_latent, cache_rotary, lengths, resid,
        norm_gain[None, :], route_ids, route_weights, w_value_out.T, gate_up, down,
    )


def attend(q_latent, q_rotary, cache_latent, cache_rotary, lengths):
    scores = jnp.einsum("shl,scl->shc", q_latent, cache_latent, preferred_element_type=jnp.float32)
    scores = scores + jnp.einsum(
        "shr,src->shc", q_rotary, cache_rotary, preferred_element_type=jnp.float32
    )
    scores = scores * softmax_scale
    position = lax.broadcasted_iota(jnp.int32, scores.shape, 2)
    scores = jnp.where(position < lengths[:, None, None], scores, -1e30)
    highest = jnp.max(scores, axis=2, keepdims=True)
    weights = jnp.exp(scores - highest)
    probs = (weights / jnp.sum(weights, axis=2, keepdims=True)).astype(jnp.bfloat16)
    return jnp.einsum(
        "shc,scl->shl", probs, cache_latent, preferred_element_type=jnp.float32
    ).astype(jnp.bfloat16)


def on_device(
    q_latent,
    q_rotary,
    cache_latent,
    cache_rotary,
    lengths,
    w_value_out,
    resid,
    norm_gain,
    route_ids,
    route_weights,
    w_gate_up,
    w_down,
):
    seq_local = q_latent.shape[0]
    if (
        lax.axis_size("head") == 2
        and lax.axis_size("expert") == LINE * PAIR * CORE
        and seq_local == 8
    ):
        return fused(
            q_latent, q_rotary, cache_latent, cache_rotary, lengths, resid, norm_gain,
            route_ids, route_weights, w_value_out, w_gate_up, w_down,
        )
    latent_out = attend(q_latent, q_rotary, cache_latent, cache_rotary, lengths)
    flattened = latent_out.reshape(seq_local, -1)
    column_terms = jnp.dot(
        lax.all_gather(flattened, "expert", axis=0, tiled=True),
        w_value_out,
        preferred_element_type=jnp.float32,
    )
    column_sums = lax.psum(column_terms, "head")
    attention = lax.all_to_all(
        column_sums.astype(jnp.bfloat16), "expert", split_axis=0, concat_axis=1, tiled=True
    )
    stream = resid.astype(jnp.float32) + attention.astype(jnp.float32)
    mean_square = jnp.mean(stream * stream, axis=1, keepdims=True)
    normed = (stream * lax.rsqrt(mean_square + norm_epsilon) * norm_gain).astype(jnp.bfloat16)
    expert_count = lax.axis_size("expert")
    top_count = route_ids.shape[1]
    capacity = max(2, -(-(seq_local * top_count) // expert_count))
    flat_ids = route_ids.reshape(-1)
    one_hot = (flat_ids[:, None] == jnp.arange(expert_count, dtype=jnp.int32)[None, :]).astype(
        jnp.int32
    )
    earlier = jnp.cumsum(one_hot, axis=0) - one_hot
    slot_index = jnp.sum(earlier * one_hot, axis=1)
    target = (flat_ids * capacity + slot_index).reshape(seq_local, top_count)
    places = jnp.arange(expert_count * capacity, dtype=jnp.int32)
    matches = target[None, :, :] == places[:, None, None]
    selector = jnp.sum(matches.astype(jnp.int32), axis=2).astype(jnp.bfloat16)
    blending = jnp.sum(jnp.where(matches, route_weights[None, :, :], 0.0), axis=2)
    outgoing = jnp.dot(selector, normed, preferred_element_type=jnp.float32).astype(jnp.bfloat16)
    outgoing = outgoing.reshape(expert_count, capacity, -1)
    gate_up = w_gate_up[0]
    down_local = w_down[0]
    col_width = stream.shape[1] // lax.axis_size("head")
    offset = lax.axis_index("head") * col_width
    arrived = lax.all_to_all(outgoing, "expert", split_axis=0, concat_axis=0, tiled=True)
    flat_rows = arrived.reshape(-1, arrived.shape[2])
    projected = jnp.einsum("rd,gfd->rgf", flat_rows, gate_up, preferred_element_type=jnp.float32)
    hidden = (jax.nn.silu(projected[:, 0]) * projected[:, 1]).astype(jnp.bfloat16)
    partial_rows = jnp.dot(hidden, down_local, preferred_element_type=jnp.float32)
    expert_terms = partial_rows.reshape(arrived.shape[0], arrived.shape[1], -1)
    summed_rows = lax.psum(expert_terms.astype(jnp.bfloat16), "head")
    returned = lax.all_to_all(summed_rows, "expert", split_axis=0, concat_axis=0, tiled=True)
    back_rows = returned.reshape(expert_count * capacity, -1).astype(jnp.float32)
    mixture = jnp.dot(blending.T, back_rows, precision=lax.Precision.HIGHEST)
    mixed_full = stream + mixture
    return lax.dynamic_slice_in_dim(mixed_full, offset, col_width, 1)


def solution(mesh):
    placed = (
        P("expert", "head", None),
        P("expert", "head", None),
        P("expert", None, None),
        P("expert", None, None),
        P("expert"),
        P("head", "expert"),
        P("expert", None),
        P(),
        P("expert", None),
        P("expert", None),
        P("expert", None, "head", None),
        P("expert", "head", None),
    )
    return jax.shard_map(
        on_device, mesh=mesh, in_specs=placed, out_specs=P("expert", "head"), check_vma=False
    )
```

```python
import functools

import jax
import jax.numpy as jnp
from jax import lax
from jax.experimental import pallas as pl
from jax.experimental.pallas import tpu as pltpu
from jax.sharding import PartitionSpec as P

MESH = pl.DeviceIdType.MESH
softmax_scale = 192.0 ** (-0.5)
norm_epsilon = 1e-06

LINE, PAIR, CORE = 4, 2, 2
CHUNKS = 2
EXTRA = 128
ROWS = 16
PARTS = 2


def rows_of(blocks):
    n, r, c = blocks.shape
    return blocks.astype(jnp.float32).reshape(n * r, c).astype(jnp.bfloat16)


def blocks_of(rows, n):
    return rows.reshape(n, rows.shape[0] // n, rows.shape[1]).astype(jnp.bfloat16)


def device(zz, yy, cc):
    return (zz * PAIR + yy) * CORE + cc


def block_of(e):
    cc, yy, zz = lax.rem(e, CORE), lax.rem(lax.div(e, CORE), PAIR), lax.div(e, PAIR * CORE)
    return (cc * PAIR + yy) * LINE + zz


def spread(z, y, c, far, buffers, up, down, side, sib, recv):
    def slot(zz, yy):
        return (c * PAIR + yy) * LINE + zz

    def copy(k, s, sems, index, target):
        return pltpu.make_async_remote_copy(
            src_ref=buffers.at[k, s],
            dst_ref=buffers.at[k, s],
            send_sem=sems.at[k, index],
            recv_sem=recv.at[k, lax.rem(s, PAIR * LINE)],
            device_id={"expert": target},
            device_id_type=MESH,
        )

    def group(k, yy, core):
        blocks = buffers.at[k, pl.ds((core * PAIR + yy) * LINE, LINE)]
        return pltpu.make_async_remote_copy(
            src_ref=blocks, dst_ref=blocks, send_sem=sib.at[k, yy],
            recv_sem=recv.at[k, PAIR * LINE + yy],
            device_id={"expert": device(z, y, 1 - c)}, device_id_type=MESH,
        )

    def each_send(k, zz, act):
        s = slot(zz, y)

        @pl.when(jnp.logical_and(zz <= z, z < LINE - 1))
        def _():
            act(copy(k, s, up, zz, device(z + 1, y, c)))

        @pl.when(jnp.logical_and(zz >= z, z > 0))
        def _():
            act(copy(k, s, down, zz, device(z - 1, y, c)))

        ends = jnp.logical_or(zz == 0, zz == LINE - 1)
        along = jnp.logical_and(jnp.logical_and(k < far, ends), zz != z)

        @pl.when(jnp.logical_not(along))
        def _():
            act(copy(k, s, side, zz, device(z, 1 - y, c)))

    def each_across(k, zz, act):
        s = slot(zz, 1 - y)

        @pl.when(jnp.logical_and(k < far, jnp.logical_and(zz == 0, z < LINE - 1)))
        def _():
            act(copy(k, s, up, LINE + zz, device(z + 1, y, c)))

        @pl.when(jnp.logical_and(k < far, jnp.logical_and(zz == LINE - 1, z > 0)))
        def _():
            act(copy(k, s, down, LINE + zz, device(z - 1, y, c)))

    def arrived(k, s):
        copy(k, s, side, 0, device(z, 1 - y, c)).wait_recv()

    def at_distance(d, act):
        if d == 0:
            act(z)
            return

        @pl.when(z - d >= 0)
        def _():
            act(z - d)

        @pl.when(z + d < LINE)
        def _():
            act(z + d)

    def step(k, d):
        def line(zz):
            if d > 0:
                arrived(k, slot(zz, y))
            each_send(k, zz, lambda x: x.start())

        def across(zz):
            arrived(k, slot(zz, 1 - y))
            each_across(k, zz, lambda x: x.start())

        if d < LINE:
            at_distance(d, line)
        if d == LINE - 1:
            group(k, y, c).start()
        if d > 0:
            at_distance(d - 1, across)
        if d == LINE:
            group(k, 1 - y, c).start()

    def finish(k):
        group(k, y, 1 - c).wait_recv()
        group(k, 1 - y, 1 - c).wait_recv()

    def drain(k):
        def body(zz, carry):
            each_send(k, zz, lambda x: x.wait_send())
            each_across(k, zz, lambda x: x.wait_send())
            return carry

        lax.fori_loop(0, LINE, body, 0)
        group(k, y, c).wait_send()
        group(k, 1 - y, c).wait_send()

    return step, finish, drain


def layer_kernel(
    q_ref, qr_ref, cache_ref, rot_ref, len_ref, resid_ref, gain_ref, ids_ref, weights_ref, wvo_hbm, wgu_hbm, wdn_hbm,
    out_ref,
    wvo, wgu, wdn, heads, gathered, partial, partner, last, last_partner, outgoing, incoming, stream,
    tokens, rows_send, rows_recv, back_out, back_in,
    w_sem, g_up, g_down, g_side, g_sib, g_recv, t_up, t_down, t_side, t_sib, t_recv,
    x_sem, y_send, y_recv, a_send, a_recv, b_send, b_recv,
):
    n = LINE * PAIR * CORE
    h, me = lax.axis_index("head"), lax.axis_index("expert")
    z, y, c = lax.div(me, PAIR * CORE), lax.rem(lax.div(me, CORE), PAIR), lax.rem(me, CORE)
    here = block_of(me)
    seqs, width = resid_ref.shape
    per_chunk, latent = gathered.shape[2], gathered.shape[4]
    cols = partial.shape[1]
    half = out_ref.shape[1]
    span = width // PARTS
    top = ids_ref.shape[1]
    capacity = rows_send.shape[1] // n
    pieces = ROWS // capacity
    piece = half // (PARTS * pieces)
    f32, bf16 = jnp.float32, jnp.bfloat16

    loads = [
        pltpu.make_async_copy(src, dst, w_sem.at[i])
        for i, (src, dst) in enumerate(((wvo_hbm, wvo), (wgu_hbm, wgu), (wdn_hbm, wdn)))
    ]
    for load in loads:
        load.start()

    barrier = pltpu.get_barrier_semaphore()

    def greet(o, carry):
        pl.semaphore_signal(
            barrier, inc=1, device_id={"expert": lax.rem(me + o, n)}, device_id_type=MESH
        )
        return carry

    lax.fori_loop(1, n, greet, 0)
    pl.semaphore_signal(barrier, inc=1, device_id={"head": 1 - h}, device_id_type=MESH)

    count = q_ref.shape[1]
    slot = lax.broadcasted_iota(jnp.int32, (count, cache_ref.shape[1]), 1)
    parts = []
    for s in range(seqs):
        scores = lax.dot_general(
            q_ref[s], cache_ref[s], (((1,), (1,)), ((), ())), preferred_element_type=f32
        )
        scores = scores + jnp.dot(qr_ref[s], rot_ref[s], preferred_element_type=f32)
        parts.append(jnp.where(slot < len_ref[s], scores * softmax_scale, -1e30))
    scores = jnp.concatenate(parts, axis=0)
    raised = jnp.exp(scores - jnp.max(scores, axis=1, keepdims=True))
    probs = (raised / jnp.sum(raised, axis=1, keepdims=True)).astype(bf16)
    for s in range(seqs):
        heads[:, s, :] = jnp.dot(
            probs[s * count : (s + 1) * count], cache_ref[s], preferred_element_type=f32
        )
    for k in range(CHUNKS):
        gathered[k, here] = heads[k * per_chunk : (k + 1) * per_chunk].astype(bf16)
    partial[...] = jnp.zeros_like(partial)
    pl.semaphore_wait(barrier, n)

    step, finish, drain = spread(z, y, c, CHUNKS // 2, gathered, g_up, g_down, g_side, g_sib, g_recv)
    swap = pltpu.make_async_remote_copy(
        src_ref=partial.at[0], dst_ref=partner, send_sem=x_sem.at[0], recv_sem=x_sem.at[1],
        device_id={"head": 1 - h}, device_id_type=MESH,
    )
    swap_last = pltpu.make_async_remote_copy(
        src_ref=last, dst_ref=last_partner, send_sem=x_sem.at[2], recv_sem=x_sem.at[3],
        device_id={"head": 1 - h}, device_id_type=MESH,
    )
    step(0, 0)
    step(1, 0)

    def turn(t, carry):
        for d in range(LINE, -1, -1):
            k = t - d if d else t + 1

            @pl.when(jnp.logical_and(k >= 0, k < CHUNKS))
            def _():
                step(k, d)

        @pl.when(t == LINE)
        def _():
            loads[0].wait()

        @pl.when(t >= LINE)
        def _():
            k = t - LINE
            finish(k)
            total = partial.at[k // (CHUNKS - 1)]
            for j in range(0, per_chunk, 2):
                x = jnp.concatenate(
                    [rows_of(gathered[k, :, j]), rows_of(gathered[k, :, j + 1])], axis=1
                )
                start = pl.multiple_of((k * per_chunk + j) * latent, 2 * latent)
                total[...] += lax.dot_general(
                    wvo[:, pl.ds(start, 2 * latent)], x, (((1,), (1,)), ((), ())),
                    preferred_element_type=f32,
                )

            @pl.when(k == CHUNKS - 2)
            def _():
                swap.start()

        return carry

    lax.fori_loop(1, CHUNKS + LINE, turn, 0)

    last[...] = partial[1].astype(bf16)
    swap_last.start()
    for k in range(CHUNKS):
        drain(k)
    swap.wait_recv()
    sums = partial[0] + partial[1] + partner[...]
    swap_last.wait_recv()
    outgoing[...] = blocks_of((sums + last_partner[...].astype(f32)).T, n)

    def owner(o, source, target, send, recv):
        to = lax.rem(me + o, n)
        return pltpu.make_async_remote_copy(
            src_ref=source.at[block_of(to)], dst_ref=target.at[me], send_sem=send.at[to],
            recv_sem=recv.at[me], device_id={"expert": to}, device_id_type=MESH,
        )

    def exchange_start(source, target, send, recv):
        def body(o, carry):
            owner(o, source, target, send, recv).start()
            return carry

        lax.fori_loop(1, n, body, 0)

    def exchange_recv(source, target, send, recv):
        def body(o, carry):
            who = lax.rem(me + o, n)
            pltpu.make_async_remote_copy(
                src_ref=source.at[block_of(who)], dst_ref=target.at[who], send_sem=send.at[who],
                recv_sem=recv.at[who], device_id={"expert": who}, device_id_type=MESH,
            ).wait_recv()
            return carry

        lax.fori_loop(1, n, body, 0)

    def exchange_sent(source, target, send, recv):
        def body(o, carry):
            owner(o, source, target, send, recv).wait_send()
            return carry

        lax.fori_loop(1, n, body, 0)

    exchange_start(outgoing, incoming, a_send, a_recv)
    incoming[me] = outgoing[here]
    ids = ids_ref[...]
    lane = lax.broadcasted_iota(jnp.int32, (seqs, EXTRA), 1)
    named = jnp.zeros((seqs, EXTRA), f32)
    for k in range(top):
        named = named + jnp.where(ids[:, k : k + 1] == lane, 1.0, 0.0)
    exchange_recv(outgoing, incoming, a_send, a_recv)

    for e in range(n):
        stream[:, e * cols : (e + 1) * cols] = incoming[e].astype(f32)
    rows = stream[...] + resid_ref[...].astype(f32)
    stream[...] = rows
    mean_square = jnp.sum(rows * rows, axis=1, keepdims=True) * (1.0 / width)
    normed = rows * lax.rsqrt(mean_square + norm_epsilon) * gain_ref[...]
    for k in range(PARTS):
        tokens[k, here, :, :span] = normed[:, k * span : (k + 1) * span].astype(bf16)
        tokens[k, here, :, span:] = named.astype(bf16)

    t_step, t_finish, t_drain = spread(z, y, c, PARTS // 2, tokens, t_up, t_down, t_side, t_sib, t_recv)
    for d in range(LINE + 1):
        for k in range(PARTS):
            t_step(k, d)

    wide = n * ROWS
    place = lax.broadcasted_iota(jnp.int32, (seqs, wide), 1)
    which, at = place // ROWS, place % ROWS
    hit = jnp.zeros((seqs, wide), f32)
    share = jnp.zeros((seqs, wide), f32)
    for k in range(top):
        same = ids[:, k : k + 1] == which
        hit = hit + jnp.where(same, 1.0, 0.0)
        share = share + jnp.where(same, weights_ref[:, k : k + 1], 0.0)
    token = lax.broadcasted_iota(jnp.int32, (seqs, wide), 0)
    rank = jnp.zeros((seqs, wide), f32)
    for t in range(seqs - 1):
        rank = rank + jnp.where(token > t, hit[t : t + 1, :], 0.0)
    mixes = []
    for a in range(pieces):
        mix = jnp.where(rank == (at - a * capacity).astype(f32), share, 0.0)
        high = mix.astype(bf16)
        mixes.append((high, (mix - high.astype(f32)).astype(bf16)))
    swap.wait_send()
    swap_last.wait_send()
    exchange_sent(outgoing, incoming, a_send, a_recv)

    t_finish(0)
    loads[1].wait()

    total = n * seqs
    flags = rows_of(tokens[0, :, :, span:])
    mine = jnp.where(lax.broadcasted_iota(jnp.int32, (8, EXTRA), 1) == me, 1.0, 0.0).astype(bf16)
    chosen = lax.dot_general(mine, flags, (((1,), (1,)), ((), ())), preferred_element_type=f32)
    first = lax.broadcasted_iota(jnp.int32, (total, total), 0)
    second = lax.broadcasted_iota(jnp.int32, (total, total), 1)
    ahead = jnp.where(
        jnp.logical_and(first < second, first // seqs == second // seqs), 1.0, 0.0
    ).astype(bf16)
    order = jnp.dot(chosen.astype(bf16), ahead, preferred_element_type=f32)
    count = capacity * n
    row = lax.broadcasted_iota(jnp.int32, (count, total), 0)
    tok = lax.broadcasted_iota(jnp.int32, (count, total), 1)
    fits = jnp.logical_and(order[0:1, :] == (row // n).astype(f32), tok // seqs == row % n)
    pick = jnp.where(fits, chosen[0:1, :], 0.0).astype(bf16)

    units = wgu.shape[1]
    gate = jnp.zeros((count, units), f32)
    lift = jnp.zeros((count, units), f32)
    for k in range(PARTS):
        if k > 0:
            t_finish(k)
        for j in range(2):
            lanes = slice(j * span // 2, (j + 1) * span // 2)
            deep = slice(k * span + j * span // 2, k * span + (j + 1) * span // 2)
            x = jnp.dot(pick, rows_of(tokens[k, :, :, lanes]), preferred_element_type=f32)
            x = x.astype(bf16)
            gate += lax.dot_general(
                x, wgu[0, :, deep], (((1,), (1,)), ((), ())), preferred_element_type=f32
            )
            lift += lax.dot_general(
                x, wgu[1, :, deep], (((1,), (1,)), ((), ())), preferred_element_type=f32
            )
    hidden = (gate / (1.0 + jnp.exp(-gate)) * lift).astype(bf16)
    loads[2].wait()
    share_cols = half // PARTS

    def trade(p):
        return pltpu.make_async_remote_copy(
            src_ref=rows_send.at[p], dst_ref=rows_recv.at[p], send_sem=y_send.at[p],
            recv_sem=y_recv.at[p], device_id={"head": 1 - h}, device_id_type=MESH,
        )

    for p in range(PARTS):
        theirs = pl.ds(pl.multiple_of((1 - h) * half + p * share_cols, share_cols), share_cols)
        rows_send[p] = jnp.dot(hidden, wdn[:, theirs], preferred_element_type=f32).astype(bf16)
        trade(p).start()
    ours = pl.ds(pl.multiple_of(h * half, half), half)
    own = jnp.dot(hidden, wdn[:, ours], preferred_element_type=f32)
    dest = lax.broadcasted_iota(jnp.int32, (wide, count), 0)
    from_row = lax.broadcasted_iota(jnp.int32, (wide, count), 1)
    home = (from_row % n) * ROWS + from_row // n
    puts = [jnp.where(dest == home + a * capacity, 1.0, 0.0).astype(bf16) for a in range(pieces)]
    for p in range(PARTS):
        t_drain(p)
    for p in range(PARTS):
        trade(p).wait_recv()
        summed = own[:, p * share_cols : (p + 1) * share_cols] + rows_recv[p].astype(f32)
        summed = summed.astype(bf16)
        back = jnp.zeros((wide, piece), f32)
        for a in range(pieces):
            columns = summed[:, a * piece : (a + 1) * piece]
            back = back + jnp.dot(puts[a], columns, preferred_element_type=f32)
        back_out[p] = blocks_of(back, n)
        exchange_start(back_out.at[p], back_in.at[p], b_send.at[p], b_recv.at[p])
        back_in[p, me] = back_out[p, here]

    for p in range(PARTS):
        exchange_recv(back_out.at[p], back_in.at[p], b_send.at[p], b_recv.at[p])
        returned = rows_of(back_in[p])
        for a in range(pieces):
            added = jnp.dot(mixes[a][0], returned, preferred_element_type=f32)
            added = added + jnp.dot(mixes[a][1], returned, preferred_element_type=f32)
            at = p * share_cols + a * piece
            start = pl.multiple_of(h * half + at, piece)
            out_ref[:, at : at + piece] = stream[:, pl.ds(start, piece)] + added

    for p in range(PARTS):
        trade(p).wait_send()
        exchange_sent(back_out.at[p], back_in.at[p], b_send.at[p], b_recv.at[p])


def fused(q_latent, q_rotary, cache_latent, cache_rotary, lengths, resid, norm_gain, route_ids, route_weights, w_value_out,
          w_gate_up, w_down):
    n = LINE * PAIR * CORE
    seqs, width = resid.shape
    head_count, latent = q_latent.shape[1:]
    cols = w_value_out.shape[1]
    half = width // 2
    capacity = -(-(seqs * route_ids.shape[1]) // n)
    gate_up, down = w_gate_up[0], w_down[0]
    bf16, f32 = jnp.bfloat16, jnp.float32
    vmem, anywhere = pl.BlockSpec(memory_space=pltpu.VMEM), pl.BlockSpec(memory_space=pl.ANY)
    dma = pltpu.SemaphoreType.DMA
    return pl.pallas_call(
        layer_kernel,
        out_shape=jax.ShapeDtypeStruct((seqs, half), f32),
        in_specs=[vmem] * 4 + [pl.BlockSpec(memory_space=pltpu.SMEM)] + [vmem] * 4 + [anywhere] * 3,
        out_specs=vmem,
        scratch_shapes=[
            pltpu.VMEM(w_value_out.shape[::-1], bf16),
            pltpu.VMEM(gate_up.shape, bf16),
            pltpu.VMEM(down.shape, bf16),
            pltpu.VMEM((head_count, seqs, latent), f32),
            pltpu.VMEM((CHUNKS, n, head_count // CHUNKS, seqs, latent), bf16),
            pltpu.VMEM((2, cols, n * seqs), f32),
            pltpu.VMEM((cols, n * seqs), f32),
            pltpu.VMEM((cols, n * seqs), bf16),
            pltpu.VMEM((cols, n * seqs), bf16),
            pltpu.VMEM((n, seqs, cols), bf16),
            pltpu.VMEM((n, seqs, cols), bf16),
            pltpu.VMEM((seqs, width), f32),
            pltpu.VMEM((PARTS, n, seqs, width // PARTS + EXTRA), bf16),
            pltpu.VMEM((PARTS, capacity * n, half // PARTS), bf16),
            pltpu.VMEM((PARTS, capacity * n, half // PARTS), bf16),
            pltpu.VMEM((PARTS, n, ROWS, half // (PARTS * (ROWS // capacity))), bf16),
            pltpu.VMEM((PARTS, n, ROWS, half // (PARTS * (ROWS // capacity))), bf16),
            dma((3,)),
            dma((CHUNKS, PAIR * LINE)), dma((CHUNKS, PAIR * LINE)), dma((CHUNKS, LINE)),
            dma((CHUNKS, PAIR)), dma((CHUNKS, PAIR * LINE + PAIR)),
            dma((PARTS, PAIR * LINE)), dma((PARTS, PAIR * LINE)), dma((PARTS, LINE)),
            dma((PARTS, PAIR)), dma((PARTS, PAIR * LINE + PAIR)),
            dma((4,)), dma((PARTS,)), dma((PARTS,)), dma((n,)), dma((n,)),
            dma((PARTS, n)), dma((PARTS, n)),
        ],
        compiler_params=pltpu.CompilerParams(
            collective_id=0, has_side_effects=True, vmem_limit_bytes=56 * 1024 * 1024
        ),
    )(
        q_latent, q_rotary, cache_latent, cache_rotary, lengths, resid,
        norm_gain[None, :], route_ids, route_weights, w_value_out.T, gate_up, down,
    )


def attend(q_latent, q_rotary, cache_latent, cache_rotary, lengths):
    scores = jnp.einsum("shl,scl->shc", q_latent, cache_latent, preferred_element_type=jnp.float32)
    scores = scores + jnp.einsum(
        "shr,src->shc", q_rotary, cache_rotary, preferred_element_type=jnp.float32
    )
    scores = scores * softmax_scale
    position = lax.broadcasted_iota(jnp.int32, scores.shape, 2)
    scores = jnp.where(position < lengths[:, None, None], scores, -1e30)
    highest = jnp.max(scores, axis=2, keepdims=True)
    weights = jnp.exp(scores - highest)
    probs = (weights / jnp.sum(weights, axis=2, keepdims=True)).astype(jnp.bfloat16)
    return jnp.einsum(
        "shc,scl->shl", probs, cache_latent, preferred_element_type=jnp.float32
    ).astype(jnp.bfloat16)


def on_device(
    q_latent,
    q_rotary,
    cache_latent,
    cache_rotary,
    lengths,
    w_value_out,
    resid,
    norm_gain,
    route_ids,
    route_weights,
    w_gate_up,
    w_down,
):
    seq_local = q_latent.shape[0]
    if (
        lax.axis_size("head") == 2
        and lax.axis_size("expert") == LINE * PAIR * CORE
        and seq_local == 8
    ):
        return fused(
            q_latent, q_rotary, cache_latent, cache_rotary, lengths, resid, norm_gain,
            route_ids, route_weights, w_value_out, w_gate_up, w_down,
        )
    latent_out = attend(q_latent, q_rotary, cache_latent, cache_rotary, lengths)
    flattened = latent_out.reshape(seq_local, -1)
    column_terms = jnp.dot(
        lax.all_gather(flattened, "expert", axis=0, tiled=True),
        w_value_out,
        preferred_element_type=jnp.float32,
    )
    column_sums = lax.psum(column_terms, "head")
    attention = lax.all_to_all(
        column_sums.astype(jnp.bfloat16), "expert", split_axis=0, concat_axis=1, tiled=True
    )
    stream = resid.astype(jnp.float32) + attention.astype(jnp.float32)
    mean_square = jnp.mean(stream * stream, axis=1, keepdims=True)
    normed = (stream * lax.rsqrt(mean_square + norm_epsilon) * norm_gain).astype(jnp.bfloat16)
    expert_count = lax.axis_size("expert")
    top_count = route_ids.shape[1]
    capacity = max(2, -(-(seq_local * top_count) // expert_count))
    flat_ids = route_ids.reshape(-1)
    one_hot = (flat_ids[:, None] == jnp.arange(expert_count, dtype=jnp.int32)[None, :]).astype(
        jnp.int32
    )
    earlier = jnp.cumsum(one_hot, axis=0) - one_hot
    slot_index = jnp.sum(earlier * one_hot, axis=1)
    target = (flat_ids * capacity + slot_index).reshape(seq_local, top_count)
    places = jnp.arange(expert_count * capacity, dtype=jnp.int32)
    matches = target[None, :, :] == places[:, None, None]
    selector = jnp.sum(matches.astype(jnp.int32), axis=2).astype(jnp.bfloat16)
    blending = jnp.sum(jnp.where(matches, route_weights[None, :, :], 0.0), axis=2)
    outgoing = jnp.dot(selector, normed, preferred_element_type=jnp.float32).astype(jnp.bfloat16)
    outgoing = outgoing.reshape(expert_count, capacity, -1)
    gate_up = w_gate_up[0]
    down_local = w_down[0]
    col_width = stream.shape[1] // lax.axis_size("head")
    offset = lax.axis_index("head") * col_width
    arrived = lax.all_to_all(outgoing, "expert", split_axis=0, concat_axis=0, tiled=True)
    flat_rows = arrived.reshape(-1, arrived.shape[2])
    projected = jnp.einsum("rd,gfd->rgf", flat_rows, gate_up, preferred_element_type=jnp.float32)
    hidden = (jax.nn.silu(projected[:, 0]) * projected[:, 1]).astype(jnp.bfloat16)
    partial_rows = jnp.dot(hidden, down_local, preferred_element_type=jnp.float32)
    expert_terms = partial_rows.reshape(arrived.shape[0], arrived.shape[1], -1)
    summed_rows = lax.psum(expert_terms.astype(jnp.bfloat16), "head")
    returned = lax.all_to_all(summed_rows, "expert", split_axis=0, concat_axis=0, tiled=True)
    back_rows = returned.reshape(expert_count * capacity, -1).astype(jnp.float32)
    mixture = jnp.dot(blending.T, back_rows, precision=lax.Precision.HIGHEST)
    mixed_full = stream + mixture
    return lax.dynamic_slice_in_dim(mixed_full, offset, col_width, 1)


def solution(mesh):
    placed = (
        P("expert", "head", None),
        P("expert", "head", None),
        P("expert", None, None),
        P("expert", None, None),
        P("expert"),
        P("head", "expert"),
        P("expert", None),
        P(),
        P("expert", None),
        P("expert", None),
        P("expert", None, "head", None),
        P("expert", "head", None),
    )
    return jax.shard_map(
        on_device, mesh=mesh, in_specs=placed, out_specs=P("expert", "head"), check_vma=False
    )
```

```python
import functools

import jax
import jax.numpy as jnp
from jax import lax
from jax.experimental import pallas as pl
from jax.experimental.pallas import tpu as pltpu
from jax.sharding import PartitionSpec as P

MESH = pl.DeviceIdType.MESH
softmax_scale = 192.0 ** (-0.5)
norm_epsilon = 1e-06

LINE, PAIR, CORE = 4, 2, 2
CHUNKS = 2
EXTRA = 128
ROWS = 16
PARTS = 1


def rows_of(blocks):
    n, r, c = blocks.shape
    return blocks.astype(jnp.float32).reshape(n * r, c).astype(jnp.bfloat16)


def blocks_of(rows, n):
    return rows.reshape(n, rows.shape[0] // n, rows.shape[1]).astype(jnp.bfloat16)


def device(zz, yy, cc):
    return (zz * PAIR + yy) * CORE + cc


def block_of(e):
    cc, yy, zz = lax.rem(e, CORE), lax.rem(lax.div(e, CORE), PAIR), lax.div(e, PAIR * CORE)
    return (cc * PAIR + yy) * LINE + zz


def spread(z, y, c, far, buffers, up, down, side, sib, recv):
    def slot(zz, yy):
        return (c * PAIR + yy) * LINE + zz

    def copy(k, s, sems, index, target):
        return pltpu.make_async_remote_copy(
            src_ref=buffers.at[k, s],
            dst_ref=buffers.at[k, s],
            send_sem=sems.at[k, index],
            recv_sem=recv.at[k, lax.rem(s, PAIR * LINE)],
            device_id={"expert": target},
            device_id_type=MESH,
        )

    def group(k, yy, core):
        blocks = buffers.at[k, pl.ds((core * PAIR + yy) * LINE, LINE)]
        return pltpu.make_async_remote_copy(
            src_ref=blocks, dst_ref=blocks, send_sem=sib.at[k, yy],
            recv_sem=recv.at[k, PAIR * LINE + yy],
            device_id={"expert": device(z, y, 1 - c)}, device_id_type=MESH,
        )

    def each_send(k, zz, act):
        s = slot(zz, y)

        @pl.when(jnp.logical_and(zz <= z, z < LINE - 1))
        def _():
            act(copy(k, s, up, zz, device(z + 1, y, c)))

        @pl.when(jnp.logical_and(zz >= z, z > 0))
        def _():
            act(copy(k, s, down, zz, device(z - 1, y, c)))

        ends = jnp.logical_or(zz == 0, zz == LINE - 1)
        along = jnp.logical_and(jnp.logical_and(k < far, ends), zz != z)

        @pl.when(jnp.logical_not(along))
        def _():
            act(copy(k, s, side, zz, device(z, 1 - y, c)))

    def each_across(k, zz, act):
        s = slot(zz, 1 - y)

        @pl.when(jnp.logical_and(k < far, jnp.logical_and(zz == 0, z < LINE - 1)))
        def _():
            act(copy(k, s, up, LINE + zz, device(z + 1, y, c)))

        @pl.when(jnp.logical_and(k < far, jnp.logical_and(zz == LINE - 1, z > 0)))
        def _():
            act(copy(k, s, down, LINE + zz, device(z - 1, y, c)))

    def arrived(k, s):
        copy(k, s, side, 0, device(z, 1 - y, c)).wait_recv()

    def at_distance(d, act):
        if d == 0:
            act(z)
            return

        @pl.when(z - d >= 0)
        def _():
            act(z - d)

        @pl.when(z + d < LINE)
        def _():
            act(z + d)

    def step(k, d):
        def line(zz):
            if d > 0:
                arrived(k, slot(zz, y))
            each_send(k, zz, lambda x: x.start())

        def across(zz):
            arrived(k, slot(zz, 1 - y))
            each_across(k, zz, lambda x: x.start())

        if d < LINE:
            at_distance(d, line)
        if d == LINE - 1:
            group(k, y, c).start()
        if d > 0:
            at_distance(d - 1, across)
        if d == LINE:
            group(k, 1 - y, c).start()

    def finish(k):
        group(k, y, 1 - c).wait_recv()
        group(k, 1 - y, 1 - c).wait_recv()

    def drain(k):
        def body(zz, carry):
            each_send(k, zz, lambda x: x.wait_send())
            each_across(k, zz, lambda x: x.wait_send())
            return carry

        lax.fori_loop(0, LINE, body, 0)
        group(k, y, c).wait_send()
        group(k, 1 - y, c).wait_send()

    return step, finish, drain


def layer_kernel(
    q_ref, qr_ref, cache_ref, rot_ref, len_ref, resid_ref, gain_ref, ids_ref, weights_ref, wvo_hbm, wgu_hbm, wdn_hbm,
    out_ref,
    wvo, wgu, wdn, heads, gathered, partial, partner, last, last_partner, outgoing, incoming, stream,
    tokens, rows_send, rows_recv, back_out, back_in,
    w_sem, g_up, g_down, g_side, g_sib, g_recv, t_up, t_down, t_side, t_sib, t_recv,
    x_sem, y_send, y_recv, a_send, a_recv, b_send, b_recv,
):
    n = LINE * PAIR * CORE
    h, me = lax.axis_index("head"), lax.axis_index("expert")
    z, y, c = lax.div(me, PAIR * CORE), lax.rem(lax.div(me, CORE), PAIR), lax.rem(me, CORE)
    here = block_of(me)
    seqs, width = resid_ref.shape
    per_chunk, latent = gathered.shape[2], gathered.shape[4]
    cols = partial.shape[1]
    half = out_ref.shape[1]
    span = width // PARTS
    top = ids_ref.shape[1]
    capacity = rows_send.shape[1] // n
    pieces = ROWS // capacity
    piece = half // (PARTS * pieces)
    f32, bf16 = jnp.float32, jnp.bfloat16

    loads = [
        pltpu.make_async_copy(src, dst, w_sem.at[i])
        for i, (src, dst) in enumerate(((wvo_hbm, wvo), (wgu_hbm, wgu), (wdn_hbm, wdn)))
    ]
    for load in loads:
        load.start()

    barrier = pltpu.get_barrier_semaphore()

    def greet(o, carry):
        pl.semaphore_signal(
            barrier, inc=1, device_id={"expert": lax.rem(me + o, n)}, device_id_type=MESH
        )
        return carry

    lax.fori_loop(1, n, greet, 0)
    pl.semaphore_signal(barrier, inc=1, device_id={"head": 1 - h}, device_id_type=MESH)

    count = q_ref.shape[1]
    slot = lax.broadcasted_iota(jnp.int32, (count, cache_ref.shape[1]), 1)
    parts = []
    for s in range(seqs):
        scores = lax.dot_general(
            q_ref[s], cache_ref[s], (((1,), (1,)), ((), ())), preferred_element_type=f32
        )
        scores = scores + jnp.dot(qr_ref[s], rot_ref[s], preferred_element_type=f32)
        parts.append(jnp.where(slot < len_ref[s], scores * softmax_scale, -1e30))
    scores = jnp.concatenate(parts, axis=0)
    raised = jnp.exp(scores - jnp.max(scores, axis=1, keepdims=True))
    probs = (raised / jnp.sum(raised, axis=1, keepdims=True)).astype(bf16)
    for s in range(seqs):
        heads[:, s, :] = jnp.dot(
            probs[s * count : (s + 1) * count], cache_ref[s], preferred_element_type=f32
        )
    for k in range(CHUNKS):
        gathered[k, here] = heads[k * per_chunk : (k + 1) * per_chunk].astype(bf16)
    partial[...] = jnp.zeros_like(partial)
    pl.semaphore_wait(barrier, n)

    step, finish, drain = spread(z, y, c, CHUNKS // 2, gathered, g_up, g_down, g_side, g_sib, g_recv)
    swap = pltpu.make_async_remote_copy(
        src_ref=partial.at[0], dst_ref=partner, send_sem=x_sem.at[0], recv_sem=x_sem.at[1],
        device_id={"head": 1 - h}, device_id_type=MESH,
    )
    swap_last = pltpu.make_async_remote_copy(
        src_ref=last, dst_ref=last_partner, send_sem=x_sem.at[2], recv_sem=x_sem.at[3],
        device_id={"head": 1 - h}, device_id_type=MESH,
    )
    step(0, 0)
    step(1, 0)

    def turn(t, carry):
        for d in range(LINE, -1, -1):
            k = t - d if d else t + 1

            @pl.when(jnp.logical_and(k >= 0, k < CHUNKS))
            def _():
                step(k, d)

        @pl.when(t == LINE)
        def _():
            loads[0].wait()

        @pl.when(t >= LINE)
        def _():
            k = t - LINE
            finish(k)
            total = partial.at[k // (CHUNKS - 1)]
            for j in range(0, per_chunk, 2):
                x = jnp.concatenate(
                    [rows_of(gathered[k, :, j]), rows_of(gathered[k, :, j + 1])], axis=1
                )
                start = pl.multiple_of((k * per_chunk + j) * latent, 2 * latent)
                total[...] += lax.dot_general(
                    wvo[:, pl.ds(start, 2 * latent)], x, (((1,), (1,)), ((), ())),
                    preferred_element_type=f32,
                )

            @pl.when(k == CHUNKS - 2)
            def _():
                swap.start()

        return carry

    lax.fori_loop(1, CHUNKS + LINE, turn, 0)

    last[...] = partial[1].astype(bf16)
    swap_last.start()
    for k in range(CHUNKS):
        drain(k)
    swap.wait_recv()
    sums = partial[0] + partial[1] + partner[...]
    swap_last.wait_recv()
    outgoing[...] = blocks_of((sums + last_partner[...].astype(f32)).T, n)

    def owner(o, source, target, send, recv):
        to = lax.rem(me + o, n)
        return pltpu.make_async_remote_copy(
            src_ref=source.at[block_of(to)], dst_ref=target.at[me], send_sem=send.at[to],
            recv_sem=recv.at[me], device_id={"expert": to}, device_id_type=MESH,
        )

    def exchange_start(source, target, send, recv):
        def body(o, carry):
            owner(o, source, target, send, recv).start()
            return carry

        lax.fori_loop(1, n, body, 0)

    def exchange_recv(source, target, send, recv):
        def body(o, carry):
            who = lax.rem(me + o, n)
            pltpu.make_async_remote_copy(
                src_ref=source.at[block_of(who)], dst_ref=target.at[who], send_sem=send.at[who],
                recv_sem=recv.at[who], device_id={"expert": who}, device_id_type=MESH,
            ).wait_recv()
            return carry

        lax.fori_loop(1, n, body, 0)

    def exchange_sent(source, target, send, recv):
        def body(o, carry):
            owner(o, source, target, send, recv).wait_send()
            return carry

        lax.fori_loop(1, n, body, 0)

    exchange_start(outgoing, incoming, a_send, a_recv)
    incoming[me] = outgoing[here]
    ids = ids_ref[...]
    lane = lax.broadcasted_iota(jnp.int32, (seqs, EXTRA), 1)
    named = jnp.zeros((seqs, EXTRA), f32)
    for k in range(top):
        named = named + jnp.where(ids[:, k : k + 1] == lane, 1.0, 0.0)
    exchange_recv(outgoing, incoming, a_send, a_recv)

    for e in range(n):
        stream[:, e * cols : (e + 1) * cols] = incoming[e].astype(f32)
    rows = stream[...] + resid_ref[...].astype(f32)
    stream[...] = rows
    mean_square = jnp.sum(rows * rows, axis=1, keepdims=True) * (1.0 / width)
    normed = rows * lax.rsqrt(mean_square + norm_epsilon) * gain_ref[...]
    for k in range(PARTS):
        tokens[k, here, :, :span] = normed[:, k * span : (k + 1) * span].astype(bf16)
        tokens[k, here, :, span:] = named.astype(bf16)

    t_step, t_finish, t_drain = spread(z, y, c, PARTS // 2, tokens, t_up, t_down, t_side, t_sib, t_recv)
    for d in range(LINE + 1):
        for k in range(PARTS):
            t_step(k, d)

    wide = n * ROWS
    place = lax.broadcasted_iota(jnp.int32, (seqs, wide), 1)
    which, at = place // ROWS, place % ROWS
    hit = jnp.zeros((seqs, wide), f32)
    share = jnp.zeros((seqs, wide), f32)
    for k in range(top):
        same = ids[:, k : k + 1] == which
        hit = hit + jnp.where(same, 1.0, 0.0)
        share = share + jnp.where(same, weights_ref[:, k : k + 1], 0.0)
    token = lax.broadcasted_iota(jnp.int32, (seqs, wide), 0)
    rank = jnp.zeros((seqs, wide), f32)
    for t in range(seqs - 1):
        rank = rank + jnp.where(token > t, hit[t : t + 1, :], 0.0)
    mixes = []
    for a in range(pieces):
        mix = jnp.where(rank == (at - a * capacity).astype(f32), share, 0.0)
        high = mix.astype(bf16)
        mixes.append((high, (mix - high.astype(f32)).astype(bf16)))
    swap.wait_send()
    swap_last.wait_send()
    exchange_sent(outgoing, incoming, a_send, a_recv)

    t_finish(0)
    loads[1].wait()

    total = n * seqs
    flags = rows_of(tokens[0, :, :, span:])
    mine = jnp.where(lax.broadcasted_iota(jnp.int32, (8, EXTRA), 1) == me, 1.0, 0.0).astype(bf16)
    chosen = lax.dot_general(mine, flags, (((1,), (1,)), ((), ())), preferred_element_type=f32)
    first = lax.broadcasted_iota(jnp.int32, (total, total), 0)
    second = lax.broadcasted_iota(jnp.int32, (total, total), 1)
    ahead = jnp.where(
        jnp.logical_and(first < second, first // seqs == second // seqs), 1.0, 0.0
    ).astype(bf16)
    order = jnp.dot(chosen.astype(bf16), ahead, preferred_element_type=f32)
    count = capacity * n
    row = lax.broadcasted_iota(jnp.int32, (count, total), 0)
    tok = lax.broadcasted_iota(jnp.int32, (count, total), 1)
    fits = jnp.logical_and(order[0:1, :] == (row // n).astype(f32), tok // seqs == row % n)
    pick = jnp.where(fits, chosen[0:1, :], 0.0).astype(bf16)

    units = wgu.shape[1]
    gate = jnp.zeros((count, units), f32)
    lift = jnp.zeros((count, units), f32)
    for k in range(PARTS):
        if k > 0:
            t_finish(k)
        for j in range(2):
            lanes = slice(j * span // 2, (j + 1) * span // 2)
            deep = slice(k * span + j * span // 2, k * span + (j + 1) * span // 2)
            x = jnp.dot(pick, rows_of(tokens[k, :, :, lanes]), preferred_element_type=f32)
            x = x.astype(bf16)
            gate += lax.dot_general(
                x, wgu[0, :, deep], (((1,), (1,)), ((), ())), preferred_element_type=f32
            )
            lift += lax.dot_general(
                x, wgu[1, :, deep], (((1,), (1,)), ((), ())), preferred_element_type=f32
            )
    hidden = (gate / (1.0 + jnp.exp(-gate)) * lift).astype(bf16)
    loads[2].wait()
    share_cols = half // PARTS

    def trade(p):
        return pltpu.make_async_remote_copy(
            src_ref=rows_send.at[p], dst_ref=rows_recv.at[p], send_sem=y_send.at[p],
            recv_sem=y_recv.at[p], device_id={"head": 1 - h}, device_id_type=MESH,
        )

    for p in range(PARTS):
        theirs = pl.ds(pl.multiple_of((1 - h) * half + p * share_cols, share_cols), share_cols)
        rows_send[p] = jnp.dot(hidden, wdn[:, theirs], preferred_element_type=f32).astype(bf16)
        trade(p).start()
    ours = pl.ds(pl.multiple_of(h * half, half), half)
    own = jnp.dot(hidden, wdn[:, ours], preferred_element_type=f32)
    dest = lax.broadcasted_iota(jnp.int32, (wide, count), 0)
    from_row = lax.broadcasted_iota(jnp.int32, (wide, count), 1)
    home = (from_row % n) * ROWS + from_row // n
    puts = [jnp.where(dest == home + a * capacity, 1.0, 0.0).astype(bf16) for a in range(pieces)]
    for p in range(PARTS):
        t_drain(p)
    for p in range(PARTS):
        trade(p).wait_recv()
        summed = own[:, p * share_cols : (p + 1) * share_cols] + rows_recv[p].astype(f32)
        summed = summed.astype(bf16)
        back = jnp.zeros((wide, piece), f32)
        for a in range(pieces):
            columns = summed[:, a * piece : (a + 1) * piece]
            back = back + jnp.dot(puts[a], columns, preferred_element_type=f32)
        back_out[p] = blocks_of(back, n)
        exchange_start(back_out.at[p], back_in.at[p], b_send.at[p], b_recv.at[p])
        back_in[p, me] = back_out[p, here]

    for p in range(PARTS):
        exchange_recv(back_out.at[p], back_in.at[p], b_send.at[p], b_recv.at[p])
        returned = rows_of(back_in[p])
        for a in range(pieces):
            added = jnp.dot(mixes[a][0], returned, preferred_element_type=f32)
            added = added + jnp.dot(mixes[a][1], returned, preferred_element_type=f32)
            at = p * share_cols + a * piece
            start = pl.multiple_of(h * half + at, piece)
            out_ref[:, at : at + piece] = stream[:, pl.ds(start, piece)] + added

    for p in range(PARTS):
        trade(p).wait_send()
        exchange_sent(back_out.at[p], back_in.at[p], b_send.at[p], b_recv.at[p])


def fused(q_latent, q_rotary, cache_latent, cache_rotary, lengths, resid, norm_gain, route_ids, route_weights, w_value_out,
          w_gate_up, w_down):
    n = LINE * PAIR * CORE
    seqs, width = resid.shape
    head_count, latent = q_latent.shape[1:]
    cols = w_value_out.shape[1]
    half = width // 2
    capacity = -(-(seqs * route_ids.shape[1]) // n)
    gate_up, down = w_gate_up[0], w_down[0]
    bf16, f32 = jnp.bfloat16, jnp.float32
    vmem, anywhere = pl.BlockSpec(memory_space=pltpu.VMEM), pl.BlockSpec(memory_space=pl.ANY)
    dma = pltpu.SemaphoreType.DMA
    return pl.pallas_call(
        layer_kernel,
        out_shape=jax.ShapeDtypeStruct((seqs, half), f32),
        in_specs=[vmem] * 4 + [pl.BlockSpec(memory_space=pltpu.SMEM)] + [vmem] * 4 + [anywhere] * 3,
        out_specs=vmem,
        scratch_shapes=[
            pltpu.VMEM(w_value_out.shape[::-1], bf16),
            pltpu.VMEM(gate_up.shape, bf16),
            pltpu.VMEM(down.shape, bf16),
            pltpu.VMEM((head_count, seqs, latent), f32),
            pltpu.VMEM((CHUNKS, n, head_count // CHUNKS, seqs, latent), bf16),
            pltpu.VMEM((2, cols, n * seqs), f32),
            pltpu.VMEM((cols, n * seqs), f32),
            pltpu.VMEM((cols, n * seqs), bf16),
            pltpu.VMEM((cols, n * seqs), bf16),
            pltpu.VMEM((n, seqs, cols), bf16),
            pltpu.VMEM((n, seqs, cols), bf16),
            pltpu.VMEM((seqs, width), f32),
            pltpu.VMEM((PARTS, n, seqs, width // PARTS + EXTRA), bf16),
            pltpu.VMEM((PARTS, capacity * n, half // PARTS), bf16),
            pltpu.VMEM((PARTS, capacity * n, half // PARTS), bf16),
            pltpu.VMEM((PARTS, n, ROWS, half // (PARTS * (ROWS // capacity))), bf16),
            pltpu.VMEM((PARTS, n, ROWS, half // (PARTS * (ROWS // capacity))), bf16),
            dma((3,)),
            dma((CHUNKS, PAIR * LINE)), dma((CHUNKS, PAIR * LINE)), dma((CHUNKS, LINE)),
            dma((CHUNKS, PAIR)), dma((CHUNKS, PAIR * LINE + PAIR)),
            dma((PARTS, PAIR * LINE)), dma((PARTS, PAIR * LINE)), dma((PARTS, LINE)),
            dma((PARTS, PAIR)), dma((PARTS, PAIR * LINE + PAIR)),
            dma((4,)), dma((PARTS,)), dma((PARTS,)), dma((n,)), dma((n,)),
            dma((PARTS, n)), dma((PARTS, n)),
        ],
        compiler_params=pltpu.CompilerParams(
            collective_id=0, has_side_effects=True, vmem_limit_bytes=56 * 1024 * 1024
        ),
    )(
        q_latent, q_rotary, cache_latent, cache_rotary, lengths, resid,
        norm_gain[None, :], route_ids, route_weights, w_value_out.T, gate_up, down,
    )


def attend(q_latent, q_rotary, cache_latent, cache_rotary, lengths):
    scores = jnp.einsum("shl,scl->shc", q_latent, cache_latent, preferred_element_type=jnp.float32)
    scores = scores + jnp.einsum(
        "shr,src->shc", q_rotary, cache_rotary, preferred_element_type=jnp.float32
    )
    scores = scores * softmax_scale
    position = lax.broadcasted_iota(jnp.int32, scores.shape, 2)
    scores = jnp.where(position < lengths[:, None, None], scores, -1e30)
    highest = jnp.max(scores, axis=2, keepdims=True)
    weights = jnp.exp(scores - highest)
    probs = (weights / jnp.sum(weights, axis=2, keepdims=True)).astype(jnp.bfloat16)
    return jnp.einsum(
        "shc,scl->shl", probs, cache_latent, preferred_element_type=jnp.float32
    ).astype(jnp.bfloat16)


def on_device(
    q_latent,
    q_rotary,
    cache_latent,
    cache_rotary,
    lengths,
    w_value_out,
    resid,
    norm_gain,
    route_ids,
    route_weights,
    w_gate_up,
    w_down,
):
    seq_local = q_latent.shape[0]
    if (
        lax.axis_size("head") == 2
        and lax.axis_size("expert") == LINE * PAIR * CORE
        and seq_local == 8
    ):
        return fused(
            q_latent, q_rotary, cache_latent, cache_rotary, lengths, resid, norm_gain,
            route_ids, route_weights, w_value_out, w_gate_up, w_down,
        )
    latent_out = attend(q_latent, q_rotary, cache_latent, cache_rotary, lengths)
    flattened = latent_out.reshape(seq_local, -1)
    column_terms = jnp.dot(
        lax.all_gather(flattened, "expert", axis=0, tiled=True),
        w_value_out,
        preferred_element_type=jnp.float32,
    )
    column_sums = lax.psum(column_terms, "head")
    attention = lax.all_to_all(
        column_sums.astype(jnp.bfloat16), "expert", split_axis=0, concat_axis=1, tiled=True
    )
    stream = resid.astype(jnp.float32) + attention.astype(jnp.float32)
    mean_square = jnp.mean(stream * stream, axis=1, keepdims=True)
    normed = (stream * lax.rsqrt(mean_square + norm_epsilon) * norm_gain).astype(jnp.bfloat16)
    expert_count = lax.axis_size("expert")
    top_count = route_ids.shape[1]
    capacity = max(2, -(-(seq_local * top_count) // expert_count))
    flat_ids = route_ids.reshape(-1)
    one_hot = (flat_ids[:, None] == jnp.arange(expert_count, dtype=jnp.int32)[None, :]).astype(
        jnp.int32
    )
    earlier = jnp.cumsum(one_hot, axis=0) - one_hot
    slot_index = jnp.sum(earlier * one_hot, axis=1)
    target = (flat_ids * capacity + slot_index).reshape(seq_local, top_count)
    places = jnp.arange(expert_count * capacity, dtype=jnp.int32)
    matches = target[None, :, :] == places[:, None, None]
    selector = jnp.sum(matches.astype(jnp.int32), axis=2).astype(jnp.bfloat16)
    blending = jnp.sum(jnp.where(matches, route_weights[None, :, :], 0.0), axis=2)
    outgoing = jnp.dot(selector, normed, preferred_element_type=jnp.float32).astype(jnp.bfloat16)
    outgoing = outgoing.reshape(expert_count, capacity, -1)
    gate_up = w_gate_up[0]
    down_local = w_down[0]
    col_width = stream.shape[1] // lax.axis_size("head")
    offset = lax.axis_index("head") * col_width
    arrived = lax.all_to_all(outgoing, "expert", split_axis=0, concat_axis=0, tiled=True)
    flat_rows = arrived.reshape(-1, arrived.shape[2])
    projected = jnp.einsum("rd,gfd->rgf", flat_rows, gate_up, preferred_element_type=jnp.float32)
    hidden = (jax.nn.silu(projected[:, 0]) * projected[:, 1]).astype(jnp.bfloat16)
    partial_rows = jnp.dot(hidden, down_local, preferred_element_type=jnp.float32)
    expert_terms = partial_rows.reshape(arrived.shape[0], arrived.shape[1], -1)
    summed_rows = lax.psum(expert_terms.astype(jnp.bfloat16), "head")
    returned = lax.all_to_all(summed_rows, "expert", split_axis=0, concat_axis=0, tiled=True)
    back_rows = returned.reshape(expert_count * capacity, -1).astype(jnp.float32)
    mixture = jnp.dot(blending.T, back_rows, precision=lax.Precision.HIGHEST)
    mixed_full = stream + mixture
    return lax.dynamic_slice_in_dim(mixed_full, offset, col_width, 1)


def solution(mesh):
    placed = (
        P("expert", "head", None),
        P("expert", "head", None),
        P("expert", None, None),
        P("expert", None, None),
        P("expert"),
        P("head", "expert"),
        P("expert", None),
        P(),
        P("expert", None),
        P("expert", None),
        P("expert", None, "head", None),
        P("expert", "head", None),
    )
    return jax.shard_map(
        on_device, mesh=mesh, in_specs=placed, out_specs=P("expert", "head"), check_vma=False
    )
```
